32 devices in a mesh: rows: 16 (over z, y, x), mp: 2 (over core).
Axes of the slice: x: 2, y: 2, z: 4, core: 2. Of those that a mesh axis runs over, the one named last changes fastest.
Arguments:
- params: float32 [329728], P(('rows', 'mp'))
- momentum: float32 [329728], P(('rows', 'mp')), may hold values from -0.0008544922 to 0.0008544922
- average: float32 [329728], P(('rows', 'mp'))
- table: float32 [1024, 256], P('rows'), may hold values from -5 to 5
- code_first: float32 [1024, 256], P('rows'), may hold values from -5.340576e-05 to 5.340576e-05
- code_second: float32 [1024, 256], P('rows'), may hold values from 9.765625e-13 to 3.90625e-12
- coords: float32 [3, 131072], P(None, ('rows', 'mp')), may hold values from -3 to 3
- targets: float32 [131072], P(('rows', 'mp')), may hold values from -0.6 to 0.6
- segment_ids: int32 [131072], P(('rows', 'mp')), may hold values from -1 to 63, as said below
- shape_code: int32 [64], replicated, may hold values from 0 to 1023, as said below
Outputs:
- loss: float32 [], replicated
- new_momentum: float32 [329728], P(('rows', 'mp'))
- new_params: float32 [329728], P(('rows', 'mp'))
- new_average: float32 [329728], P(('rows', 'mp'))
- new_table: float32 [1024, 256], P('rows')
- new_first: float32 [1024, 256], P('rows')
- new_second: float32 [1024, 256], P('rows')
The draws below stay inside these ranges and needn't reach their ends.
Inputs may be any that keep to these rules, and one draw needn't show every extreme that they name: `segment_ids`: devices counted over rows+mp in mesh order, each holding 4096 consecutive samples: the first 256 samples of every device belong to one shape, the same on all devices, and are never padding; the other samples of device d are -1 or belong to shapes d * 2 to d * 2 + 1 in non-decreasing order, each of these shapes with at least one sample there. `shape_code`: distinct table rows.
All inputs are finite; a program needn't handle non-finite values.
Results may differ from the reference program's by a relative error of at most 0.0003.
Values sent between devices are 32-bit elements; how exact they have to be, the bound alone decides.
A program may use at most 64 MiB of HBM per device.

```python
import math
import jax
import jax.numpy as jnp
from jax import lax

CODE = 256
H2 = 512
PTS_DEV = 4096
SHAPES_DEV = 2
STEP = 10
CODES = 1024
NSHAPES = 64
POINTS = 131072
PAR_DEV = 10304
N_ROWS = 16
N_MP = 2


def parameter_values(key):
    in_width = CODE + 3
    inner = H2 - CODE - 3
    keys = jax.random.split(key, 8)
    total = PAR_DEV * N_ROWS * N_MP
    row_scale = jnp.where(jnp.arange(in_width) >= CODE, 20.0, 1.0).astype(jnp.float32)
    first_dirs = jax.random.normal(keys[0], (in_width * inner,), jnp.float32) * in_width ** (-0.5)
    first_dirs = (first_dirs.reshape(in_width, inner) * row_scale[:, None]).reshape(-1)
    pieces = [first_dirs, jax.random.normal(keys[1], (H2 * H2,), jnp.float32) * H2 ** (-0.5), jax.random.normal(keys[2], (H2,), jnp.float32) * (0.2 * H2 ** (-0.5)), jax.random.uniform(keys[3], (inner,), jnp.float32, minval=0.6, maxval=1.6), jax.random.uniform(keys[4], (H2,), jnp.float32, minval=0.6, maxval=1.6), jax.random.normal(keys[5], (inner,), jnp.float32) * 0.3, jax.random.normal(keys[6], (H2,), jnp.float32) * 0.3, jax.random.normal(keys[7], (1,), jnp.float32) * 0.1]
    values = jnp.concatenate(pieces)
    return jnp.concatenate([values, jnp.zeros((total - values.shape[0],), jnp.float32)])


def draw_params(key, part):
    shared = parameter_values(key)
    return shared


def draw_average(key, part):
    shared = parameter_values(key)
    key = jax.random.fold_in(key, 4)
    return shared + 0.02 * jax.random.normal(key, shared.shape, jnp.float32)


def draw_segment_ids(key, part):
    key = jax.random.fold_in(key, 11)
    devices = N_ROWS * N_MP
    head_len = PTS_DEV // 16
    remain = PTS_DEV - head_len
    global_shape = jax.random.randint(jax.random.fold_in(key, 1), (), 0, NSHAPES)
    local = jax.random.randint(jax.random.fold_in(key, 2), (devices, remain), 0, SHAPES_DEV)
    places = jnp.arange(remain)[None, :]
    local = jnp.where(places < SHAPES_DEV, places, local)
    local = jnp.sort(local, axis=1)
    previous = jnp.concatenate([jnp.full((devices, 1), -1, local.dtype), local[:, :-1]], axis=1)
    starts = local != previous
    device_ids = jnp.arange(devices)[:, None]
    factor = jax.random.randint(jax.random.fold_in(key, 4), (devices, 1), 1, 21)
    kept = jax.random.randint(jax.random.fold_in(key, 3), (devices, remain), 0, 60 * (devices - 1)) < (devices - 1 + 2 * device_ids) * factor
    local_ids = jnp.where(starts | kept, device_ids * SHAPES_DEV + local, -1)
    heads = jnp.full((devices, head_len), global_shape, local_ids.dtype)
    return jnp.concatenate([heads, local_ids], axis=1).reshape(-1).astype(jnp.int32)


def draw_shape_code(key, part):
    key = jax.random.fold_in(key, 12)
    return jax.random.permutation(key, CODES)[:NSHAPES].astype(jnp.int32)


def levels(stream_key, shape, shards, low, top_value):
    def one(position, shards_of):
        heights = jax.random.uniform(jax.random.fold_in(jax.random.fold_in(stream_key, 6), position), (shards_of,), jnp.float32, low / len(shards), top_value / len(shards))
        return jnp.repeat(jnp.exp(heights), shape[position] // shards_of).reshape((-1,) + (1,) * (len(shape) - position - 1))

    gain = one(*shards[0])
    for cut in shards[1:]:
        gain = gain * one(*cut)
    return gain


def scatter_about(own_key, shape, scale, most, shards=(), held_as=jnp.bfloat16):
    level = levels(own_key, shape, shards, -0.22, 0.18) if shards else 1.0
    array = jax.random.normal(own_key, shape, jnp.float32) * scale * level
    return jnp.minimum(jnp.maximum(array, -most), most).astype(held_as)


def setup_inputs(seed: int = 0) -> dict:
    arg_keys = jax.random.split(jax.random.key(seed), 11)
    params = draw_params(jax.random.fold_in(arg_keys[10], 71), 0)
    momentum = scatter_about(arg_keys[1], (PAR_DEV * N_ROWS * N_MP,), (0.02 * POINTS ** -0.5), 0.0008544922, ((0, 32),), jnp.float32)
    average = draw_average(jax.random.fold_in(arg_keys[10], 71), 0)
    table = scatter_about(arg_keys[3], (CODES, CODE), 1.0, 5.0, ((0, 16),), jnp.float32)
    code_first = scatter_about(arg_keys[4], (CODES, CODE), (0.11 * 0.002 / NSHAPES), 5.340576171875e-05, ((0, 16),), jnp.float32)
    code_second = jnp.clip(jnp.exp(math.log(3.906249889523705e-12) - 1.3862944 * jax.random.uniform(arg_keys[5], (CODES, CODE), jnp.float32) ** levels(arg_keys[5], (CODES, CODE), ((0, 16),), -0.2, 0.2)), 9.765624723809263e-13, 3.906249889523705e-12)
    coords = scatter_about(arg_keys[6], (3, POINTS), 1.0, 3.0, ((1, 32),), jnp.float32)
    targets = scatter_about(arg_keys[7], (POINTS,), 0.1, 0.6, ((0, 32),), jnp.float32)
    segment_ids = draw_segment_ids(jax.random.fold_in(arg_keys[10], 71), 0)
    shape_code = draw_shape_code(jax.random.fold_in(arg_keys[10], 71), 0)
    return dict(params=params, momentum=momentum, average=average, table=table, code_first=code_first, code_second=code_second, coords=coords, targets=targets, segment_ids=segment_ids, shape_code=shape_code)


PRECISE = lax.Precision.HIGHEST
CLAMP_DELTA = 0.1
SMOOTH = 0.01
PRIOR_WEIGHT = 0.001
LEARN_RATE = 200.0
MOMENTUM_DECAY = 0.9
AVERAGE_DECAY = 0.9
CODE_RATE = 0.5
BETA_FIRST = 0.9
BETA_SECOND = 0.999
ADAM_EPS = 1e-08
NORM_EPS = 1e-12

def layout():
    in_width = CODE + 3
    inner = H2 - CODE - 3
    shapes = [(in_width, inner), (H2, H2), (H2,), (inner,), (H2,), (inner,), (H2,), (1,)]
    pieces = []
    offset = 0
    for dims in shapes:
        entries = 1
        for extent in dims:
            entries = entries * extent
        pieces.append((offset, entries, dims))
        offset = offset + entries
    return pieces

def unpack(flat_all):
    return [flat_all[begin_at:begin_at + entries].reshape(dims) for begin_at, entries, dims in layout()]

def effective(flat_all):
    first_dir, second_dir, head_vec, first_gain, second_gain, first_bias, second_bias, head_bias = unpack(flat_all)
    first_weight = first_dir * (first_gain * lax.rsqrt(lax.optimization_barrier(jnp.sum(first_dir * first_dir, axis=0)) + NORM_EPS))
    second_weight = second_dir * (second_gain * lax.rsqrt(lax.optimization_barrier(jnp.sum(second_dir * second_dir, axis=0)) + NORM_EPS))
    return (first_weight, second_weight, head_vec, first_bias, second_bias, head_bias)

def network(weights, point_codes, coord_rows):
    first_weight, second_weight, head_vec, first_bias, second_bias, head_bias = weights
    inputs = jnp.concatenate([point_codes, coord_rows], axis=1)
    first = jax.nn.silu(jnp.dot(inputs, first_weight, precision=PRECISE) + first_bias)
    joined = jnp.concatenate([first, inputs], axis=1)
    second = jax.nn.silu(jnp.dot(joined, second_weight, precision=PRECISE) + second_bias)
    return jnp.tanh(jnp.dot(second, head_vec, precision=PRECISE) + head_bias[0])

def point_loss(predicted, targets):
    resid = CLAMP_DELTA * jnp.tanh(predicted / CLAMP_DELTA) - CLAMP_DELTA * jnp.tanh(targets / CLAMP_DELTA)
    return jnp.sqrt(resid * resid + SMOOTH * SMOOTH) - SMOOTH

def total_loss(flat_all, table, coords, targets, segment_ids, shape_code):
    weights = effective(flat_all)
    is_valid = segment_ids >= 0
    safe_ids = jnp.where(is_valid, segment_ids, 0).astype(jnp.int32)
    shape_codes = table[shape_code]
    blocks_ids = safe_ids.reshape(-1, PTS_DEV)
    blocks_xyz = coords.reshape(3, -1, PTS_DEV).transpose(1, 2, 0)

    def one_block(block_args):
        block_ids, block_xyz = block_args
        return network(weights, shape_codes[block_ids], block_xyz)
    predicted = lax.map(jax.checkpoint(one_block), (blocks_ids, blocks_xyz)).reshape(-1)
    losses = jnp.where(is_valid, point_loss(predicted, targets), 0.0)
    sums = jax.ops.segment_sum(losses, safe_ids, num_segments=NSHAPES)
    counts = jax.ops.segment_sum(is_valid.astype(jnp.float32), safe_ids, num_segments=NSHAPES)
    prior = PRIOR_WEIGHT * lax.optimization_barrier(jnp.sum(shape_codes * shape_codes, axis=1))
    return jnp.sum(sums / counts + prior) / NSHAPES

def reference(params, momentum, average, table, code_first, code_second, coords, targets, segment_ids, shape_code):

    def objective(flat_all, codes_all):
        return total_loss(flat_all, codes_all, coords, targets, segment_ids, shape_code)
    loss, pullback = jax.vjp(objective, params, table)
    grad_flat, grad_table = pullback(jnp.ones((), loss.dtype))
    new_momentum = MOMENTUM_DECAY * momentum + grad_flat
    new_params = params - LEARN_RATE * (grad_flat + MOMENTUM_DECAY * new_momentum)
    new_average = AVERAGE_DECAY * average + (1.0 - AVERAGE_DECAY) * new_params
    marks = jnp.zeros((CODES,), table.dtype).at[shape_code].set(1.0)
    used_rows = marks[:, None] > 0.5
    first_new = BETA_FIRST * code_first + (1.0 - BETA_FIRST) * grad_table
    second_new = BETA_SECOND * code_second + (1.0 - BETA_SECOND) * grad_table * grad_table
    step_vals = CODE_RATE * (first_new / (1.0 - BETA_FIRST ** STEP)) / (jnp.sqrt(second_new / (1.0 - BETA_SECOND ** STEP)) + ADAM_EPS)
    new_table = jnp.where(used_rows, table - step_vals, table)
    new_first = jnp.where(used_rows, first_new, code_first)
    new_second = jnp.where(used_rows, second_new, code_second)
    return (loss, new_momentum, new_params, new_average, new_table, new_first, new_second)
```

```python
import functools
import math

import jax
import jax.numpy as jnp
from jax import lax
from jax.experimental import pallas as pl
from jax.experimental.pallas import tpu as pltpu
from jax.sharding import PartitionSpec as P

MESH = pl.DeviceIdType.MESH
F32, BF16 = jnp.float32, jnp.bfloat16
EXACT = lax.Precision.HIGHEST
CODE = 256
H2 = 512
INNER = H2 - CODE - 3
STEP = 10
CLAMP_DELTA = 0.1
SMOOTH = 0.01
PRIOR_WEIGHT = 0.001
LEARN_RATE = 200.0
MOMENTUM_DECAY = 0.9
AVERAGE_DECAY = 0.9
CODE_RATE = 0.5
BETA_FIRST = 0.9
BETA_SECOND = 0.999
ADAM_EPS = 1e-08
NORM_EPS = 1e-12
LANES = 128

SECOND_AT = (CODE + 3) * INNER
SECOND_ROW, SHIFT = divmod(SECOND_AT, LANES)
TAIL_AT = SECOND_AT + H2 * H2 + H2
TAIL_ROW = TAIL_AT // LANES
TAIL_PIECES = (INNER, H2, INNER, H2, 1)


def chip_dims(rows):
    return {16: (4, 2, 2), 128: (4, 4, 8)}.get(rows, (rows, 1, 1))


def piece_rows(per_device, devices):
    most = max((per_device * d) % LANES for d in range(devices))
    rows = -(-(most + per_device) // LANES)
    return rows, (rows // 8 + 1) * 8


class Place:
    def __init__(self, dims):
        self.dims = dims
        self.row = lax.axis_index("rows")
        self.core = lax.axis_index("mp")
        d0, d1, d2 = dims
        self.at = [self.row // (d1 * d2), (self.row // d2) % d1, self.row % d2]

    def peer(self, dim, step):
        at = list(self.at)
        at[dim] = (at[dim] + step) % self.dims[dim]
        d0, d1, d2 = self.dims
        return at[dim], ((at[0] * d1 + at[1]) * d2 + at[2], self.core)

    def sibling(self):
        return (self.row, 1 - self.core)

    def steps(self, dim):
        return range(1, self.dims[dim])


def remote(src, dst, send, recv, device):
    return pltpu.make_async_remote_copy(
        src, dst, send, recv, device_id=device, device_id_type=MESH
    )


class Gather:
    def __init__(self, place, buf, chunks, orders, send, recv):
        self.p, self.buf, self.chunks, self.orders = place, buf, chunks, orders
        self.send, self.recv, self.live = send, recv, {}

    def view(self, done, core, k):
        idx = [slice(None) if d in done else self.p.at[d] for d in range(3)]
        begin, size = self.chunks[k]
        return self.buf.at[core, idx[0], idx[1], idx[2], pl.ds(begin, size)]

    def start(self, k, stage):
        order = self.orders[k % len(self.orders)]
        core = self.p.core
        copies = []
        if stage == 3:
            v = self.view(order, core, k)
            copies.append(remote(v, v, self.send.at[k, 3, 0], self.recv.at[k, 3, 0], self.p.sibling()))
        else:
            for o in self.p.steps(order[stage]):
                v = self.view(order[:stage], core, k)
                dev = self.p.peer(order[stage], o)[1]
                copies.append(remote(v, v, self.send.at[k, stage, o], self.recv.at[k, stage, o], dev))
        for c in copies:
            c.start()
        self.live[k, stage] = copies

    def arrive(self, k, stage):
        for c in self.live[k, stage]:
            c.wait_recv()

    def finish(self):
        for copies in self.live.values():
            for c in copies:
                c.wait_send()


class Reduce:
    def __init__(self, place, buf, landing, chunks, orders, send, recv, cores):
        self.p, self.buf, self.landing, self.chunks, self.orders = place, buf, landing, chunks, orders
        self.send, self.recv, self.cores, self.live = send, recv, cores, {}

    def index(self, k, stage, last):
        order = self.orders[k % len(self.orders)]
        idx = [self.p.at[d] if d in order[:stage] else slice(None) for d in range(3)]
        if last is not None:
            idx[order[stage]] = last
        begin, size = self.chunks[k]
        return tuple(idx) + (pl.ds(begin, size),)

    def landed(self, k, stage, o):
        ref = self.landing[1 + 3 * (k % len(self.orders)) + stage]
        begin, size = self.chunks[k]
        return ref.at[(o - 1,) + (slice(None),) * (2 - stage) + (pl.ds(begin, size),)]

    def start(self, k, stage):
        order = self.orders[k % len(self.orders)]
        copies = []
        if stage < 0:
            idx = self.index(k, 0, None)
            copies.append(
                remote(
                    self.buf.at[(1 - self.p.core,) + idx],
                    self.landing[0].at[idx],
                    self.send.at[k, 3, 0],
                    self.recv.at[k, 3, 0],
                    self.p.sibling(),
                )
            )
        else:
            for o in self.p.steps(order[stage]):
                at, dev = self.p.peer(order[stage], o)
                idx = self.index(k, stage, at)
                copies.append(
                    remote(
                        self.buf.at[(self.p.core,) + idx],
                        self.landed(k, stage, o),
                        self.send.at[k, stage, o],
                        self.recv.at[k, stage, o],
                        dev,
                    )
                )
        for c in copies:
            c.start()
        self.live[k, stage] = copies

    def arrive(self, k, stage):
        for c in self.live[k, stage]:
            c.wait_recv()
        order = self.orders[k % len(self.orders)]
        if stage < 0:
            idx = self.index(k, 0, None)
            mine = (self.p.core,) + idx
            self.buf[mine] = self.buf[mine] + self.landing[0][idx]
        else:
            idx = self.index(k, stage, self.p.at[order[stage]])
            mine = (self.p.core,) + idx
            total = self.buf[mine]
            for o in self.p.steps(order[stage]):
                total = total + self.landed(k, stage, o)[...]
            self.buf[mine] = total

    def finish(self):
        for copies in self.live.values():
            for c in copies:
                c.wait_send()


def landings(dims, orders, tail):
    shapes = [tuple(dims) + tail]
    for order in orders:
        for stage, d in enumerate(order):
            rest = tuple(dims[e] for e in range(3) if e not in order[: stage + 1])
            shapes.append((max(dims[d] - 1, 1),) + rest + tail)
    return [pltpu.VMEM(shape, F32) for shape in shapes]


def iota(shape, dim):
    return lax.broadcasted_iota(jnp.int32, shape, dim)


def dot(a, b, precision=None):
    return jnp.dot(a, b, precision=precision, preferred_element_type=F32)


def dot_nt(a, b, precision=None):
    return lax.dot_general(
        a, b, (((1,), (1,)), ((), ())), precision=precision, preferred_element_type=F32
    )


def dot_tn(a, b, precision=None):
    return lax.dot_general(
        a, b, (((0,), (0,)), ((), ())), precision=precision, preferred_element_type=F32
    )


def turn(x, by):
    by = by % x.shape[1]
    return pltpu.roll(x, by, 1) if by else x


def widen(x, width):
    return jnp.concatenate([x, jnp.zeros((x.shape[0], width - x.shape[1]), F32)], axis=1)


def one_row(x, count):
    return jnp.concatenate([x[k : k + 1] for k in range(count)], axis=1)


def bounds(devices, per_device):
    for d in range(devices):
        row, phase = divmod(per_device * d, LANES)
        yield d, row, phase, -(-(phase + per_device) // LANES)


def assemble(dims, per_device, buf, flat):
    rows = dims[0] * dims[1] * dims[2]
    for d, row, phase, count in bounds(2 * rows, per_device):
        chip = d // 2
        src = buf.at[d % 2, chip // (dims[1] * dims[2]), (chip // dims[2]) % dims[1], chip % dims[2]]
        if phase:
            flat[row : row + 1, :] = flat[row : row + 1, :] + src[0:1, :]
            flat[row + 1 : row + count, :] = src[1:count, :]
        else:
            flat[row : row + count, :] = src[0:count, :]


def scatter(dims, per_device, rows_kept, flat, buf):
    rows = dims[0] * dims[1] * dims[2]
    for d, row, phase, count in bounds(2 * rows, per_device):
        chip = d // 2
        dst = buf.at[d % 2, chip // (dims[1] * dims[2]), (chip // dims[2]) % dims[1], chip % dims[2]]
        dst[...] = flat[row : row + rows_kept, :]


def first_blocks():
    for back in range(4):
        begin = -(-256 * back // 3)
        end = min(-(-256 * (back + 1) // 3), CODE + 3)
        for at in range(begin, end, 8):
            yield back, at, min(8, end - at)


def unpack_first(flat, wide, v1):
    wide[0:8, :] = jnp.zeros((8, 256), F32)
    for half in range(2):
        lanes = slice(half * LANES, (half + 1) * LANES)
        wide[8:272, lanes] = flat[pl.ds(half, 264, stride=2), :]
    v1[256:264, :] = jnp.zeros((8, 256), F32)
    for back, at, n in first_blocks():
        base = 3 * at - 256 * back
        lane = iota((n, 256), 1)
        move = base + 3 * iota((n, 256), 0)
        here = wide[8 + at - back : 8 + at - back + n, :]
        before = wide[7 + at - back : 7 + at - back + n, :]
        mixed = jnp.where(lane < 256 - move, here, before)
        mixed = turn(mixed, base)
        if n > 1:
            mixed = pltpu.roll(mixed, 0, 1, stride=3, stride_axis=0)
        v1[at : at + n, :] = jnp.where(lane < INNER, mixed, 0.0)


def pack_first(v1, wide, flat):
    wide[...] = jnp.zeros(wide.shape, F32)
    for back, at, n in first_blocks():
        base = 3 * at - 256 * back
        lane = iota((n, 256), 1)
        sub = iota((n, 256), 0)
        moved = turn(v1[at : at + n, :], -base)
        for bit in range(3):
            moved = jnp.where((sub >> bit) & 1 == 1, turn(moved, -3 * (1 << bit)), moved)
        here = lane < 256 - (base + 3 * sub)
        a = slice(8 + at - back, 8 + at - back + n)
        b = slice(7 + at - back, 7 + at - back + n)
        wide[a, :] = wide[a, :] + jnp.where(here, moved, 0.0)
        wide[b, :] = wide[b, :] + jnp.where(here, 0.0, moved)
    for half in range(2):
        lanes = slice(half * LANES, (half + 1) * LANES)
        flat[pl.ds(half, 256, stride=2), :] = wide[8:264, lanes]


def unpack_second(flat, v2):
    for q in range(H2 // LANES):
        lanes = slice(q * LANES, (q + 1) * LANES)
        for at in range(0, H2 + 8, 104):
            rows = flat[pl.ds(SECOND_ROW + q + 4 * at, 104, stride=4), :]
            if q == 0:
                after = flat[pl.ds(SECOND_ROW + 4 + 4 * at, 104, stride=4), :]
                rows = jnp.where(iota((104, LANES), 1) < SHIFT, after, rows)
            v2[at : at + 104, lanes] = rows


def pack_second(v2, flat):
    low = iota((1, LANES), 1) < SHIFT
    for q in range(1, H2 // LANES):
        lanes = slice(q * LANES, (q + 1) * LANES)
        flat[pl.ds(SECOND_ROW + q, H2, stride=4), :] = v2[0:H2, lanes]
        flat[SECOND_ROW + q + 4 * H2 : SECOND_ROW + q + 4 * H2 + 1, :] = v2[H2 : H2 + 1, lanes]
    flat[pl.ds(SECOND_ROW + 4, H2, stride=4), :] = jnp.where(low, v2[0:H2, 0:LANES], v2[1 : H2 + 1, 0:LANES])
    flat[SECOND_ROW : SECOND_ROW + 1, :] = jnp.where(
        low, flat[SECOND_ROW : SECOND_ROW + 1, :], v2[0:1, 0:LANES]
    )
    flat[TAIL_ROW : TAIL_ROW + 1, :] = jnp.where(low, v2[H2 : H2 + 1, 0:LANES], 0.0)


def unpack_tail(flat):
    count = 13
    tail = one_row(flat[TAIL_ROW : TAIL_ROW + count, :], count)
    at = SHIFT
    parts = []
    for width in TAIL_PIECES:
        lanes = {INNER: 256, H2: H2, 1: LANES}[width]
        piece = turn(tail, -at)[:, 0:lanes]
        if width == H2:
            piece = turn(piece, SHIFT)
        else:
            piece = jnp.where(iota((1, lanes), 1) < width, piece, 0.0)
        parts.append(piece)
        at += width
    return parts


def pack_tail(parts, flat):
    count = 13
    at = SHIFT
    total = jnp.zeros((1, count * LANES), F32)
    for width, piece in zip(TAIL_PIECES, parts):
        if width == H2:
            piece = turn(piece, -SHIFT)
        else:
            piece = jnp.where(iota(piece.shape, 1) < width, piece, 0.0)
        total = total + turn(widen(piece, count * LANES), at)
        at += width
    flat[TAIL_ROW : TAIL_ROW + 1, :] = flat[TAIL_ROW : TAIL_ROW + 1, :] + total[:, 0:LANES]
    for k in range(1, count):
        flat[TAIL_ROW + k : TAIL_ROW + k + 1, :] = total[:, k * LANES : (k + 1) * LANES]


def split2(x):
    high = x.astype(BF16)
    return high, (x - high.astype(F32)).astype(BF16)


def split3(x):
    a = x.astype(BF16).astype(F32)
    b = (x - a).astype(BF16).astype(F32)
    return a, b, x - a - b


def kernel(
    cfg,
    piece_ref,
    table_ref,
    code_first_ref,
    code_second_ref,
    coords_ref,
    targets_ref,
    seg_ref,
    shape_code_ref,
    loss_ref,
    grad_ref,
    new_table_ref,
    new_first_ref,
    new_second_ref,
    buf,
    landing,
    flat,
    wide,
    v1,
    v2,
    g1,
    g2,
    w2t,
    w2b,
    w0,
    bias,
    head,
    points,
    hc,
    h1,
    slope1,
    h2,
    act,
    second,
    d2b,
    df,
    d1b,
    dw2,
    dw1,
    dhead,
    sums,
    codes_buf,
    codes_landing,
    grads_buf,
    psend,
    precv,
    csend,
    crecv,
    dsend,
    drecv,
    rsend,
    rrecv,
):
    dims, per_device, tile = cfg["dims"], cfg["per_device"], cfg["tile"]
    used, kept = piece_rows(per_device, 2 * cfg["rows"])
    rows = cfg["rows"]
    shapes = cfg["shapes"]
    place = Place(dims)
    device = place.row * 2 + place.core
    tiles = seg_ref.shape[0] * LANES // tile
    per_tile = tile // LANES
    head_len = seg_ref.shape[0] * LANES // 16

    barrier = pltpu.get_barrier_semaphore()
    greeted = 1
    pl.semaphore_signal(barrier, inc=1, device_id=place.sibling(), device_id_type=MESH)
    for dim in range(3):
        for o in place.steps(dim):
            pl.semaphore_signal(barrier, inc=1, device_id=place.peer(dim, o)[1], device_id_type=MESH)
            greeted += 1
    pl.semaphore_wait(barrier, greeted)

    seg_heads = seg_ref[0 : head_len // LANES, :].astype(F32)
    shared = jnp.max(jnp.max(seg_heads, axis=1, keepdims=True), axis=0, keepdims=True)
    for q in range(per_tile):
        lanes = slice(q * LANES, (q + 1) * LANES)
        points[0, :, lanes] = seg_ref[pl.ds(q, tiles, stride=per_tile), :].astype(F32)
        points[1, :, lanes] = jnp.tanh(targets_ref[pl.ds(q, tiles, stride=per_tile), :] * (1.0 / CLAMP_DELTA))
    seg = points[0]

    def count(where):
        return jnp.sum(jnp.sum(where.astype(F32), axis=1, keepdims=True), axis=0, keepdims=True)

    mine = (device * 2).astype(F32)
    counts = [count(seg == shared), count(seg == mine), count(seg == mine + 1.0)]

    own = buf.at[place.core, place.at[0], place.at[1], place.at[2]]
    own[0 : kept - 8, :] = piece_ref[0 : kept - 8, :]
    own[kept - 8 : kept, :] = jnp.where(
        iota((8, LANES), 0) == 7, jnp.broadcast_to(counts[0], (8, LANES)), piece_ref[kept - 8 : kept, :]
    )

    gather = Gather(place, buf, cfg["chunks"], cfg["gather_orders"], psend, precv)
    chunk_ids = range(len(cfg["chunks"]))
    for k in chunk_ids:
        gather.start(k, 0)

    base = (place.row * table_ref.shape[0]).astype(F32)
    codes_of = jnp.broadcast_to(shape_code_ref[...].astype(F32) + 1.0, (8, shapes))
    slots = rows * 8
    kind = iota((slots, shapes), 0) & 7
    owner = (iota((slots, shapes), 0) >> 3) * 2 + place.core
    shape_id = iota((slots, shapes), 1)
    asked = jnp.where(
        kind == 3,
        (shape_id.astype(F32) == shared).astype(F32),
        jnp.where((kind == 4) | (kind == 5), (shape_id == owner * 2 + kind - 4).astype(F32), 0.0),
    )
    wanted = dot_nt(asked, codes_of, EXACT)[:, 0:1] - 1.0 - base
    pick = (wanted == iota((slots, table_ref.shape[0]), 1).astype(F32)).astype(F32)
    answer = dot(pick, table_ref[...], EXACT)
    codes_buf[place.core] = answer.reshape(dims + (8, CODE))
    codes = Reduce(place, codes_buf, codes_landing, [(0, 8)], [(2, 1, 0)], csend, crecv, False)
    codes.start(0, 0)

    for stage in range(4):
        if stage < 3:
            codes.arrive(0, stage)
            if stage < 2:
                codes.start(0, stage + 1)
        for k in chunk_ids:
            gather.arrive(k, stage)
            if stage < 3:
                gather.start(k, stage + 1)
    z8 = codes_buf[place.core, place.at[0], place.at[1], place.at[2]]

    assemble(dims, per_device, buf, flat)
    unpack_first(flat, wide, v1)
    unpack_second(flat, v2)
    gain1, gain2, bias1, bias2, head_bias = unpack_tail(flat)
    norm1 = jnp.sum(v1[...] * v1[...], axis=0, keepdims=True) + NORM_EPS
    norm2 = jnp.sum(v2[0:H2, :] * v2[0:H2, :], axis=0, keepdims=True) + NORM_EPS
    inv1, inv2 = lax.rsqrt(norm1), lax.rsqrt(norm2)
    scale1, scale2 = gain1 * inv1, gain2 * inv2
    head_row = v2[H2 : H2 + 1, :]
    hbias = head_bias[:, 0:1]

    total = jnp.sum(buf[:, :, :, :, kept - 8 : kept, :], axis=(0, 1, 2, 3))[7:8, 0:1]
    counts_all = [total]
    for k in (1, 2):
        counts_all.append(jnp.where(shared == mine + (k - 1.0), total, jnp.maximum(counts[k], 1.0)))
    inv_counts = [1.0 / (n * float(shapes)) for n in counts_all]
    position = iota((tiles, tile), 0) * tile + iota((tiles, tile), 1)
    is_two = (seg == mine + 1.0) & (position >= head_len)
    per_point = jnp.where(
        position < head_len, inv_counts[0], jnp.where(is_two, inv_counts[2], inv_counts[1])
    )
    points[2] = jnp.where(seg >= 0.0, per_point, 0.0)
    points[3] = jnp.where(is_two, 1.0, 0.0)

    lane1 = iota((8, 256), 1)
    sub1 = iota((8, 256), 0)
    code1 = dot(z8, v1[0:CODE, :], EXACT) * scale1 + bias1
    xyz1 = v1[CODE : CODE + 8, :] * scale1
    rows1 = 0.5 * jnp.where(sub1 < 3, xyz1, jnp.where(sub1 < 6, code1, 0.0))
    rows1 = jnp.where(lane1 < INNER, rows1, (lane1 == INNER + sub1).astype(F32))
    rows1 = jnp.where(sub1 < 6, rows1, 0.0)
    wa, wb, wc = split3(rows1)
    stack = jnp.concatenate([wa, wa, wb, wb, wa, wc] + [jnp.zeros((8, 256), F32)] * 10, axis=0)
    w0[...] = stack.T.astype(BF16)

    z_wide = turn(widen(z8, H2), INNER)
    code2 = 0.5 * (dot(z_wide, v2[0:H2, :], EXACT) * scale2 + bias2)
    sub2 = iota((8, H2), 0)
    columns = jnp.where(sub2 == 6, jnp.broadcast_to(0.5 * head_row, (8, H2)), code2)
    columns = jnp.concatenate([columns, jnp.zeros((LANES - 8, H2), F32)], axis=0).T
    for k in range(3):
        bias[k] = jnp.broadcast_to(columns[:, 3 + k : 4 + k], (H2, LANES))
    head[...] = jnp.broadcast_to(columns[:, 6:7], (H2, LANES))
    xyz2 = pltpu.roll(v2[H2 - 8 : H2, :], 0, 0)
    last = jnp.where(iota((8, H2), 0) < 5, v2[248:256, :], xyz2)
    normal = jnp.concatenate([v2[0:248, :], last], axis=0) * scale2
    w2b[...] = normal.astype(BF16)
    high, low = split2(0.5 * normal.T)
    w2t[:, 0:256] = high
    w2t[:, 256:512] = high
    w2t[:, 512:768] = low

    dw2[...] = jnp.zeros(dw2.shape, F32)
    dw1[...] = jnp.zeros(dw1.shape, F32)
    dhead[...] = jnp.zeros(dhead.shape, F32)
    sums[...] = jnp.zeros(sums.shape, F32)
    block = 32

    def one_tile(t, _):
        at = pl.ds(pl.multiple_of(t * tile, tile), tile)
        two = points[3, pl.ds(t, 1), :]
        here = t * tile + iota((1, tile), 1)
        is_head = (here < head_len).astype(F32)
        one = 1.0 - two - is_head
        x8 = jnp.concatenate(
            [coords_ref[:, at], is_head, one, two, jnp.zeros((2, tile), F32)], axis=0
        )
        xa, xb, xc = split3(x8)
        x48 = jnp.concatenate([xa, xb, xa, xb, xc, xa], axis=0).astype(BF16)
        hc[768:784, :] = jnp.concatenate([xa, xb], axis=0).astype(BF16)
        h1[...] = dot(w0[:, 0:48], x48)
        for u in range(0, 256, block):
            for q in range(per_tile):
                lanes = slice(q * LANES, (q + 1) * LANES)
                us = slice(u, u + block)
                h = h1[us, lanes]
                th = jnp.tanh(h)
                m = h * th
                f = h + m
                slope1[us, lanes] = (0.5 + 0.5 * th) * (1.0 + (h - m))
                if u + block > INNER:
                    f = jnp.where(iota((block, LANES), 0) + u >= INNER, h, f)
                fh, fl = split2(f)
                hc[us, lanes] = fh
                hc[256 + u : 256 + u + block, lanes] = fl
                hc[512 + u : 512 + u + block, lanes] = fh
        h2[...] = dot(w2t[...], hc[0:768, :])
        parts = []
        for q in range(per_tile):
            lanes = slice(q * LANES, (q + 1) * LANES)
            in_head = t * per_tile + q < head_len // LANES
            b_one = jnp.where(in_head, 0, 1)
            b_two = jnp.where(in_head, 0, 2)
            is_second = jnp.broadcast_to(two[:, lanes], (block, LANES)) > 0.5
            part = jnp.zeros((8, LANES), F32)
            for u in range(0, H2, block):
                us = slice(u, u + block)
                h = h2[us, lanes] + jnp.where(is_second, bias[b_two, us, :], bias[b_one, us, :])
                th = jnp.tanh(h)
                m = h * th
                s = h + m
                hw = head[us, :]
                second[us, lanes] = s
                act[us, lanes] = hw * ((1.0 + th) * (1.0 + (h - m)))
                w = hw * s
                for v in range(0, block, 8):
                    part = part + w[v : v + 8]
            parts.append(jnp.sum(part, axis=0, keepdims=True))
        raw = 2.0 * jnp.concatenate(parts, axis=1) + hbias
        pred = jnp.tanh(raw)
        squash = jnp.tanh(pred * (1.0 / CLAMP_DELTA))
        resid = CLAMP_DELTA * squash - CLAMP_DELTA * points[1, pl.ds(t, 1), :]
        square = resid * resid + SMOOTH * SMOOTH
        inv_radius = lax.rsqrt(square)
        share = points[2, pl.ds(t, 1), :]
        dpred = share * (resid * inv_radius) * (1.0 - squash * squash) * (1.0 - pred * pred)
        sums[0:1, :] = sums[0:1, :] + share * (square * inv_radius - SMOOTH)
        sums[1:2, :] = sums[1:2, :] + dpred
        for u in range(0, H2, block):
            us = slice(u, u + block)
            total_u = dhead[us, :]
            for q in range(per_tile):
                lanes = slice(q * LANES, (q + 1) * LANES)
                dp = jnp.broadcast_to(dpred[:, lanes], (block, LANES))
                d2b[us, lanes] = (act[us, lanes] * dp).astype(BF16)
                total_u = total_u + second[us, lanes] * dp
            dhead[us, :] = total_u
        df[...] = dot(w2b[...], d2b[...])
        dw2[...] = dw2[...] + dot_nt(hc[512:784, :], d2b[...])
        for u in range(0, 256, block):
            us = slice(u, u + block)
            d1b[us, :] = (df[us, :] * slope1[us, :]).astype(BF16)
        dw1[...] = dw1[...] + dot_nt(hc[768:784, :], d1b[...])
        return 0

    lax.fori_loop(0, tiles, one_tile, 0)

    outer1 = jnp.where(lane1 < INNER, dw1[0:8, :] + dw1[8:16, :], 0.0)
    outer2 = dw2[256:264, :] + dw2[264:272, :]
    slot_rows = (sub1 >= 3) & (sub1 < 6)
    d1 = jnp.where(slot_rows, outer1, 0.0)
    d2 = jnp.where((sub2 >= 3) & (sub2 < 6), outer2, 0.0)
    dz = dot_nt(d1 * scale1, v1[0:CODE, :], EXACT)
    dz = dz + turn(dot_nt(d2 * scale2, v2[0:H2, :], EXACT), -INNER)[:, 0:CODE]
    own_rows = (sub1 == 4) | (sub1 == 5)
    dz = dz + jnp.where(own_rows, (2.0 * PRIOR_WEIGHT / shapes) * z8, 0.0)
    prior = jnp.where(own_rows, z8 * z8, 0.0)
    prior = (PRIOR_WEIGHT / shapes) * jnp.sum(jnp.sum(prior, axis=1, keepdims=True), axis=0, keepdims=True)
    loss_here = jnp.sum(sums[0:1, :], axis=1, keepdims=True) + prior
    message = jnp.where(slot_rows, dz, 0.0)
    message = jnp.where(sub1 == 0, jnp.broadcast_to(loss_here, (8, CODE)), message)
    grads_buf[place.core, place.at[0], place.at[1], place.at[2]] = message
    spread = Gather(place, grads_buf, [(0, 8)], [(0, 1, 2)], dsend, drecv)
    spread.start(0, 0)

    g1[0:CODE, :] = dot_tn(z8, d1, EXACT)
    g1[CODE : CODE + 8, :] = jnp.where(sub1 < 3, outer1, 0.0)
    along1 = jnp.sum(v1[...] * g1[...], axis=0, keepdims=True)
    g1[...] = g1[...] * scale1 - v1[...] * (scale1 * inv1 * inv1 * along1)
    g2[0:H2, :] = dot_tn(z_wide, d2, EXACT)
    g2[0:256, :] = g2[0:256, :] + jnp.where(iota((256, H2), 0) < INNER, dw2[0:256, :], 0.0)
    g2[H2 - 8 : H2, :] = g2[H2 - 8 : H2, :] + jnp.where(sub2 >= 5, dw2[248:256, :], 0.0)
    along2 = jnp.sum(v2[0:H2, :] * g2[0:H2, :], axis=0, keepdims=True)
    g2[0:H2, :] = g2[0:H2, :] * scale2 - v2[0:H2, :] * (scale2 * inv2 * inv2 * along2)
    g2[H2 : H2 + 8, :] = dot_nt(jnp.ones((8, LANES), F32), dhead[...], EXACT)
    dbias = jnp.broadcast_to(jnp.sum(sums[1:2, :], axis=1, keepdims=True), (1, LANES))
    pack_first(g1, wide, flat)
    pack_second(g2, flat)
    pack_tail(
        [
            along1 * inv1,
            along2 * inv2,
            jnp.sum(d1, axis=0, keepdims=True),
            jnp.sum(d2, axis=0, keepdims=True),
            dbias,
        ],
        flat,
    )
    gather.finish()
    codes.finish()
    scatter(dims, per_device, kept, flat, buf)
    reduce = Reduce(place, buf, landing, cfg["chunks"], cfg["reduce_orders"], rsend, rrecv, True)
    for k in chunk_ids:
        reduce.start(k, -1)
    for stage in range(-1, 3):
        for k in chunk_ids:
            reduce.arrive(k, stage)
            if stage < 2:
                reduce.start(k, stage + 1)
        spread.arrive(0, stage + 1)
        if stage < 2:
            spread.start(0, stage + 2)
    grad_ref[...] = buf[place.core, place.at[0], place.at[1], place.at[2]]

    everyone = grads_buf[...].reshape(2 * slots, CODE)
    kind = iota((shapes, 2 * slots), 1) & 7
    owner = ((iota((shapes, 2 * slots), 1) >> 3) & (rows - 1)) * 2 + (iota((shapes, 2 * slots), 1) >> int(math.log2(slots)))
    shape_id = iota((shapes, 2 * slots), 0)
    asked = jnp.where(
        kind == 3,
        (shape_id.astype(F32) == shared).astype(F32),
        jnp.where((kind == 4) | (kind == 5), (shape_id == owner * 2 + kind - 4).astype(F32), 0.0),
    )
    code_rows = table_ref.shape[0]
    target_row = dot(codes_of, asked, EXACT)[0:1, :] - 1.0 - base
    pick = (target_row == iota((code_rows, 2 * slots), 0).astype(F32)).astype(F32)
    grad_table = dot(pick, everyone, EXACT)
    here_codes = (codes_of[0:1, :] - 1.0 - base) == iota((code_rows, shapes), 0).astype(F32)
    is_used = jnp.sum(here_codes.astype(F32), axis=1, keepdims=True) > 0.5
    table, code_first, code_second = table_ref[...], code_first_ref[...], code_second_ref[...]
    first_new = BETA_FIRST * code_first + (1.0 - BETA_FIRST) * grad_table
    second_new = BETA_SECOND * code_second + (1.0 - BETA_SECOND) * grad_table * grad_table
    step_vals = (
        CODE_RATE
        * (first_new / (1.0 - BETA_FIRST**STEP))
        / (jnp.sqrt(second_new / (1.0 - BETA_SECOND**STEP)) + ADAM_EPS)
    )
    new_table_ref[...] = jnp.where(is_used, table - step_vals, table)
    new_first_ref[...] = jnp.where(is_used, first_new, code_first)
    new_second_ref[...] = jnp.where(is_used, second_new, code_second)
    loss_ref[...] = jnp.sum(grads_buf[:, :, :, :, 0:8, 0:LANES], axis=(0, 1, 2, 3))[0:1, 0:1]
    spread.finish()
    reduce.finish()


def chunked(rows, count):
    blocks = rows // 8
    count = min(count, blocks)
    out, at = [], 0
    for k in range(count):
        size = (blocks * (k + 1)) // count * 8 - at
        out.append((at, size))
        at += size
    return out


def shards(rows, params, momentum, average, table, code_first, code_second, coords, targets, segment_ids, shape_code):
    per_device = params.shape[0]
    devices = 2 * rows
    used, kept = piece_rows(per_device, devices)
    dims = chip_dims(rows)
    device = lax.axis_index(("rows", "mp"))
    phase = (device * per_device) % LANES
    piece = lax.dynamic_update_slice(jnp.zeros((kept * LANES,), F32), params, (phase,)).reshape(kept, LANES)
    points_here = segment_ids.shape[0]
    tile = 512
    tiles = points_here // tile
    shapes = shape_code.shape[0]
    code_rows = table.shape[0]
    chunks = chunked(kept, 4)
    cfg = dict(
        dims=dims,
        rows=rows,
        per_device=per_device,
        tile=tile,
        shapes=shapes,
        chunks=chunks,
        gather_orders=[(0, 1, 2), (0, 2, 1)],
        reduce_orders=[(1, 2, 0), (2, 1, 0)],
    )
    flat_rows = per_device * devices // LANES + kept + 8
    most = max(dims)
    n = len(chunks)
    vm = pltpu.VMEM
    dma = pltpu.SemaphoreType.DMA
    scratch = [
        vm((2,) + dims + (kept, LANES), F32),
        landings(dims, cfg["reduce_orders"], (kept, LANES)),
        vm((flat_rows, LANES), F32),
        vm((272, 256), F32),
        vm((264, 256), F32),
        vm((520, H2), F32),
        vm((264, 256), F32),
        vm((520, H2), F32),
        vm((H2, 768), BF16),
        vm((256, H2), BF16),
        vm((256, LANES), BF16),
        vm((3, H2, LANES), F32),
        vm((H2, LANES), F32),
        vm((4, tiles, tile), F32),
        vm((784, tile), BF16),
        vm((256, tile), F32),
        vm((256, tile), F32),
        vm((H2, tile), F32),
        vm((H2, tile), F32),
        vm((H2, tile), F32),
        vm((H2, tile), BF16),
        vm((256, tile), F32),
        vm((256, tile), BF16),
        vm((272, H2), F32),
        vm((16, 256), F32),
        vm((H2, LANES), F32),
        vm((8, tile), F32),
        vm((2,) + dims + (8, CODE), F32),
        landings(dims, [(2, 1, 0)], (8, CODE)),
        vm((2,) + dims + (8, CODE), F32),
        dma((n, 4, most)),
        dma((n, 4, most)),
        dma((1, 4, most)),
        dma((1, 4, most)),
        dma((1, 4, most)),
        dma((1, 4, most)),
        dma((n, 4, most)),
        dma((n, 4, most)),
    ]
    spec = pl.BlockSpec(memory_space=pltpu.VMEM)
    loss, grad, new_table, new_first, new_second = pl.pallas_call(
        functools.partial(kernel, cfg),
        out_shape=(
            jax.ShapeDtypeStruct((1, 1), F32),
            jax.ShapeDtypeStruct((kept, LANES), F32),
            jax.ShapeDtypeStruct((code_rows, CODE), F32),
            jax.ShapeDtypeStruct((code_rows, CODE), F32),
            jax.ShapeDtypeStruct((code_rows, CODE), F32),
        ),
        in_specs=[spec] * 8,
        out_specs=(spec,) * 5,
        scratch_shapes=scratch,
        compiler_params=pltpu.CompilerParams(
            collective_id=0, has_side_effects=True, vmem_limit_bytes=56 << 20
        ),
    )(
        piece,
        table,
        code_first,
        code_second,
        coords,
        targets.reshape(-1, LANES),
        segment_ids.reshape(-1, LANES),
        shape_code.reshape(1, shapes),
    )
    grad_shard = lax.dynamic_slice(grad.reshape(-1), (phase,), (per_device,))
    new_momentum = MOMENTUM_DECAY * momentum + grad_shard
    new_params = params - LEARN_RATE * (grad_shard + MOMENTUM_DECAY * new_momentum)
    new_average = AVERAGE_DECAY * average + (1.0 - AVERAGE_DECAY) * new_params
    return (loss.reshape(()), new_momentum, new_params, new_average, new_table, new_first, new_second)


def solution(mesh):
    flat = P(("rows", "mp"))
    placed = (flat, flat, flat, P("rows", None), P("rows", None), P("rows", None), P(None, ("rows", "mp")), flat, flat, P())
    return jax.shard_map(
        functools.partial(shards, mesh.shape["rows"]),
        mesh=mesh,
        in_specs=placed,
        out_specs=(P(), flat, flat, flat, P("rows", None), P("rows", None), P("rows", None)),
        check_vma=False,
    )
```

```python
import functools
import math

import jax
import jax.numpy as jnp
from jax import lax
from jax.experimental import pallas as pl
from jax.experimental.pallas import tpu as pltpu
from jax.sharding import PartitionSpec as P

MESH = pl.DeviceIdType.MESH
F32, BF16 = jnp.float32, jnp.bfloat16
EXACT = lax.Precision.HIGHEST
CODE = 256
H2 = 512
INNER = H2 - CODE - 3
STEP = 10
CLAMP_DELTA = 0.1
SMOOTH = 0.01
PRIOR_WEIGHT = 0.001
LEARN_RATE = 200.0
MOMENTUM_DECAY = 0.9
AVERAGE_DECAY = 0.9
CODE_RATE = 0.5
BETA_FIRST = 0.9
BETA_SECOND = 0.999
ADAM_EPS = 1e-08
NORM_EPS = 1e-12
LANES = 128

SECOND_AT = (CODE + 3) * INNER
SECOND_ROW, SHIFT = divmod(SECOND_AT, LANES)
TAIL_AT = SECOND_AT + H2 * H2 + H2
TAIL_ROW = TAIL_AT // LANES
TAIL_PIECES = (INNER, H2, INNER, H2, 1)


def chip_dims(rows):
    return {16: (4, 2, 2), 128: (4, 4, 8)}.get(rows, (rows, 1, 1))


def piece_rows(per_device, devices):
    most = max((per_device * d) % LANES for d in range(devices))
    rows = -(-(most + per_device) // LANES)
    return rows, (rows // 8 + 1) * 8


class Place:
    def __init__(self, dims):
        self.dims = dims
        self.row = lax.axis_index("rows")
        self.core = lax.axis_index("mp")
        d0, d1, d2 = dims
        self.at = [self.row // (d1 * d2), (self.row // d2) % d1, self.row % d2]

    def peer(self, dim, step):
        at = list(self.at)
        at[dim] = (at[dim] + step) % self.dims[dim]
        d0, d1, d2 = self.dims
        return at[dim], ((at[0] * d1 + at[1]) * d2 + at[2], self.core)

    def sibling(self):
        return (self.row, 1 - self.core)

    def steps(self, dim):
        return range(1, self.dims[dim])


def remote(src, dst, send, recv, device):
    return pltpu.make_async_remote_copy(
        src, dst, send, recv, device_id=device, device_id_type=MESH
    )


class Gather:
    def __init__(self, place, buf, chunks, orders, send, recv):
        self.p, self.buf, self.chunks, self.orders = place, buf, chunks, orders
        self.send, self.recv, self.live = send, recv, {}

    def view(self, done, core, k):
        idx = [slice(None) if d in done else self.p.at[d] for d in range(3)]
        begin, size = self.chunks[k]
        return self.buf.at[core, idx[0], idx[1], idx[2], pl.ds(begin, size)]

    def start(self, k, stage):
        order = self.orders[k % len(self.orders)]
        core = self.p.core
        copies = []
        if stage == 3:
            v = self.view(order, core, k)
            copies.append(remote(v, v, self.send.at[k, 3, 0], self.recv.at[k, 3, 0], self.p.sibling()))
        else:
            for o in self.p.steps(order[stage]):
                v = self.view(order[:stage], core, k)
                dev = self.p.peer(order[stage], o)[1]
                copies.append(remote(v, v, self.send.at[k, stage, o], self.recv.at[k, stage, o], dev))
        for c in copies:
            c.start()
        self.live[k, stage] = copies

    def arrive(self, k, stage):
        for c in self.live[k, stage]:
            c.wait_recv()

    def finish(self):
        for copies in self.live.values():
            for c in copies:
                c.wait_send()


class Reduce:
    def __init__(self, place, buf, landing, chunks, orders, send, recv, cores):
        self.p, self.buf, self.landing, self.chunks, self.orders = place, buf, landing, chunks, orders
        self.send, self.recv, self.cores, self.live = send, recv, cores, {}

    def index(self, k, stage, last):
        order = self.orders[k % len(self.orders)]
        idx = [self.p.at[d] if d in order[:stage] else slice(None) for d in range(3)]
        if last is not None:
            idx[order[stage]] = last
        begin, size = self.chunks[k]
        return tuple(idx) + (pl.ds(begin, size),)

    def landed(self, k, stage, o):
        ref = self.landing[1 + 3 * (k % len(self.orders)) + stage]
        begin, size = self.chunks[k]
        return ref.at[(o - 1,) + (slice(None),) * (2 - stage) + (pl.ds(begin, size),)]

    def start(self, k, stage):
        order = self.orders[k % len(self.orders)]
        copies = []
        if stage < 0:
            idx = self.index(k, 0, None)
            copies.append(
                remote(
                    self.buf.at[(1 - self.p.core,) + idx],
                    self.landing[0].at[idx],
                    self.send.at[k, 3, 0],
                    self.recv.at[k, 3, 0],
                    self.p.sibling(),
                )
            )
        else:
            for o in self.p.steps(order[stage]):
                at, dev = self.p.peer(order[stage], o)
                idx = self.index(k, stage, at)
                copies.append(
                    remote(
                        self.buf.at[(self.p.core,) + idx],
                        self.landed(k, stage, o),
                        self.send.at[k, stage, o],
                        self.recv.at[k, stage, o],
                        dev,
                    )
                )
        for c in copies:
            c.start()
        self.live[k, stage] = copies

    def arrive(self, k, stage):
        for c in self.live[k, stage]:
            c.wait_recv()
        order = self.orders[k % len(self.orders)]
        if stage < 0:
            idx = self.index(k, 0, None)
            mine = (self.p.core,) + idx
            self.buf[mine] = self.buf[mine] + self.landing[0][idx]
        else:
            idx = self.index(k, stage, self.p.at[order[stage]])
            mine = (self.p.core,) + idx
            total = self.buf[mine]
            for o in self.p.steps(order[stage]):
                total = total + self.landed(k, stage, o)[...]
            self.buf[mine] = total

    def finish(self):
        for copies in self.live.values():
            for c in copies:
                c.wait_send()


def landings(dims, orders, tail):
    shapes = [tuple(dims) + tail]
    for order in orders:
        for stage, d in enumerate(order):
            rest = tuple(dims[e] for e in range(3) if e not in order[: stage + 1])
            shapes.append((max(dims[d] - 1, 1),) + rest + tail)
    return [pltpu.VMEM(shape, F32) for shape in shapes]


def iota(shape, dim):
    return lax.broadcasted_iota(jnp.int32, shape, dim)


def dot(a, b, precision=None):
    return jnp.dot(a, b, precision=precision, preferred_element_type=F32)


def dot_nt(a, b, precision=None):
    return lax.dot_general(
        a, b, (((1,), (1,)), ((), ())), precision=precision, preferred_element_type=F32
    )


def dot_tn(a, b, precision=None):
    return lax.dot_general(
        a, b, (((0,), (0,)), ((), ())), precision=precision, preferred_element_type=F32
    )


def turn(x, by):
    by = by % x.shape[1]
    return pltpu.roll(x, by, 1) if by else x


def widen(x, width):
    return jnp.concatenate([x, jnp.zeros((x.shape[0], width - x.shape[1]), F32)], axis=1)


def one_row(x, count):
    return jnp.concatenate([x[k : k + 1] for k in range(count)], axis=1)


def rows_of(ref, count):
    whole = count // LANES
    rows = ref[pl.ds(0, whole * LANES)].reshape(whole, LANES)
    if count % LANES:
        rest = ref[pl.ds(whole * LANES, count % LANES)].reshape(1, count % LANES)
        rows = jnp.concatenate([rows, widen(rest, LANES)], axis=0)
    return rows


def store_rows(ref, rows, count):
    whole = count // LANES
    ref[pl.ds(0, whole * LANES)] = rows[:whole].reshape(whole * LANES)
    if count % LANES:
        ref[pl.ds(whole * LANES, count % LANES)] = rows[whole : whole + 1, : count % LANES].reshape(count % LANES)


def update(
    per_device,
    grad_ref,
    grad_table_ref,
    used_ref,
    loss_in_ref,
    params_ref,
    momentum_ref,
    average_ref,
    table_ref,
    code_first_ref,
    code_second_ref,
    loss_ref,
    new_momentum_ref,
    new_params_ref,
    new_average_ref,
    new_table_ref,
    new_first_ref,
    new_second_ref,
):
    count = -(-per_device // LANES)
    grad = grad_ref[0:count, :]
    params = rows_of(params_ref, per_device)
    new_momentum = MOMENTUM_DECAY * rows_of(momentum_ref, per_device) + grad
    new_params = params - LEARN_RATE * (grad + MOMENTUM_DECAY * new_momentum)
    new_average = AVERAGE_DECAY * rows_of(average_ref, per_device) + (1.0 - AVERAGE_DECAY) * new_params
    store_rows(new_momentum_ref, new_momentum, per_device)
    store_rows(new_params_ref, new_params, per_device)
    store_rows(new_average_ref, new_average, per_device)
    grad_table = grad_table_ref[...]
    is_used = used_ref[...] > 0.5
    table, code_first, code_second = table_ref[...], code_first_ref[...], code_second_ref[...]
    first_new = BETA_FIRST * code_first + (1.0 - BETA_FIRST) * grad_table
    second_new = BETA_SECOND * code_second + (1.0 - BETA_SECOND) * grad_table * grad_table
    step_vals = (
        CODE_RATE
        * (first_new / (1.0 - BETA_FIRST**STEP))
        / (jnp.sqrt(second_new / (1.0 - BETA_SECOND**STEP)) + ADAM_EPS)
    )
    new_table_ref[...] = jnp.where(is_used, table - step_vals, table)
    new_first_ref[...] = jnp.where(is_used, first_new, code_first)
    new_second_ref[...] = jnp.where(is_used, second_new, code_second)
    loss_ref[...] = loss_in_ref[...]


def bounds(devices, per_device):
    for d in range(devices):
        row, phase = divmod(per_device * d, LANES)
        yield d, row, phase, -(-(phase + per_device) // LANES)


def assemble(dims, per_device, buf, flat):
    rows = dims[0] * dims[1] * dims[2]
    for d, row, phase, count in bounds(2 * rows, per_device):
        chip = d // 2
        src = buf.at[d % 2, chip // (dims[1] * dims[2]), (chip // dims[2]) % dims[1], chip % dims[2]]
        if phase:
            flat[row : row + 1, :] = flat[row : row + 1, :] + src[0:1, :]
            flat[row + 1 : row + count, :] = src[1:count, :]
        else:
            flat[row : row + count, :] = src[0:count, :]


def scatter(dims, per_device, rows_kept, flat, buf):
    rows = dims[0] * dims[1] * dims[2]
    for d, row, phase, count in bounds(2 * rows, per_device):
        chip = d // 2
        dst = buf.at[d % 2, chip // (dims[1] * dims[2]), (chip // dims[2]) % dims[1], chip % dims[2]]
        dst[...] = flat[row : row + rows_kept, :]


def first_blocks():
    for back in range(4):
        begin = -(-256 * back // 3)
        end = min(-(-256 * (back + 1) // 3), CODE + 3)
        for at in range(begin, end, 8):
            yield back, at, min(8, end - at)


def unpack_first(flat, wide, v1):
    wide[0:8, :] = jnp.zeros((8, 256), F32)
    for half in range(2):
        lanes = slice(half * LANES, (half + 1) * LANES)
        wide[8:272, lanes] = flat[pl.ds(half, 264, stride=2), :]
    v1[256:264, :] = jnp.zeros((8, 256), F32)
    for back, at, n in first_blocks():
        base = 3 * at - 256 * back
        lane = iota((n, 256), 1)
        move = base + 3 * iota((n, 256), 0)
        here = wide[8 + at - back : 8 + at - back + n, :]
        before = wide[7 + at - back : 7 + at - back + n, :]
        mixed = jnp.where(lane < 256 - move, here, before)
        mixed = turn(mixed, base)
        if n > 1:
            mixed = pltpu.roll(mixed, 0, 1, stride=3, stride_axis=0)
        v1[at : at + n, :] = jnp.where(lane < INNER, mixed, 0.0)


def pack_first(v1, wide, flat):
    wide[...] = jnp.zeros(wide.shape, F32)
    for back, at, n in first_blocks():
        base = 3 * at - 256 * back
        lane = iota((n, 256), 1)
        sub = iota((n, 256), 0)
        moved = turn(v1[at : at + n, :], -base)
        for bit in range(3):
            moved = jnp.where((sub >> bit) & 1 == 1, turn(moved, -3 * (1 << bit)), moved)
        here = lane < 256 - (base + 3 * sub)
        a = slice(8 + at - back, 8 + at - back + n)
        b = slice(7 + at - back, 7 + at - back + n)
        wide[a, :] = wide[a, :] + jnp.where(here, moved, 0.0)
        wide[b, :] = wide[b, :] + jnp.where(here, 0.0, moved)
    for half in range(2):
        lanes = slice(half * LANES, (half + 1) * LANES)
        flat[pl.ds(half, 256, stride=2), :] = wide[8:264, lanes]


def unpack_second(flat, v2):
    for q in range(H2 // LANES):
        lanes = slice(q * LANES, (q + 1) * LANES)
        for at in range(0, H2 + 8, 104):
            rows = flat[pl.ds(SECOND_ROW + q + 4 * at, 104, stride=4), :]
            if q == 0:
                after = flat[pl.ds(SECOND_ROW + 4 + 4 * at, 104, stride=4), :]
                rows = jnp.where(iota((104, LANES), 1) < SHIFT, after, rows)
            v2[at : at + 104, lanes] = rows


def pack_second(v2, flat):
    low = iota((1, LANES), 1) < SHIFT
    for q in range(1, H2 // LANES):
        lanes = slice(q * LANES, (q + 1) * LANES)
        flat[pl.ds(SECOND_ROW + q, H2, stride=4), :] = v2[0:H2, lanes]
        flat[SECOND_ROW + q + 4 * H2 : SECOND_ROW + q + 4 * H2 + 1, :] = v2[H2 : H2 + 1, lanes]
    flat[pl.ds(SECOND_ROW + 4, H2, stride=4), :] = jnp.where(low, v2[0:H2, 0:LANES], v2[1 : H2 + 1, 0:LANES])
    flat[SECOND_ROW : SECOND_ROW + 1, :] = jnp.where(
        low, flat[SECOND_ROW : SECOND_ROW + 1, :], v2[0:1, 0:LANES]
    )
    flat[TAIL_ROW : TAIL_ROW + 1, :] = jnp.where(low, v2[H2 : H2 + 1, 0:LANES], 0.0)


def unpack_tail(flat):
    count = 13
    tail = one_row(flat[TAIL_ROW : TAIL_ROW + count, :], count)
    at = SHIFT
    parts = []
    for width in TAIL_PIECES:
        lanes = {INNER: 256, H2: H2, 1: LANES}[width]
        piece = turn(tail, -at)[:, 0:lanes]
        if width == H2:
            piece = turn(piece, SHIFT)
        else:
            piece = jnp.where(iota((1, lanes), 1) < width, piece, 0.0)
        parts.append(piece)
        at += width
    return parts


def pack_tail(parts, flat):
    count = 13
    at = SHIFT
    total = jnp.zeros((1, count * LANES), F32)
    for width, piece in zip(TAIL_PIECES, parts):
        if width == H2:
            piece = turn(piece, -SHIFT)
        else:
            piece = jnp.where(iota(piece.shape, 1) < width, piece, 0.0)
        total = total + turn(widen(piece, count * LANES), at)
        at += width
    flat[TAIL_ROW : TAIL_ROW + 1, :] = flat[TAIL_ROW : TAIL_ROW + 1, :] + total[:, 0:LANES]
    for k in range(1, count):
        flat[TAIL_ROW + k : TAIL_ROW + k + 1, :] = total[:, k * LANES : (k + 1) * LANES]


def split2(x):
    high = x.astype(BF16)
    return high, (x - high.astype(F32)).astype(BF16)


def split3(x):
    a = x.astype(BF16).astype(F32)
    b = (x - a).astype(BF16).astype(F32)
    return a, b, x - a - b


def kernel(
    cfg,
    params_ref,
    table_ref,
    coords_ref,
    targets_ref,
    seg_ref,
    shape_code_ref,
    loss_ref,
    grad_ref,
    grad_table_ref,
    used_ref,
    buf,
    landing,
    flat,
    wide,
    v1,
    v2,
    g1,
    g2,
    w2t,
    w2b,
    w0,
    bias,
    head,
    points,
    hc,
    h1,
    slope1,
    h2,
    act,
    second,
    preds,
    d2b,
    df,
    d1b,
    dw2,
    dw1,
    dhead,
    sums,
    codes_buf,
    codes_landing,
    grads_buf,
    psend,
    precv,
    csend,
    crecv,
    dsend,
    drecv,
    rsend,
    rrecv,
):
    dims, per_device, tile = cfg["dims"], cfg["per_device"], cfg["tile"]
    used, kept = piece_rows(per_device, 2 * cfg["rows"])
    rows = cfg["rows"]
    shapes = cfg["shapes"]
    place = Place(dims)
    device = place.row * 2 + place.core
    tiles = seg_ref.shape[0] * LANES // tile
    per_tile = tile // LANES
    head_len = seg_ref.shape[0] * LANES // 16

    barrier = pltpu.get_barrier_semaphore()
    greeted = 1
    pl.semaphore_signal(barrier, inc=1, device_id=place.sibling(), device_id_type=MESH)
    for dim in range(3):
        for o in place.steps(dim):
            pl.semaphore_signal(barrier, inc=1, device_id=place.peer(dim, o)[1], device_id_type=MESH)
            greeted += 1

    seg_heads = seg_ref[0 : head_len // LANES, :].astype(F32)
    shared = jnp.max(jnp.max(seg_heads, axis=1, keepdims=True), axis=0, keepdims=True)
    for q in range(per_tile):
        lanes = slice(q * LANES, (q + 1) * LANES)
        points[0, :, lanes] = seg_ref[pl.ds(q, tiles, stride=per_tile), :].astype(F32)
        points[1, :, lanes] = jnp.tanh(targets_ref[pl.ds(q, tiles, stride=per_tile), :] * (1.0 / CLAMP_DELTA))
    seg = points[0]

    def count(where):
        return jnp.sum(jnp.sum(where.astype(F32), axis=1, keepdims=True), axis=0, keepdims=True)

    mine = (device * 2).astype(F32)
    counts = [count(seg == shared), count(seg == mine), count(seg == mine + 1.0)]

    phase = (device * per_device) % LANES
    own = buf.at[place.core, place.at[0], place.at[1], place.at[2]]
    raw = rows_of(params_ref, per_device)
    raw = jnp.concatenate(
        [raw, jnp.zeros((kept - 1 - raw.shape[0], LANES), F32), jnp.broadcast_to(counts[0], (1, LANES))], axis=0
    )
    if any(p for _, _, p, _ in bounds(2 * rows, per_device)):
        moved = pltpu.roll(raw, phase, 1)
        before = jnp.concatenate([jnp.zeros((1, LANES), F32), moved[: kept - 1]], axis=0)
        raw = jnp.where((iota((kept, LANES), 1) < phase) & (iota((kept, LANES), 0) < kept - 1), before, moved)
    own[...] = raw

    base = (place.row * table_ref.shape[0]).astype(F32)
    codes_of = jnp.broadcast_to(shape_code_ref[...].astype(F32) + 1.0, (8, shapes))
    slots = rows * 8
    kind = iota((slots, shapes), 0) & 7
    owner = (iota((slots, shapes), 0) >> 3) * 2 + place.core
    shape_id = iota((slots, shapes), 1)
    asked = jnp.where(
        kind == 3,
        (shape_id.astype(F32) == shared).astype(F32),
        jnp.where((kind == 4) | (kind == 5), (shape_id == owner * 2 + kind - 4).astype(F32), 0.0),
    )
    wanted = dot_nt(asked, codes_of, EXACT)[:, 0:1] - 1.0 - base
    pick = (wanted == iota((slots, table_ref.shape[0]), 1).astype(F32)).astype(F32)
    answer = dot(pick, table_ref[...], EXACT)
    codes_buf[place.core] = answer.reshape(dims + (8, CODE))

    pl.semaphore_wait(barrier, greeted)
    gather = Gather(place, buf, cfg["chunks"], cfg["gather_orders"], psend, precv)
    chunk_ids = range(len(cfg["chunks"]))
    for k in chunk_ids:
        gather.start(k, 0)

    codes = Reduce(place, codes_buf, codes_landing, [(0, 8)], [(2, 1, 0)], csend, crecv, False)
    codes.start(0, 0)

    for stage in range(4):
        if stage < 3:
            codes.arrive(0, stage)
            if stage < 2:
                codes.start(0, stage + 1)
        for k in chunk_ids:
            gather.arrive(k, stage)
            if stage < 3:
                gather.start(k, stage + 1)
    z8 = codes_buf[place.core, place.at[0], place.at[1], place.at[2]]

    assemble(dims, per_device, buf, flat)
    unpack_first(flat, wide, v1)
    unpack_second(flat, v2)
    gain1, gain2, bias1, bias2, head_bias = unpack_tail(flat)
    norm1 = jnp.sum(v1[...] * v1[...], axis=0, keepdims=True) + NORM_EPS
    norm2 = jnp.sum(v2[0:H2, :] * v2[0:H2, :], axis=0, keepdims=True) + NORM_EPS
    inv1, inv2 = lax.rsqrt(norm1), lax.rsqrt(norm2)
    scale1, scale2 = gain1 * inv1, gain2 * inv2
    head_row = v2[H2 : H2 + 1, :]
    hbias = head_bias[:, 0:1]

    total = jnp.sum(buf[:, :, :, :, kept - 8 : kept, :], axis=(0, 1, 2, 3))[7:8, 0:1]
    counts_all = [total]
    for k in (1, 2):
        counts_all.append(jnp.where(shared == mine + (k - 1.0), total, jnp.maximum(counts[k], 1.0)))
    inv_counts = [1.0 / (n * float(shapes)) for n in counts_all]
    position = iota((tiles, tile), 0) * tile + iota((tiles, tile), 1)
    is_two = (seg == mine + 1.0) & (position >= head_len)
    per_point = jnp.where(
        position < head_len, inv_counts[0], jnp.where(is_two, inv_counts[2], inv_counts[1])
    )
    points[2] = jnp.where(seg >= 0.0, per_point, 0.0)
    points[3] = jnp.where(is_two, 1.0, 0.0)

    lane1 = iota((8, 256), 1)
    sub1 = iota((8, 256), 0)
    code1 = dot(z8, v1[0:CODE, :], EXACT) * scale1 + bias1
    xyz1 = v1[CODE : CODE + 8, :] * scale1
    rows1 = 0.5 * jnp.where(sub1 < 3, xyz1, jnp.where(sub1 < 6, code1, 0.0))
    rows1 = jnp.where(lane1 < INNER, rows1, (lane1 == INNER + sub1).astype(F32))
    rows1 = jnp.where(sub1 < 6, rows1, 0.0)
    wa, wb, wc = split3(rows1)
    stack = jnp.concatenate([wa, wa, wb, wb, wa, wc] + [jnp.zeros((8, 256), F32)] * 10, axis=0)
    w0[...] = stack.T.astype(BF16)

    z_wide = turn(widen(z8, H2), INNER)
    code2 = 0.5 * (dot(z_wide, v2[0:H2, :], EXACT) * scale2 + bias2)
    sub2 = iota((8, H2), 0)
    columns = jnp.where(sub2 == 6, jnp.broadcast_to(0.5 * head_row, (8, H2)), code2)
    columns = jnp.concatenate([columns, jnp.zeros((LANES - 8, H2), F32)], axis=0).T
    for k in range(3):
        bias[k] = jnp.broadcast_to(columns[:, 3 + k : 4 + k], (H2, LANES))
    head[...] = jnp.broadcast_to(columns[:, 6:7], (H2, LANES))
    last = jnp.where(sub2 < 5, v2[248:256, :], v2[H2 - 8 : H2, :])
    normal = jnp.concatenate([v2[0:248, :], last], axis=0) * scale2
    w2b[...] = normal.astype(BF16)
    high, low = split2(0.5 * normal.T)
    w2t[:, 0:256] = high
    w2t[:, 256:512] = high
    w2t[:, 512:768] = low

    dw2[...] = jnp.zeros(dw2.shape, F32)
    dw1[...] = jnp.zeros(dw1.shape, F32)
    dhead[...] = jnp.zeros(dhead.shape, F32)
    sums[...] = jnp.zeros(sums.shape, F32)
    block = 32

    def lanes_of(q):
        return slice(q * LANES, (q + 1) * LANES)

    def first_layer(t):
        at = slice(t * tile, (t + 1) * tile)
        two = points[3, t : t + 1, :]
        is_head = (t * tile + iota((1, tile), 1) < head_len).astype(F32)
        x8 = jnp.concatenate(
            [coords_ref[:, at], is_head, 1.0 - two - is_head, two, jnp.zeros((2, tile), F32)], axis=0
        )
        xa, xb, xc = split3(x8)
        x48 = jnp.concatenate([xa, xb, xa, xb, xc, xa], axis=0).astype(BF16)
        hc[t % 2, 768:784, :] = jnp.concatenate([xa, xb], axis=0).astype(BF16)
        h1[...] = dot(w0[:, 0:48], x48)
        for q in range(per_tile):
            lanes = lanes_of(q)
            for u in range(0, 256, block):
                us = slice(u, u + block)
                h = h1[us, lanes]
                th = jnp.tanh(h)
                m = h * th
                f = h + m
                slope1[t % 2, us, lanes] = (0.5 + 0.5 * th) * (1.0 + (h - m))
                if u + block > INNER:
                    f = jnp.where(iota((block, LANES), 0) + u >= INNER, h, f)
                fh, fl = split2(f)
                hc[t % 2, us, lanes] = fh
                hc[t % 2, 256 + u : 256 + u + block, lanes] = fl
                hc[t % 2, 512 + u : 512 + u + block, lanes] = fh

    def second_product(t):
        h2[t % 2] = dot(w2t[...], hc[t % 2, 0:768, :])

    def second_layer(t):
        parts = []
        for q in range(per_tile):
            lanes = lanes_of(q)
            in_head = t * per_tile + q < head_len // LANES
            is_second = jnp.broadcast_to(points[3, t : t + 1, lanes], (block, LANES)) > 0.5
            part = jnp.zeros((8, LANES), F32)
            for u in range(0, H2, block):
                us = slice(u, u + block)
                b = bias[0, us, :] if in_head else jnp.where(is_second, bias[2, us, :], bias[1, us, :])
                h = h2[t % 2, us, lanes] + b
                th = jnp.tanh(h)
                m = h * th
                s = h + m
                hw = head[us, :]
                second[t % 2, us, lanes] = s
                act[t % 2, us, lanes] = hw * ((1.0 + th) * (1.0 + (h - m)))
                w = hw * s
                for v in range(0, block, 8):
                    part = part + w[v : v + 8]
            parts.append(jnp.sum(part, axis=0, keepdims=True))
        preds[t % 2, 0:1, :] = 2.0 * jnp.concatenate(parts, axis=1) + hbias

    def back_second(t):
        pred = jnp.tanh(preds[t % 2, 0:1, :])
        squash = jnp.tanh(pred * (1.0 / CLAMP_DELTA))
        resid = CLAMP_DELTA * squash - CLAMP_DELTA * points[1, t : t + 1, :]
        square = resid * resid + SMOOTH * SMOOTH
        inv_radius = lax.rsqrt(square)
        share = points[2, t : t + 1, :]
        dpred = share * (resid * inv_radius) * (1.0 - squash * squash) * (1.0 - pred * pred)
        sums[0:1, :] = sums[0:1, :] + share * (square * inv_radius - SMOOTH)
        sums[1:2, :] = sums[1:2, :] + dpred
        for u in range(0, H2, block):
            us = slice(u, u + block)
            total_u = dhead[us, :]
            for q in range(per_tile):
                lanes = lanes_of(q)
                dp = jnp.broadcast_to(dpred[:, lanes], (block, LANES))
                d2b[t % 2, us, lanes] = (act[t % 2, us, lanes] * dp).astype(BF16)
                total_u = total_u + second[t % 2, us, lanes] * dp
            dhead[us, :] = total_u

    def back_products(t):
        df[...] = dot(w2b[...], d2b[t % 2])
        dw2[...] = dw2[...] + dot_nt(hc[t % 2, 512:784, :], d2b[t % 2])

    def back_first(t):
        for u in range(0, 256, block):
            us = slice(u, u + block)
            d1b[us, :] = (df[us, :] * slope1[t % 2, us, :]).astype(BF16)
        dw1[...] = dw1[...] + dot_nt(hc[t % 2, 768:784, :], d1b[...])

    first_layer(0)
    for t in range(tiles + 1):
        if t < tiles:
            second_product(t)
        if t > 0:
            back_second(t - 1)
            back_products(t - 1)
        if t < tiles:
            second_layer(t)
        if t > 0:
            back_first(t - 1)
        if t + 1 < tiles:
            first_layer(t + 1)

    outer1 = jnp.where(lane1 < INNER, dw1[0:8, :] + dw1[8:16, :], 0.0)
    outer2 = dw2[256:264, :] + dw2[264:272, :]
    slot_rows = (sub1 >= 3) & (sub1 < 6)
    d1 = jnp.where(slot_rows, outer1, 0.0)
    d2 = jnp.where((sub2 >= 3) & (sub2 < 6), outer2, 0.0)
    dz = dot_nt(d1 * scale1, v1[0:CODE, :], EXACT)
    dz = dz + turn(dot_nt(d2 * scale2, v2[0:H2, :], EXACT), -INNER)[:, 0:CODE]
    own_rows = (sub1 == 4) | (sub1 == 5)
    dz = dz + jnp.where(own_rows, (2.0 * PRIOR_WEIGHT / shapes) * z8, 0.0)
    prior = jnp.where(own_rows, z8 * z8, 0.0)
    prior = (PRIOR_WEIGHT / shapes) * jnp.sum(jnp.sum(prior, axis=1, keepdims=True), axis=0, keepdims=True)
    loss_here = jnp.sum(sums[0:1, :], axis=1, keepdims=True) + prior
    message = jnp.where(slot_rows, dz, 0.0)
    message = jnp.where(sub1 == 0, jnp.broadcast_to(loss_here, (8, CODE)), message)
    grads_buf[place.core, place.at[0], place.at[1], place.at[2]] = message
    spread = Gather(place, grads_buf, [(0, 8)], [(0, 1, 2)], dsend, drecv)
    spread.start(0, 0)

    g1[0:CODE, :] = dot_tn(z8, d1, EXACT)
    g1[CODE : CODE + 8, :] = jnp.where(sub1 < 3, outer1, 0.0)
    along1 = jnp.sum(v1[...] * g1[...], axis=0, keepdims=True)
    g1[...] = g1[...] * scale1 - v1[...] * (scale1 * inv1 * inv1 * along1)
    g2[0:H2, :] = dot_tn(z_wide, d2, EXACT)
    g2[0:256, :] = g2[0:256, :] + jnp.where(iota((256, H2), 0) < INNER, dw2[0:256, :], 0.0)
    g2[H2 - 8 : H2, :] = g2[H2 - 8 : H2, :] + jnp.where(sub2 >= 5, dw2[248:256, :], 0.0)
    along2 = jnp.sum(v2[0:H2, :] * g2[0:H2, :], axis=0, keepdims=True)
    g2[0:H2, :] = g2[0:H2, :] * scale2 - v2[0:H2, :] * (scale2 * inv2 * inv2 * along2)
    g2[H2 : H2 + 8, :] = dot_nt(jnp.ones((8, LANES), F32), dhead[...], EXACT)
    dbias = jnp.broadcast_to(jnp.sum(sums[1:2, :], axis=1, keepdims=True), (1, LANES))
    pack_first(g1, wide, flat)
    pack_second(g2, flat)
    pack_tail(
        [
            along1 * inv1,
            along2 * inv2,
            jnp.sum(d1, axis=0, keepdims=True),
            jnp.sum(d2, axis=0, keepdims=True),
            dbias,
        ],
        flat,
    )
    gather.finish()
    codes.finish()
    scatter(dims, per_device, kept, flat, buf)
    reduce = Reduce(place, buf, landing, cfg["chunks"], cfg["reduce_orders"], rsend, rrecv, True)
    for k in chunk_ids:
        reduce.start(k, -1)
    for stage in range(-1, 3):
        for k in chunk_ids:
            reduce.arrive(k, stage)
            if stage < 2:
                reduce.start(k, stage + 1)
        spread.arrive(0, stage + 1)
        if stage < 2:
            spread.start(0, stage + 2)
    piece = own[...]
    if any(p for _, _, p, _ in bounds(2 * rows, per_device)):
        moved = pltpu.roll(piece, (LANES - phase) % LANES, 1)
        after = jnp.concatenate([moved[1:], moved[:1]], axis=0)
        piece = jnp.where(iota((kept, LANES), 1) < LANES - phase, moved, after)
    grad_ref[...] = piece

    everyone = grads_buf[...].reshape(2 * slots, CODE)
    kind = iota((shapes, 2 * slots), 1) & 7
    owner = ((iota((shapes, 2 * slots), 1) >> 3) & (rows - 1)) * 2 + (iota((shapes, 2 * slots), 1) >> int(math.log2(slots)))
    shape_id = iota((shapes, 2 * slots), 0)
    asked = jnp.where(
        kind == 3,
        (shape_id.astype(F32) == shared).astype(F32),
        jnp.where((kind == 4) | (kind == 5), (shape_id == owner * 2 + kind - 4).astype(F32), 0.0),
    )
    code_rows = table_ref.shape[0]
    target_row = dot(codes_of, asked, EXACT)[0:1, :] - 1.0 - base
    pick = (target_row == iota((code_rows, 2 * slots), 0).astype(F32)).astype(F32)
    grad_table = dot(pick, everyone, EXACT)
    here_codes = (codes_of[0:1, :] - 1.0 - base) == iota((code_rows, shapes), 0).astype(F32)
    is_used = jnp.sum(here_codes.astype(F32), axis=1, keepdims=True) > 0.5
    grad_table_ref[...] = grad_table
    used_ref[...] = jnp.broadcast_to(is_used.astype(F32), used_ref.shape)
    loss_ref[...] = jnp.sum(grads_buf[:, :, :, :, 0:8, 0:LANES], axis=(0, 1, 2, 3))[0:1, 0:1]
    spread.finish()
    reduce.finish()


def chunked(rows, count):
    blocks = rows // 8
    count = min(count, blocks)
    out, at = [], 0
    for k in range(count):
        size = (blocks * (k + 1)) // count * 8 - at
        out.append((at, size))
        at += size
    return out


def shards(rows, params, momentum, average, table, code_first, code_second, coords, targets, segment_ids, shape_code):
    per_device = params.shape[0]
    devices = 2 * rows
    used, kept = piece_rows(per_device, devices)
    dims = chip_dims(rows)
    points_here = segment_ids.shape[0]
    tile = 1024
    tiles = points_here // tile
    shapes = shape_code.shape[0]
    code_rows = table.shape[0]
    chunks = chunked(kept, 4)
    cfg = dict(
        dims=dims,
        rows=rows,
        per_device=per_device,
        tile=tile,
        shapes=shapes,
        chunks=chunks,
        gather_orders=[(0, 1, 2), (0, 2, 1)],
        reduce_orders=[(1, 2, 0), (2, 1, 0)],
    )
    flat_rows = per_device * devices // LANES + kept + 8
    most = max(dims)
    n = len(chunks)
    vm = pltpu.VMEM
    dma = pltpu.SemaphoreType.DMA
    scratch = [
        vm((2,) + dims + (kept, LANES), F32),
        landings(dims, cfg["reduce_orders"], (kept, LANES)),
        vm((flat_rows, LANES), F32),
        vm((272, 256), F32),
        vm((264, 256), F32),
        vm((520, H2), F32),
        vm((264, 256), F32),
        vm((520, H2), F32),
        vm((H2, 768), BF16),
        vm((256, H2), BF16),
        vm((256, LANES), BF16),
        vm((3, H2, LANES), F32),
        vm((H2, LANES), F32),
        vm((4, tiles, tile), F32),
        vm((2, 784, tile), BF16),
        vm((256, tile), F32),
        vm((2, 256, tile), F32),
        vm((2, H2, tile), F32),
        vm((2, H2, tile), F32),
        vm((2, H2, tile), F32),
        vm((2, 8, tile), F32),
        vm((2, H2, tile), BF16),
        vm((256, tile), F32),
        vm((256, tile), BF16),
        vm((272, H2), F32),
        vm((16, 256), F32),
        vm((H2, LANES), F32),
        vm((8, tile), F32),
        vm((2,) + dims + (8, CODE), F32),
        landings(dims, [(2, 1, 0)], (8, CODE)),
        vm((2,) + dims + (8, CODE), F32),
        dma((n, 4, most)),
        dma((n, 4, most)),
        dma((1, 4, most)),
        dma((1, 4, most)),
        dma((1, 4, most)),
        dma((1, 4, most)),
        dma((n, 4, most)),
        dma((n, 4, most)),
    ]
    spec = pl.BlockSpec(memory_space=pltpu.VMEM)
    loss, grad, grad_table, marks = pl.pallas_call(
        functools.partial(kernel, cfg),
        out_shape=(
            jax.ShapeDtypeStruct((1, 1), F32),
            jax.ShapeDtypeStruct((kept, LANES), F32),
            jax.ShapeDtypeStruct((code_rows, CODE), F32),
            jax.ShapeDtypeStruct((code_rows, CODE), F32),
        ),
        in_specs=[spec] * 6,
        out_specs=(spec,) * 4,
        scratch_shapes=scratch,
        compiler_params=pltpu.CompilerParams(
            collective_id=0, has_side_effects=True, vmem_limit_bytes=56 << 20
        ),
    )(
        params,
        table,
        coords,
        targets.reshape(-1, LANES),
        segment_ids.reshape(-1, LANES),
        shape_code.reshape(1, shapes),
    )
    flat_out = jax.ShapeDtypeStruct((per_device,), F32)
    table_out = jax.ShapeDtypeStruct((code_rows, CODE), F32)
    outs = pl.pallas_call(
        functools.partial(update, per_device),
        out_shape=(jax.ShapeDtypeStruct((1, 1), F32),) + (flat_out,) * 3 + (table_out,) * 3,
        in_specs=[spec] * 10,
        out_specs=(spec,) * 7,
    )(grad, grad_table, marks, loss, params, momentum, average, table, code_first, code_second)
    return (outs[0].reshape(()),) + tuple(outs[1:])


def solution(mesh):
    flat = P(("rows", "mp"))
    placed = (flat, flat, flat, P("rows", None), P("rows", None), P("rows", None), P(None, ("rows", "mp")), flat, flat, P())
    return jax.shard_map(
        functools.partial(shards, mesh.shape["rows"]),
        mesh=mesh,
        in_specs=placed,
        out_specs=(P(), flat, flat, flat, P("rows", None), P("rows", None), P("rows", None)),
        check_vma=False,
    )
```

```python
import functools
import itertools
import math

import jax
import jax.numpy as jnp
from jax import lax
from jax.experimental import pallas as pl
from jax.experimental.pallas import tpu as pltpu
from jax.sharding import PartitionSpec as P

MESH = pl.DeviceIdType.MESH
F32, BF16 = jnp.float32, jnp.bfloat16
EXACT = lax.Precision.HIGHEST
THREE = lax.Precision.HIGH
DEEP = 8
CODE = 256
H2 = 512
INNER = H2 - CODE - 3
STEP = 10
CLAMP_DELTA = 0.1
SMOOTH = 0.01
PRIOR_WEIGHT = 0.001
LEARN_RATE = 200.0
MOMENTUM_DECAY = 0.9
AVERAGE_DECAY = 0.9
CODE_RATE = 0.5
BETA_FIRST = 0.9
BETA_SECOND = 0.999
ADAM_EPS = 1e-08
NORM_EPS = 1e-12
LANES = 128

SECOND_AT = (CODE + 3) * INNER
SECOND_ROW, SHIFT = divmod(SECOND_AT, LANES)
TAIL_AT = SECOND_AT + H2 * H2 + H2
TAIL_ROW = TAIL_AT // LANES
TAIL_PIECES = (INNER, H2, INNER, H2, 1)


def chip_dims(rows):
    return {16: (4, 2, 2), 128: (4, 4, 8)}.get(rows, (rows, 1, 1))


def piece_rows(per_device, devices):
    most = max((per_device * d) % LANES for d in range(devices))
    rows = -(-(most + per_device) // LANES)
    return rows, rows + 1


class Place:
    def __init__(self, dims):
        self.dims = dims
        self.row = lax.axis_index("rows")
        self.core = lax.axis_index("mp")
        d0, d1, d2 = dims
        self.at = [self.row // (d1 * d2), (self.row // d2) % d1, self.row % d2]

    def peer(self, steps):
        d0, d1, d2 = self.dims
        at = [(a + o) % d if o else a for a, o, d in zip(self.at, steps, self.dims)]
        return at, ((at[0] * d1 + at[1]) * d2 + at[2], self.core)

    def sibling(self):
        return (self.row, 1 - self.core)


def steps_of(dims, stage):
    ranges = [range(dims[d]) if d in stage else range(1) for d in range(3)]
    return [o for o in itertools.product(*ranges) if any(o)]


def rest_of(dims, order, stage):
    gone = [d for axes in order[: stage + 1] for d in axes]
    return tuple(dims[d] for d in range(3) if d not in gone)


def remote(src, dst, send, recv, device):
    return pltpu.make_async_remote_copy(
        src, dst, send, recv, device_id=device, device_id_type=MESH
    )


class Gather:
    def __init__(self, place, buf, chunks, send, recv):
        self.p, self.buf, self.chunks = place, buf, chunks
        self.send, self.recv, self.live = send, recv, {}

    def start(self, k, stage):
        begin, size, order = self.chunks[k]
        done = [d for axes in order[:stage] for d in axes]
        idx = tuple(slice(None) if d in done else self.p.at[d] for d in range(3))
        v = self.buf.at[(self.p.core,) + idx + (pl.ds(begin, size),)]
        if stage == len(order):
            devices = [self.p.sibling()]
        else:
            devices = [self.p.peer(o)[1] for o in steps_of(self.p.dims, order[stage])]
        self.live[k, stage] = [
            remote(v, v, self.send.at[k, stage, i], self.recv.at[k, stage, i], device)
            for i, device in enumerate(devices)
        ]
        for c in self.live[k, stage]:
            c.start()

    def arrive(self, k, stage):
        for c in self.live[k, stage]:
            c.wait_recv()

    def run(self):
        for stage in range(max(len(order) for _, _, order in self.chunks) + 1):
            for k, (_, _, order) in enumerate(self.chunks):
                if stage <= len(order):
                    self.arrive(k, stage)
                    if stage < len(order):
                        self.start(k, stage + 1)
            yield

    def finish(self):
        for copies in self.live.values():
            for c in copies:
                c.wait_send()


class Reduce:
    def __init__(self, place, buf, landing, chunks, send, recv, cores):
        self.p, self.buf, self.landing, self.chunks = place, buf, landing, chunks
        self.send, self.recv, self.first, self.live = send, recv, -1 if cores else 0, {}

    def index(self, k, stage, at):
        begin, size, order = self.chunks[k]
        gone = [d for axes in order[: stage + 1] for d in axes]
        return tuple(at[d] if d in gone else slice(None) for d in range(3)) + (pl.ds(begin, size),)

    def landed(self, k, stage, i):
        begin, size, order = self.chunks[k]
        rest = len(rest_of(self.p.dims, order, stage))
        return self.landing[k][stage + 1].at[(i,) + (slice(None),) * (rest + 2)]

    def start(self, k, stage):
        order = self.chunks[k][2]
        copies = []
        if stage < 0:
            src = self.buf.at[(1 - self.p.core,) + self.index(k, -1, None)]
            copies.append((src, self.p.sibling()))
        else:
            for o in steps_of(self.p.dims, order[stage]):
                at, device = self.p.peer(o)
                copies.append((self.buf.at[(self.p.core,) + self.index(k, stage, at)], device))
        self.live[k, stage] = [
            remote(
                src,
                self.landed(k, stage, i),
                self.send.at[k, stage + 1, i],
                self.recv.at[k, stage + 1, i],
                device,
            )
            for i, (src, device) in enumerate(copies)
        ]
        for c in self.live[k, stage]:
            c.start()

    def arrive(self, k, stage):
        mine = (self.p.core,) + self.index(k, stage, self.p.at)
        for c in self.live[k, stage]:
            c.wait_recv()
        total = self.buf[mine]
        for i in range(len(self.live[k, stage])):
            total = total + self.landed(k, stage, i)[...]
        self.buf[mine] = total

    def begin(self):
        for k in range(len(self.chunks)):
            self.start(k, self.first)

    def run(self):
        for stage in range(self.first, max(len(order) for _, _, order in self.chunks)):
            for k, (_, _, order) in enumerate(self.chunks):
                if stage < len(order):
                    self.arrive(k, stage)
                    if stage + 1 < len(order):
                        self.start(k, stage + 1)
            yield

    def finish(self):
        for copies in self.live.values():
            for c in copies:
                c.wait_send()


def landings(dims, chunks, width, cores):
    out = []
    for _, size, order in chunks:
        shapes = [(1,) + tuple(dims) + (size, width) if cores else (1, 8, 128)]
        for stage, axes in enumerate(order):
            shapes.append((len(steps_of(dims, axes)),) + rest_of(dims, order, stage) + (size, width))
        out.append([pltpu.VMEM(tuple(max(n, 1) for n in shape), F32) for shape in shapes])
    return out


def semaphores(dims, chunks):
    stages = max(len(order) for _, _, order in chunks) + 1
    most = max(len(steps_of(dims, axes)) for _, _, order in chunks for axes in order)
    return [pltpu.SemaphoreType.DMA((len(chunks), stages, max(most, 1)))] * 2


def iota(shape, dim):
    return lax.broadcasted_iota(jnp.int32, shape, dim)


def dot(a, b, precision=None):
    return jnp.dot(a, b, precision=precision, preferred_element_type=F32)


def dot_nt(a, b, precision=None):
    return lax.dot_general(
        a, b, (((1,), (1,)), ((), ())), precision=precision, preferred_element_type=F32
    )


def dot_tn(a, b, precision=None):
    return lax.dot_general(
        a, b, (((0,), (0,)), ((), ())), precision=precision, preferred_element_type=F32
    )


def turn(x, by):
    by = by % x.shape[1]
    return pltpu.roll(x, by, 1) if by else x


def widen(x, width):
    return jnp.concatenate([x, jnp.zeros((x.shape[0], width - x.shape[1]), F32)], axis=1)


def one_row(x, count):
    return jnp.concatenate([x[k : k + 1] for k in range(count)], axis=1)


def rows_of(ref, count):
    whole = count // LANES
    rows = ref[pl.ds(0, whole * LANES)].reshape(whole, LANES)
    if count % LANES:
        rest = ref[pl.ds(whole * LANES, count % LANES)].reshape(1, count % LANES)
        rows = jnp.concatenate([rows, widen(rest, LANES)], axis=0)
    return rows


def store_rows(ref, rows, count):
    whole = count // LANES
    ref[pl.ds(0, whole * LANES)] = rows[:whole].reshape(whole * LANES)
    if count % LANES:
        ref[pl.ds(whole * LANES, count % LANES)] = rows[whole : whole + 1, : count % LANES].reshape(count % LANES)


def update(
    per_device,
    grad_ref,
    grad_table_ref,
    shape_code_ref,
    loss_in_ref,
    params_ref,
    momentum_ref,
    average_ref,
    table_ref,
    code_first_ref,
    code_second_ref,
    loss_ref,
    new_momentum_ref,
    new_params_ref,
    new_average_ref,
    new_table_ref,
    new_first_ref,
    new_second_ref,
):
    count = -(-per_device // LANES)
    grad = grad_ref[0:count, :]
    params = rows_of(params_ref, per_device)
    new_momentum = MOMENTUM_DECAY * rows_of(momentum_ref, per_device) + grad
    new_params = params - LEARN_RATE * (grad + MOMENTUM_DECAY * new_momentum)
    new_average = AVERAGE_DECAY * rows_of(average_ref, per_device) + (1.0 - AVERAGE_DECAY) * new_params
    store_rows(new_momentum_ref, new_momentum, per_device)
    store_rows(new_params_ref, new_params, per_device)
    store_rows(new_average_ref, new_average, per_device)
    grad_table = grad_table_ref[...]
    code_rows = table_ref.shape[0]
    here = shape_code_ref[...] - lax.axis_index("rows") * code_rows == iota((code_rows, shape_code_ref.shape[1]), 0)
    is_used = jnp.sum(here.astype(F32), axis=1, keepdims=True) > 0.5
    table, code_first, code_second = table_ref[...], code_first_ref[...], code_second_ref[...]
    first_new = BETA_FIRST * code_first + (1.0 - BETA_FIRST) * grad_table
    second_new = BETA_SECOND * code_second + (1.0 - BETA_SECOND) * grad_table * grad_table
    step_vals = (
        CODE_RATE
        * (first_new / (1.0 - BETA_FIRST**STEP))
        / (jnp.sqrt(second_new / (1.0 - BETA_SECOND**STEP)) + ADAM_EPS)
    )
    new_table_ref[...] = jnp.where(is_used, table - step_vals, table)
    new_first_ref[...] = jnp.where(is_used, first_new, code_first)
    new_second_ref[...] = jnp.where(is_used, second_new, code_second)
    loss_ref[...] = loss_in_ref[...]


def bounds(devices, per_device):
    for d in range(devices):
        row, phase = divmod(per_device * d, LANES)
        yield d, row, phase, -(-(phase + per_device) // LANES)


def assemble(dims, per_device, buf, flat):
    rows = dims[0] * dims[1] * dims[2]
    for d, row, phase, count in bounds(2 * rows, per_device):
        chip = d // 2
        src = buf.at[d % 2, chip // (dims[1] * dims[2]), (chip // dims[2]) % dims[1], chip % dims[2]]
        if phase:
            flat[row : row + 1, :] = flat[row : row + 1, :] + src[0:1, :]
            flat[row + 1 : row + count, :] = src[1:count, :]
        else:
            flat[row : row + count, :] = src[0:count, :]


def scatter(dims, per_device, rows_kept, flat, buf):
    rows = dims[0] * dims[1] * dims[2]
    for d, row, phase, count in bounds(2 * rows, per_device):
        chip = d // 2
        dst = buf.at[d % 2, chip // (dims[1] * dims[2]), (chip // dims[2]) % dims[1], chip % dims[2]]
        dst[...] = flat[row : row + rows_kept, :]


def first_blocks():
    for back in range(4):
        begin = -(-256 * back // 3)
        end = min(-(-256 * (back + 1) // 3), CODE + 3)
        for at in range(begin, end, 8):
            yield back, at, min(8, end - at)


def unpack_first(flat, wide, v1):
    wide[0:8, :] = jnp.zeros((8, 256), F32)
    for half in range(2):
        lanes = slice(half * LANES, (half + 1) * LANES)
        wide[8:272, lanes] = flat[pl.ds(half, 264, stride=2), :]
    v1[256:264, :] = jnp.zeros((8, 256), F32)
    for back, at, n in first_blocks():
        base = 3 * at - 256 * back
        lane = iota((n, 256), 1)
        move = base + 3 * iota((n, 256), 0)
        here = wide[8 + at - back : 8 + at - back + n, :]
        before = wide[7 + at - back : 7 + at - back + n, :]
        mixed = jnp.where(lane < 256 - move, here, before)
        mixed = turn(mixed, base)
        if n > 1:
            mixed = pltpu.roll(mixed, 0, 1, stride=3, stride_axis=0)
        v1[at : at + n, :] = jnp.where(lane < INNER, mixed, 0.0)


def pack_first(v1, wide, flat):
    wide[...] = jnp.zeros(wide.shape, F32)
    for back, at, n in first_blocks():
        base = 3 * at - 256 * back
        lane = iota((n, 256), 1)
        sub = iota((n, 256), 0)
        moved = turn(v1[at : at + n, :], -base)
        for bit in range(3):
            moved = jnp.where((sub >> bit) & 1 == 1, turn(moved, -3 * (1 << bit)), moved)
        here = lane < 256 - (base + 3 * sub)
        a = slice(8 + at - back, 8 + at - back + n)
        b = slice(7 + at - back, 7 + at - back + n)
        wide[a, :] = wide[a, :] + jnp.where(here, moved, 0.0)
        wide[b, :] = wide[b, :] + jnp.where(here, 0.0, moved)
    for half in range(2):
        lanes = slice(half * LANES, (half + 1) * LANES)
        flat[pl.ds(half, 256, stride=2), :] = wide[8:264, lanes]


def unpack_second(flat, v2):
    for q in range(H2 // LANES):
        lanes = slice(q * LANES, (q + 1) * LANES)
        for at in range(0, H2 + 8, 104):
            rows = flat[pl.ds(SECOND_ROW + q + 4 * at, 104, stride=4), :]
            if q == 0:
                after = flat[pl.ds(SECOND_ROW + 4 + 4 * at, 104, stride=4), :]
                rows = jnp.where(iota((104, LANES), 1) < SHIFT, after, rows)
            v2[at : at + 104, lanes] = rows


def pack_second(v2, flat):
    low = iota((1, LANES), 1) < SHIFT
    for q in range(1, H2 // LANES):
        lanes = slice(q * LANES, (q + 1) * LANES)
        flat[pl.ds(SECOND_ROW + q, H2, stride=4), :] = v2[0:H2, lanes]
        flat[SECOND_ROW + q + 4 * H2 : SECOND_ROW + q + 4 * H2 + 1, :] = v2[H2 : H2 + 1, lanes]
    flat[pl.ds(SECOND_ROW + 4, H2, stride=4), :] = jnp.where(low, v2[0:H2, 0:LANES], v2[1 : H2 + 1, 0:LANES])
    flat[SECOND_ROW : SECOND_ROW + 1, :] = jnp.where(
        low, flat[SECOND_ROW : SECOND_ROW + 1, :], v2[0:1, 0:LANES]
    )
    flat[TAIL_ROW : TAIL_ROW + 1, :] = jnp.where(low, v2[H2 : H2 + 1, 0:LANES], 0.0)


def unpack_tail(flat):
    count = 13
    tail = one_row(flat[TAIL_ROW : TAIL_ROW + count, :], count)
    at = SHIFT
    parts = []
    for width in TAIL_PIECES:
        lanes = {INNER: 256, H2: H2, 1: LANES}[width]
        piece = turn(tail, -at)[:, 0:lanes]
        if width == H2:
            piece = turn(piece, SHIFT)
        else:
            piece = jnp.where(iota((1, lanes), 1) < width, piece, 0.0)
        parts.append(piece)
        at += width
    return parts


def pack_tail(parts, flat):
    count = 13
    at = SHIFT
    total = jnp.zeros((1, count * LANES), F32)
    for width, piece in zip(TAIL_PIECES, parts):
        if width == H2:
            piece = turn(piece, -SHIFT)
        else:
            piece = jnp.where(iota(piece.shape, 1) < width, piece, 0.0)
        total = total + turn(widen(piece, count * LANES), at)
        at += width
    flat[TAIL_ROW : TAIL_ROW + 1, :] = flat[TAIL_ROW : TAIL_ROW + 1, :] + total[:, 0:LANES]
    for k in range(1, count):
        flat[TAIL_ROW + k : TAIL_ROW + k + 1, :] = total[:, k * LANES : (k + 1) * LANES]


def split2(x):
    high = x.astype(BF16)
    return high, (x - high.astype(F32)).astype(BF16)


def split3(x):
    a = x.astype(BF16).astype(F32)
    b = (x - a).astype(BF16).astype(F32)
    return a, b, x - a - b


def kernel(
    cfg,
    params_hbm,
    table_hbm,
    coords_hbm,
    targets_hbm,
    seg_hbm,
    shape_code_hbm,
    loss_ref,
    grad_ref,
    grad_table_ref,
    params_ref,
    table_ref,
    coords_ref,
    targets_ref,
    seg_ref,
    shape_code_ref,
    fetched,
    buf,
    landing,
    flat,
    wide,
    v1,
    v2,
    g1,
    g2,
    w2t,
    w2b,
    w0,
    bias,
    head,
    points,
    hc,
    h1,
    slope1,
    h2,
    act,
    second,
    preds,
    d2b,
    df,
    d1b,
    dw2,
    dw1,
    dhead,
    sums,
    codes_buf,
    codes_landing,
    grads_buf,
    psend,
    precv,
    csend,
    crecv,
    dsend,
    drecv,
    rsend,
    rrecv,
):
    dims, per_device, tile = cfg["dims"], cfg["per_device"], cfg["tile"]
    used, kept = piece_rows(per_device, 2 * cfg["rows"])
    rows = cfg["rows"]
    shapes = cfg["shapes"]
    place = Place(dims)
    device = place.row * 2 + place.core
    tiles = seg_ref.shape[0] * LANES // tile
    per_tile = tile // LANES
    head_len = seg_ref.shape[0] * LANES // 16

    barrier = pltpu.get_barrier_semaphore()
    greeted = {place_steps for table in cfg["tables"] for _, _, order in table for axes in order for place_steps in steps_of(dims, axes)}
    pl.semaphore_signal(barrier, inc=1, device_id=place.sibling(), device_id_type=MESH)
    for o in sorted(greeted):
        pl.semaphore_signal(barrier, inc=1, device_id=place.peer(o)[1], device_id_type=MESH)

    inputs = dict(
        params=(params_hbm, params_ref),
        seg=(seg_hbm, seg_ref),
        codes=(shape_code_hbm, shape_code_ref),
        table=(table_hbm, table_ref),
        targets=(targets_hbm, targets_ref),
        coords=(coords_hbm, coords_ref),
    )
    copies = {}
    for i, (name, (src, dst)) in enumerate(inputs.items()):
        copies[name] = pltpu.make_async_copy(src, dst, fetched.at[i])
        copies[name].start()

    copies["params"].wait()
    copies["seg"].wait()
    seg_heads = seg_ref[0 : head_len // LANES, :].astype(F32)
    shared = jnp.max(jnp.max(seg_heads, axis=1, keepdims=True), axis=0, keepdims=True)

    def count(where):
        return jnp.sum(jnp.sum(where.astype(F32), axis=1, keepdims=True), axis=0, keepdims=True)

    mine = (device * 2).astype(F32)
    seg_all = seg_ref[...].astype(F32)
    counts = [count(seg_all == shared), count(seg_all == mine), count(seg_all == mine + 1.0)]

    phase = (device * per_device) % LANES
    own = buf.at[place.core, place.at[0], place.at[1], place.at[2]]
    raw = rows_of(params_ref, per_device)
    while raw.shape[0] < kept - 1:
        raw = jnp.concatenate([raw, jnp.zeros((1, LANES), F32)], axis=0)
    raw = jnp.concatenate([raw, jnp.broadcast_to(counts[0], (1, LANES))], axis=0)
    if any(p for _, _, p, _ in bounds(2 * rows, per_device)):
        moved = pltpu.roll(raw, phase, 1)
        before = jnp.concatenate([jnp.zeros((1, LANES), F32), moved[: kept - 1]], axis=0)
        raw = jnp.where((iota((kept, LANES), 1) < phase) & (iota((kept, LANES), 0) < kept - 1), before, moved)
    own[...] = raw

    pl.semaphore_wait(barrier, len(greeted) + 1)
    gather_table, reduce_table, codes_table, spread_table = cfg["tables"]
    gather = Gather(place, buf, gather_table, psend, precv)
    for k in range(len(gather_table)):
        gather.start(k, 0)

    for name in ("codes", "table", "targets", "coords"):
        copies[name].wait()

    base = (place.row * table_ref.shape[0]).astype(F32)
    codes_of = jnp.broadcast_to(shape_code_ref[...].astype(F32) + 1.0, (8, shapes))
    slots = rows * 8
    kind = iota((slots, shapes), 0) & 7
    owner = (iota((slots, shapes), 0) >> 3) * 2 + place.core
    shape_id = iota((slots, shapes), 1)
    asked = jnp.where(
        kind == 3,
        (shape_id.astype(F32) == shared).astype(F32),
        jnp.where((kind == 4) | (kind == 5), (shape_id == owner * 2 + kind - 4).astype(F32), 0.0),
    )
    wanted = dot_nt(asked, codes_of, EXACT)[:, 0:1] - 1.0 - base
    pick = (wanted == iota((slots, table_ref.shape[0]), 1).astype(F32)).astype(F32)
    answer = dot(pick, table_ref[...], EXACT)
    codes_buf[place.core] = answer.reshape(dims + (8, CODE))

    codes = Reduce(place, codes_buf, codes_landing, codes_table, csend, crecv, False)
    codes.begin()
    for q in range(per_tile):
        lanes = slice(q * LANES, (q + 1) * LANES)
        points[0, :, lanes] = seg_ref[pl.ds(q, tiles, stride=per_tile), :].astype(F32)
        points[1, :, lanes] = jnp.tanh(targets_ref[pl.ds(q, tiles, stride=per_tile), :] * (1.0 / CLAMP_DELTA))
    seg = points[0]

    for _ in itertools.zip_longest(gather.run(), codes.run()):
        pass
    z8 = codes_buf[place.core, place.at[0], place.at[1], place.at[2]]

    assemble(dims, per_device, buf, flat)
    unpack_first(flat, wide, v1)
    unpack_second(flat, v2)
    gain1, gain2, bias1, bias2, head_bias = unpack_tail(flat)
    norm1 = jnp.sum(v1[...] * v1[...], axis=0, keepdims=True) + NORM_EPS
    norm2 = jnp.sum(v2[0:H2, :] * v2[0:H2, :], axis=0, keepdims=True) + NORM_EPS
    inv1, inv2 = lax.rsqrt(norm1), lax.rsqrt(norm2)
    scale1, scale2 = gain1 * inv1, gain2 * inv2
    head_row = v2[H2 : H2 + 1, :]
    hbias = head_bias[:, 0:1]

    total = jnp.sum(buf[:, :, :, :, kept - 1 : kept, :], axis=(0, 1, 2, 3))[:, 0:1]
    counts_all = [total]
    for k in (1, 2):
        counts_all.append(jnp.where(shared == mine + (k - 1.0), total, jnp.maximum(counts[k], 1.0)))
    inv_counts = [1.0 / (n * float(shapes)) for n in counts_all]
    position = iota((tiles, tile), 0) * tile + iota((tiles, tile), 1)
    is_two = (seg == mine + 1.0) & (position >= head_len)
    per_point = jnp.where(
        position < head_len, inv_counts[0], jnp.where(is_two, inv_counts[2], inv_counts[1])
    )
    points[2] = jnp.where(seg >= 0.0, per_point, 0.0)
    points[3] = jnp.where(is_two, 1.0, 0.0)

    lane1 = iota((8, 256), 1)
    sub1 = iota((8, 256), 0)
    code1 = dot(z8, v1[0:CODE, :], THREE) * scale1 + bias1
    xyz1 = v1[CODE : CODE + 8, :] * scale1
    rows1 = 0.5 * jnp.where(sub1 < 3, xyz1, jnp.where(sub1 < 6, code1, 0.0))
    rows1 = jnp.where(lane1 < INNER, rows1, (lane1 == INNER + sub1).astype(F32))
    rows1 = jnp.where(sub1 < 6, rows1, 0.0)
    wa, wb, wc = split3(rows1)
    stack = jnp.concatenate([wa, wa, wb, wb, wa, wc] + [jnp.zeros((8, 256), F32)] * 10, axis=0)
    w0[...] = stack.T.astype(BF16)

    z_wide = turn(widen(z8, H2), INNER)
    code2 = 0.5 * (dot(z_wide, v2[0:H2, :], THREE) * scale2 + bias2)
    sub2 = iota((8, H2), 0)
    columns = jnp.where(sub2 == 6, jnp.broadcast_to(0.5 * head_row, (8, H2)), code2)
    columns = jnp.concatenate([columns, jnp.zeros((LANES - 8, H2), F32)], axis=0).T
    for k in range(3):
        bias[k] = jnp.broadcast_to(columns[:, 3 + k : 4 + k], (H2, LANES))
    head[...] = jnp.broadcast_to(columns[:, 6:7], (H2, LANES))
    last = jnp.where(sub2 < 5, v2[248:256, :], v2[H2 - 8 : H2, :])
    normal = jnp.concatenate([v2[0:248, :], last], axis=0) * scale2
    w2b[...] = normal.astype(BF16)
    high, low = split2(0.5 * normal.T)
    w2t[:, 0:256] = high
    w2t[:, 256:512] = high
    w2t[:, 512:768] = low

    dw2[...] = jnp.zeros(dw2.shape, F32)
    dw1[...] = jnp.zeros(dw1.shape, F32)
    dhead[...] = jnp.zeros(dhead.shape, F32)
    sums[...] = jnp.zeros(sums.shape, F32)
    block = 32

    def lanes_of(q):
        return slice(q * LANES, (q + 1) * LANES)

    def first_product(t):
        at = slice(t * tile, (t + 1) * tile)
        two = points[3, t : t + 1, :]
        is_head = (t * tile + iota((1, tile), 1) < head_len).astype(F32)
        x8 = jnp.concatenate(
            [coords_ref[:, at], is_head, 1.0 - two - is_head, two, jnp.zeros((2, tile), F32)], axis=0
        )
        xa, xb, xc = split3(x8)
        x48 = jnp.concatenate([xa, xb, xa, xb, xc, xa], axis=0).astype(BF16)
        hc[t % DEEP, 768:784, :] = jnp.concatenate([xa, xb], axis=0).astype(BF16)
        h1[t % 2] = dot(w0[:, 0:48], x48)

    def first_layer(t):
        for q in range(per_tile):
            lanes = lanes_of(q)
            for u in range(0, 256, block):
                us = slice(u, u + block)
                h = h1[t % 2, us, lanes]
                th = jnp.tanh(h)
                m = h * th
                f = h + m
                slope1[t % DEEP, us, lanes] = (0.5 + 0.5 * th) * (1.0 + (h - m))
                if u + block > INNER:
                    f = jnp.where(iota((block, LANES), 0) + u >= INNER, h, f)
                fh, fl = split2(f)
                hc[t % DEEP, us, lanes] = fh
                hc[t % DEEP, 256 + u : 256 + u + block, lanes] = fl
                hc[t % DEEP, 512 + u : 512 + u + block, lanes] = fh

    def second_product(t):
        h2[t % 2] = dot(w2t[...], hc[t % DEEP, 0:768, :])

    def second_layer(t):
        parts = []
        for q in range(per_tile):
            lanes = lanes_of(q)
            in_head = t * per_tile + q < head_len // LANES
            is_second = jnp.broadcast_to(points[3, t : t + 1, lanes], (block, LANES)) > 0.5
            part = jnp.zeros((8, LANES), F32)
            for u in range(0, H2, block):
                us = slice(u, u + block)
                b = bias[0, us, :] if in_head else jnp.where(is_second, bias[2, us, :], bias[1, us, :])
                h = h2[t % 2, us, lanes] + b
                th = jnp.tanh(h)
                m = h * th
                s = h + m
                hw = head[us, :]
                second[t % 2, us, lanes] = s
                act[t % 2, us, lanes] = hw * ((1.0 + th) * (1.0 + (h - m)))
                w = hw * s
                for v in range(0, block, 8):
                    part = part + w[v : v + 8]
            parts.append(jnp.sum(part, axis=0, keepdims=True))
        preds[t % 2, 0:1, :] = 2.0 * jnp.concatenate(parts, axis=1) + hbias

    def back_second(t):
        pred = jnp.tanh(preds[t % 2, 0:1, :])
        squash = jnp.tanh(pred * (1.0 / CLAMP_DELTA))
        resid = CLAMP_DELTA * squash - CLAMP_DELTA * points[1, t : t + 1, :]
        square = resid * resid + SMOOTH * SMOOTH
        inv_radius = lax.rsqrt(square)
        share = points[2, t : t + 1, :]
        dpred = share * (resid * inv_radius) * (1.0 - squash * squash) * (1.0 - pred * pred)
        sums[0:1, :] = sums[0:1, :] + share * (square * inv_radius - SMOOTH)
        sums[1:2, :] = sums[1:2, :] + dpred
        for u in range(0, H2, block):
            us = slice(u, u + block)
            total_u = dhead[us, :]
            for q in range(per_tile):
                lanes = lanes_of(q)
                dp = jnp.broadcast_to(dpred[:, lanes], (block, LANES))
                d2b[t % 2, us, lanes] = (act[t % 2, us, lanes] * dp).astype(BF16)
                total_u = total_u + second[t % 2, us, lanes] * dp
            dhead[us, :] = total_u

    def back_products(t):
        df[t % 2] = dot(w2b[...], d2b[t % 2])
        dw2[...] = dw2[...] + dot_nt(hc[t % DEEP, 512:784, :], d2b[t % 2])

    def back_first(t):
        for u in range(0, 256, block):
            us = slice(u, u + block)
            d1b[t % 2, us, :] = (df[t % 2, us, :] * slope1[t % DEEP, us, :]).astype(BF16)

    def back_first_product(t):
        dw1[...] = dw1[...] + dot_nt(hc[t % DEEP, 768:784, :], d1b[t % 2])

    steps = ((first_product, 2), (second_product, 0), (first_layer, 1), (second_layer, -1), (back_products, -3), (back_second, -2), (back_first_product, -5), (back_first, -4))
    for i in range(-max(lag for _, lag in steps), tiles - min(lag for _, lag in steps)):
        for stage, lag in steps:
            if 0 <= i + lag < tiles:
                stage(i + lag)

    outer1 = jnp.where(lane1 < INNER, dw1[0:8, :] + dw1[8:16, :], 0.0)
    outer2 = dw2[256:264, :] + dw2[264:272, :]
    slot_rows = (sub1 >= 3) & (sub1 < 6)
    d1 = jnp.where(slot_rows, outer1, 0.0)
    d2 = jnp.where((sub2 >= 3) & (sub2 < 6), outer2, 0.0)
    dz = dot_nt(d1 * scale1, v1[0:CODE, :], THREE)
    dz = dz + turn(dot_nt(d2 * scale2, v2[0:H2, :], THREE), -INNER)[:, 0:CODE]
    own_rows = (sub1 == 4) | (sub1 == 5)
    dz = dz + jnp.where(own_rows, (2.0 * PRIOR_WEIGHT / shapes) * z8, 0.0)
    prior = jnp.where(own_rows, z8 * z8, 0.0)
    prior = (PRIOR_WEIGHT / shapes) * jnp.sum(jnp.sum(prior, axis=1, keepdims=True), axis=0, keepdims=True)
    loss_here = jnp.sum(sums[0:1, :], axis=1, keepdims=True) + prior
    message = jnp.where(slot_rows, dz, 0.0)
    message = jnp.where(sub1 == 0, jnp.broadcast_to(loss_here, (8, CODE)), message)
    grads_buf[place.core, place.at[0], place.at[1], place.at[2]] = message
    spread = Gather(place, grads_buf, spread_table, dsend, drecv)
    spread.start(0, 0)

    g1[0:CODE, :] = dot_tn(z8, d1, THREE)
    g1[CODE : CODE + 8, :] = jnp.where(sub1 < 3, outer1, 0.0)
    along1 = jnp.sum(v1[...] * g1[...], axis=0, keepdims=True)
    g1[...] = g1[...] * scale1 - v1[...] * (scale1 * inv1 * inv1 * along1)
    g2[0:H2, :] = dot_tn(z_wide, d2, THREE)
    g2[0:256, :] = g2[0:256, :] + jnp.where(iota((256, H2), 0) < INNER, dw2[0:256, :], 0.0)
    g2[H2 - 8 : H2, :] = g2[H2 - 8 : H2, :] + jnp.where(sub2 >= 5, dw2[248:256, :], 0.0)
    along2 = jnp.sum(v2[0:H2, :] * g2[0:H2, :], axis=0, keepdims=True)
    g2[0:H2, :] = g2[0:H2, :] * scale2 - v2[0:H2, :] * (scale2 * inv2 * inv2 * along2)
    high, low = split2(dhead[...])
    ones = jnp.ones((16, LANES), BF16)
    g2[H2 : H2 + 8, :] = (dot_nt(ones, high) + dot_nt(ones, low))[0:8, :]
    dbias = jnp.broadcast_to(jnp.sum(sums[1:2, :], axis=1, keepdims=True), (1, LANES))
    pack_first(g1, wide, flat)
    pack_second(g2, flat)
    pack_tail(
        [
            along1 * inv1,
            along2 * inv2,
            jnp.sum(d1, axis=0, keepdims=True),
            jnp.sum(d2, axis=0, keepdims=True),
            dbias,
        ],
        flat,
    )
    gather.finish()
    codes.finish()
    scatter(dims, per_device, kept, flat, buf)
    reduce = Reduce(place, buf, landing, reduce_table, rsend, rrecv, True)
    reduce.begin()
    arriving, summing = spread.run(), reduce.run()
    for _ in range(2):
        next(summing)
        next(arriving)
    next(arriving)

    everyone = grads_buf[...].reshape(2 * slots, CODE)
    kind = iota((shapes, 2 * slots), 1) & 7
    owner = ((iota((shapes, 2 * slots), 1) >> 3) & (rows - 1)) * 2 + (iota((shapes, 2 * slots), 1) >> int(math.log2(slots)))
    shape_id = iota((shapes, 2 * slots), 0)
    asked = jnp.where(
        kind == 3,
        (shape_id.astype(F32) == shared).astype(F32),
        jnp.where((kind == 4) | (kind == 5), (shape_id == owner * 2 + kind - 4).astype(F32), 0.0),
    )
    code_rows = table_ref.shape[0]
    target_row = dot(codes_of, asked, EXACT)[0:1, :] - 1.0 - base
    pick = (target_row == iota((code_rows, 2 * slots), 0).astype(F32)).astype(F32)
    grad_table = dot(pick, everyone, THREE)
    grad_table_ref[...] = grad_table
    loss_ref[...] = jnp.sum(grads_buf[:, :, :, :, 0:8, 0:LANES], axis=(0, 1, 2, 3))[0:1, 0:1]
    next(summing)
    piece = own[...]
    if any(p for _, _, p, _ in bounds(2 * rows, per_device)):
        moved = pltpu.roll(piece, (LANES - phase) % LANES, 1)
        after = jnp.concatenate([moved[1:], moved[:1]], axis=0)
        piece = jnp.where(iota((kept, LANES), 1) < LANES - phase, moved, after)
    grad_ref[...] = piece

    spread.finish()
    reduce.finish()


def chunked(rows, parts):
    blocks = -(-rows // 8)
    whole = sum(share for share, _ in parts)
    out, at, upto = [], 0, 0
    for share, order in parts:
        upto += share
        end = min((blocks * upto + whole // 2) // whole * 8, rows)
        if end > at:
            out.append((at, end - at, order))
        at = end
    return out


def shards(rows, params, momentum, average, table, code_first, code_second, coords, targets, segment_ids, shape_code):
    per_device = params.shape[0]
    devices = 2 * rows
    used, kept = piece_rows(per_device, devices)
    dims = chip_dims(rows)
    points_here = segment_ids.shape[0]
    tile = 256
    tiles = points_here // tile
    shapes = shape_code.shape[0]
    code_rows = table.shape[0]
    out_first, out_last = ((0,), (1, 2)), ((1, 2), (0,))
    tables = [
        chunked(kept, [(4, out_first), (4, out_first), (3, out_last)]),
        chunked(kept, [(4, out_last), (4, out_last), (3, out_first)]),
        [(0, 8, out_last)],
        [(0, 8, out_first)],
    ]
    cfg = dict(
        dims=dims,
        rows=rows,
        per_device=per_device,
        tile=tile,
        shapes=shapes,
        tables=tables,
    )
    flat_rows = per_device * devices // LANES + kept + 8
    vm = pltpu.VMEM
    scratch = [
        vm((per_device,), F32),
        vm((code_rows, CODE), F32),
        vm((3, points_here), F32),
        vm((points_here // LANES, LANES), F32),
        vm((points_here // LANES, LANES), jnp.int32),
        vm((1, shapes), jnp.int32),
        pltpu.SemaphoreType.DMA((6,)),
        vm((2,) + dims + (kept, LANES), F32),
        landings(dims, tables[1], LANES, True),
        vm((flat_rows, LANES), F32),
        vm((272, 256), F32),
        vm((264, 256), F32),
        vm((520, H2), F32),
        vm((264, 256), F32),
        vm((520, H2), F32),
        vm((H2, 768), BF16),
        vm((256, H2), BF16),
        vm((256, LANES), BF16),
        vm((3, H2, LANES), F32),
        vm((H2, LANES), F32),
        vm((4, tiles, tile), F32),
        vm((DEEP, 784, tile), BF16),
        vm((2, 256, tile), F32),
        vm((DEEP, 256, tile), F32),
        vm((2, H2, tile), F32),
        vm((2, H2, tile), F32),
        vm((2, H2, tile), F32),
        vm((2, 8, tile), F32),
        vm((2, H2, tile), BF16),
        vm((2, 256, tile), F32),
        vm((2, 256, tile), BF16),
        vm((272, H2), F32),
        vm((16, 256), F32),
        vm((H2, LANES), F32),
        vm((8, tile), F32),
        vm((2,) + dims + (8, CODE), F32),
        landings(dims, tables[2], CODE, False),
        vm((2,) + dims + (8, CODE), F32),
        *semaphores(dims, tables[0]),
        *semaphores(dims, tables[2]),
        *semaphores(dims, tables[3]),
        *semaphores(dims, tables[1]),
    ]
    spec = pl.BlockSpec(memory_space=pltpu.VMEM)
    loss, grad, grad_table = pl.pallas_call(
        functools.partial(kernel, cfg),
        out_shape=(
            jax.ShapeDtypeStruct((1, 1), F32),
            jax.ShapeDtypeStruct((kept, LANES), F32),
            jax.ShapeDtypeStruct((code_rows, CODE), F32),
        ),
        in_specs=[pl.BlockSpec(memory_space=pl.ANY)] * 6,
        out_specs=(spec,) * 3,
        scratch_shapes=scratch,
        compiler_params=pltpu.CompilerParams(
            collective_id=0, has_side_effects=True, vmem_limit_bytes=56 << 20
        ),
    )(
        params,
        table,
        coords,
        targets.reshape(-1, LANES),
        segment_ids.reshape(-1, LANES),
        shape_code.reshape(1, shapes),
    )
    flat_out = jax.ShapeDtypeStruct((per_device,), F32)
    table_out = jax.ShapeDtypeStruct((code_rows, CODE), F32)
    outs = pl.pallas_call(
        functools.partial(update, per_device),
        out_shape=(jax.ShapeDtypeStruct((1, 1), F32),) + (flat_out,) * 3 + (table_out,) * 3,
        in_specs=[spec] * 10,
        out_specs=(spec,) * 7,
    )(grad, grad_table, shape_code.reshape(1, shapes), loss, params, momentum, average, table, code_first, code_second)
    return (outs[0].reshape(()),) + tuple(outs[1:])


def solution(mesh):
    flat = P(("rows", "mp"))
    placed = (flat, flat, flat, P("rows", None), P("rows", None), P("rows", None), P(None, ("rows", "mp")), flat, flat, P())
    return jax.shard_map(
        functools.partial(shards, mesh.shape["rows"]),
        mesh=mesh,
        in_specs=placed,
        out_specs=(P(), flat, flat, flat, P("rows", None), P("rows", None), P("rows", None)),
        check_vma=False,
    )
```

```python
import functools
import itertools
import math

import jax
import jax.numpy as jnp
from jax import lax
from jax.experimental import pallas as pl
from jax.experimental.pallas import tpu as pltpu
from jax.sharding import PartitionSpec as P

MESH = pl.DeviceIdType.MESH
F32, BF16 = jnp.float32, jnp.bfloat16
EXACT = lax.Precision.HIGHEST
THREE = lax.Precision.HIGH
DEEP = 8
CODE = 256
H2 = 512
INNER = H2 - CODE - 3
STEP = 10
CLAMP_DELTA = 0.1
SMOOTH = 0.01
PRIOR_WEIGHT = 0.001
LEARN_RATE = 200.0
MOMENTUM_DECAY = 0.9
AVERAGE_DECAY = 0.9
CODE_RATE = 0.5
BETA_FIRST = 0.9
BETA_SECOND = 0.999
ADAM_EPS = 1e-08
NORM_EPS = 1e-12
LANES = 128

SECOND_AT = (CODE + 3) * INNER
SECOND_ROW, SHIFT = divmod(SECOND_AT, LANES)
TAIL_AT = SECOND_AT + H2 * H2 + H2
TAIL_ROW = TAIL_AT // LANES
TAIL_PIECES = (INNER, H2, INNER, H2, 1)


def chip_dims(rows):
    return {16: (4, 2, 2), 128: (4, 4, 8)}.get(rows, (rows, 1, 1))


def piece_rows(per_device, devices):
    most = max((per_device * d) % LANES for d in range(devices))
    rows = -(-(most + per_device) // LANES)
    return rows, rows + 1


class Place:
    def __init__(self, dims):
        self.dims = dims
        self.row = lax.axis_index("rows")
        self.core = lax.axis_index("mp")
        d0, d1, d2 = dims
        self.at = [self.row // (d1 * d2), (self.row // d2) % d1, self.row % d2]

    def peer(self, steps):
        d0, d1, d2 = self.dims
        at = [(a + o) % d if o else a for a, o, d in zip(self.at, steps, self.dims)]
        return at, ((at[0] * d1 + at[1]) * d2 + at[2], self.core)

    def sibling(self):
        return (self.row, 1 - self.core)


def steps_of(dims, stage):
    ranges = [range(dims[d]) if d in stage else range(1) for d in range(3)]
    return [o for o in itertools.product(*ranges) if any(o)]


def rest_of(dims, order, stage):
    gone = [d for axes in order[: stage + 1] for d in axes]
    return tuple(dims[d] for d in range(3) if d not in gone)


def remote(src, dst, send, recv, device):
    return pltpu.make_async_remote_copy(
        src, dst, send, recv, device_id=device, device_id_type=MESH
    )


class Gather:
    def __init__(self, place, buf, chunks, send, recv):
        self.p, self.buf, self.chunks = place, buf, chunks
        self.send, self.recv, self.live = send, recv, {}

    def start(self, k, stage):
        begin, size, order = self.chunks[k]
        done = [d for axes in order[:stage] for d in axes]
        idx = tuple(slice(None) if d in done else self.p.at[d] for d in range(3))
        v = self.buf.at[(self.p.core,) + idx + (pl.ds(begin, size),)]
        if stage == len(order):
            devices = [self.p.sibling()]
        else:
            devices = [self.p.peer(o)[1] for o in steps_of(self.p.dims, order[stage])]
        self.live[k, stage] = [
            remote(v, v, self.send.at[k, stage, i], self.recv.at[k, stage, i], device)
            for i, device in enumerate(devices)
        ]
        for c in self.live[k, stage]:
            c.start()

    def arrive(self, k, stage):
        for c in self.live[k, stage]:
            c.wait_recv()

    def run(self):
        for stage in range(max(len(order) for _, _, order in self.chunks) + 1):
            for k, (_, _, order) in enumerate(self.chunks):
                if stage <= len(order):
                    self.arrive(k, stage)
                    if stage < len(order):
                        self.start(k, stage + 1)
            yield

    def finish(self):
        for copies in self.live.values():
            for c in copies:
                c.wait_send()


class Reduce:
    def __init__(self, place, buf, landing, chunks, send, recv, cores):
        self.p, self.buf, self.landing, self.chunks = place, buf, landing, chunks
        self.send, self.recv, self.first, self.live = send, recv, -1 if cores else 0, {}

    def index(self, k, stage, at):
        begin, size, order = self.chunks[k]
        gone = [d for axes in order[: stage + 1] for d in axes]
        return tuple(at[d] if d in gone else slice(None) for d in range(3)) + (pl.ds(begin, size),)

    def landed(self, k, stage, i):
        begin, size, order = self.chunks[k]
        rest = len(rest_of(self.p.dims, order, stage))
        return self.landing[k][stage + 1].at[(i,) + (slice(None),) * (rest + 2)]

    def start(self, k, stage):
        order = self.chunks[k][2]
        copies = []
        if stage < 0:
            src = self.buf.at[(1 - self.p.core,) + self.index(k, -1, None)]
            copies.append((src, self.p.sibling()))
        else:
            for o in steps_of(self.p.dims, order[stage]):
                at, device = self.p.peer(o)
                copies.append((self.buf.at[(self.p.core,) + self.index(k, stage, at)], device))
        self.live[k, stage] = [
            remote(
                src,
                self.landed(k, stage, i),
                self.send.at[k, stage + 1, i],
                self.recv.at[k, stage + 1, i],
                device,
            )
            for i, (src, device) in enumerate(copies)
        ]
        for c in self.live[k, stage]:
            c.start()

    def arrive(self, k, stage):
        mine = (self.p.core,) + self.index(k, stage, self.p.at)
        for c in self.live[k, stage]:
            c.wait_recv()
        total = self.buf[mine]
        for i in range(len(self.live[k, stage])):
            total = total + self.landed(k, stage, i)[...]
        self.buf[mine] = total

    def begin(self):
        for k in range(len(self.chunks)):
            self.start(k, self.first)

    def run(self):
        for stage in range(self.first, max(len(order) for _, _, order in self.chunks)):
            for k, (_, _, order) in enumerate(self.chunks):
                if stage < len(order):
                    self.arrive(k, stage)
                    if stage + 1 < len(order):
                        self.start(k, stage + 1)
            yield

    def finish(self):
        for copies in self.live.values():
            for c in copies:
                c.wait_send()


def landings(dims, chunks, width, cores):
    out = []
    for _, size, order in chunks:
        shapes = [(1,) + tuple(dims) + (size, width) if cores else (1, 8, 128)]
        for stage, axes in enumerate(order):
            shapes.append((len(steps_of(dims, axes)),) + rest_of(dims, order, stage) + (size, width))
        out.append([pltpu.VMEM(tuple(max(n, 1) for n in shape), F32) for shape in shapes])
    return out


def semaphores(dims, chunks):
    stages = max(len(order) for _, _, order in chunks) + 1
    most = max(len(steps_of(dims, axes)) for _, _, order in chunks for axes in order)
    return [pltpu.SemaphoreType.DMA((len(chunks), stages, max(most, 1)))] * 2


def iota(shape, dim):
    return lax.broadcasted_iota(jnp.int32, shape, dim)


def dot(a, b, precision=None):
    return jnp.dot(a, b, precision=precision, preferred_element_type=F32)


def dot_nt(a, b, precision=None):
    return lax.dot_general(
        a, b, (((1,), (1,)), ((), ())), precision=precision, preferred_element_type=F32
    )


def dot_tn(a, b, precision=None):
    return lax.dot_general(
        a, b, (((0,), (0,)), ((), ())), precision=precision, preferred_element_type=F32
    )


def turn(x, by):
    by = by % x.shape[1]
    return pltpu.roll(x, by, 1) if by else x


def widen(x, width):
    return jnp.concatenate([x, jnp.zeros((x.shape[0], width - x.shape[1]), F32)], axis=1)


def one_row(x, count):
    return jnp.concatenate([x[k : k + 1] for k in range(count)], axis=1)


def rows_of(ref, count):
    whole = count // LANES
    rows = ref[pl.ds(0, whole * LANES)].reshape(whole, LANES)
    if count % LANES:
        rest = ref[pl.ds(whole * LANES, count % LANES)].reshape(1, count % LANES)
        rows = jnp.concatenate([rows, widen(rest, LANES)], axis=0)
    return rows


def store_rows(ref, rows, count):
    whole = count // LANES
    ref[pl.ds(0, whole * LANES)] = rows[:whole].reshape(whole * LANES)
    if count % LANES:
        ref[pl.ds(whole * LANES, count % LANES)] = rows[whole : whole + 1, : count % LANES].reshape(count % LANES)


def update(
    per_device,
    grad_ref,
    grad_table_ref,
    shape_code_ref,
    loss_in_ref,
    params_ref,
    momentum_ref,
    average_ref,
    table_ref,
    code_first_ref,
    code_second_ref,
    loss_ref,
    new_momentum_ref,
    new_params_ref,
    new_average_ref,
    new_table_ref,
    new_first_ref,
    new_second_ref,
):
    count = -(-per_device // LANES)
    grad = grad_ref[0:count, :]
    params = rows_of(params_ref, per_device)
    new_momentum = MOMENTUM_DECAY * rows_of(momentum_ref, per_device) + grad
    new_params = params - LEARN_RATE * (grad + MOMENTUM_DECAY * new_momentum)
    new_average = AVERAGE_DECAY * rows_of(average_ref, per_device) + (1.0 - AVERAGE_DECAY) * new_params
    store_rows(new_momentum_ref, new_momentum, per_device)
    store_rows(new_params_ref, new_params, per_device)
    store_rows(new_average_ref, new_average, per_device)
    grad_table = grad_table_ref[...]
    code_rows = table_ref.shape[0]
    here = shape_code_ref[...] - lax.axis_index("rows") * code_rows == iota((code_rows, shape_code_ref.shape[1]), 0)
    is_used = jnp.sum(here.astype(F32), axis=1, keepdims=True) > 0.5
    table, code_first, code_second = table_ref[...], code_first_ref[...], code_second_ref[...]
    first_new = BETA_FIRST * code_first + (1.0 - BETA_FIRST) * grad_table
    second_new = BETA_SECOND * code_second + (1.0 - BETA_SECOND) * grad_table * grad_table
    step_vals = (
        CODE_RATE
        * (first_new / (1.0 - BETA_FIRST**STEP))
        / (jnp.sqrt(second_new / (1.0 - BETA_SECOND**STEP)) + ADAM_EPS)
    )
    new_table_ref[...] = jnp.where(is_used, table - step_vals, table)
    new_first_ref[...] = jnp.where(is_used, first_new, code_first)
    new_second_ref[...] = jnp.where(is_used, second_new, code_second)
    loss_ref[...] = loss_in_ref[...]


def bounds(devices, per_device):
    for d in range(devices):
        row, phase = divmod(per_device * d, LANES)
        yield d, row, phase, -(-(phase + per_device) // LANES)


def assemble(dims, per_device, buf, flat):
    rows = dims[0] * dims[1] * dims[2]
    for d, row, phase, count in bounds(2 * rows, per_device):
        chip = d // 2
        src = buf.at[d % 2, chip // (dims[1] * dims[2]), (chip // dims[2]) % dims[1], chip % dims[2]]
        if phase:
            flat[row : row + 1, :] = flat[row : row + 1, :] + src[0:1, :]
            flat[row + 1 : row + count, :] = src[1:count, :]
        else:
            flat[row : row + count, :] = src[0:count, :]


def scatter(dims, per_device, rows_kept, flat, buf):
    rows = dims[0] * dims[1] * dims[2]
    for d, row, phase, count in bounds(2 * rows, per_device):
        chip = d // 2
        dst = buf.at[d % 2, chip // (dims[1] * dims[2]), (chip // dims[2]) % dims[1], chip % dims[2]]
        dst[...] = flat[row : row + rows_kept, :]


def first_blocks():
    for back in range(4):
        begin = -(-256 * back // 3)
        end = min(-(-256 * (back + 1) // 3), CODE + 3)
        for at in range(begin, end, 8):
            yield back, at, min(8, end - at)


def unpack_first(flat, wide, v1):
    wide[0:8, :] = jnp.zeros((8, 256), F32)
    for half in range(2):
        lanes = slice(half * LANES, (half + 1) * LANES)
        wide[8:272, lanes] = flat[pl.ds(half, 264, stride=2), :]
    v1[256:264, :] = jnp.zeros((8, 256), F32)
    for back, at, n in first_blocks():
        base = 3 * at - 256 * back
        lane = iota((n, 256), 1)
        move = base + 3 * iota((n, 256), 0)
        here = wide[8 + at - back : 8 + at - back + n, :]
        before = wide[7 + at - back : 7 + at - back + n, :]
        mixed = jnp.where(lane < 256 - move, here, before)
        mixed = turn(mixed, base)
        if n > 1:
            mixed = pltpu.roll(mixed, 0, 1, stride=3, stride_axis=0)
        v1[at : at + n, :] = jnp.where(lane < INNER, mixed, 0.0)


def pack_first(v1, wide, flat):
    wide[...] = jnp.zeros(wide.shape, F32)
    for back, at, n in first_blocks():
        base = 3 * at - 256 * back
        lane = iota((n, 256), 1)
        sub = iota((n, 256), 0)
        moved = turn(v1[at : at + n, :], -base)
        for bit in range(3):
            moved = jnp.where((sub >> bit) & 1 == 1, turn(moved, -3 * (1 << bit)), moved)
        here = lane < 256 - (base + 3 * sub)
        a = slice(8 + at - back, 8 + at - back + n)
        b = slice(7 + at - back, 7 + at - back + n)
        wide[a, :] = wide[a, :] + jnp.where(here, moved, 0.0)
        wide[b, :] = wide[b, :] + jnp.where(here, 0.0, moved)
    for half in range(2):
        lanes = slice(half * LANES, (half + 1) * LANES)
        flat[pl.ds(half, 256, stride=2), :] = wide[8:264, lanes]


def unpack_second(flat, v2):
    for q in range(H2 // LANES):
        lanes = slice(q * LANES, (q + 1) * LANES)
        for at in range(0, H2 + 8, 104):
            rows = flat[pl.ds(SECOND_ROW + q + 4 * at, 104, stride=4), :]
            if q == 0:
                after = flat[pl.ds(SECOND_ROW + 4 + 4 * at, 104, stride=4), :]
                rows = jnp.where(iota((104, LANES), 1) < SHIFT, after, rows)
            v2[at : at + 104, lanes] = rows


def pack_second(v2, flat):
    low = iota((1, LANES), 1) < SHIFT
    for q in range(1, H2 // LANES):
        lanes = slice(q * LANES, (q + 1) * LANES)
        flat[pl.ds(SECOND_ROW + q, H2, stride=4), :] = v2[0:H2, lanes]
        flat[SECOND_ROW + q + 4 * H2 : SECOND_ROW + q + 4 * H2 + 1, :] = v2[H2 : H2 + 1, lanes]
    flat[pl.ds(SECOND_ROW + 4, H2, stride=4), :] = jnp.where(low, v2[0:H2, 0:LANES], v2[1 : H2 + 1, 0:LANES])
    flat[SECOND_ROW : SECOND_ROW + 1, :] = jnp.where(
        low, flat[SECOND_ROW : SECOND_ROW + 1, :], v2[0:1, 0:LANES]
    )
    flat[TAIL_ROW : TAIL_ROW + 1, :] = jnp.where(low, v2[H2 : H2 + 1, 0:LANES], 0.0)


def unpack_tail(flat):
    count = 13
    tail = one_row(flat[TAIL_ROW : TAIL_ROW + count, :], count)
    at = SHIFT
    parts = []
    for width in TAIL_PIECES:
        lanes = {INNER: 256, H2: H2, 1: LANES}[width]
        piece = turn(tail, -at)[:, 0:lanes]
        if width == H2:
            piece = turn(piece, SHIFT)
        else:
            piece = jnp.where(iota((1, lanes), 1) < width, piece, 0.0)
        parts.append(piece)
        at += width
    return parts


def pack_tail(parts, flat):
    count = 13
    at = SHIFT
    total = jnp.zeros((1, count * LANES), F32)
    for width, piece in zip(TAIL_PIECES, parts):
        if width == H2:
            piece = turn(piece, -SHIFT)
        else:
            piece = jnp.where(iota(piece.shape, 1) < width, piece, 0.0)
        total = total + turn(widen(piece, count * LANES), at)
        at += width
    flat[TAIL_ROW : TAIL_ROW + 1, :] = flat[TAIL_ROW : TAIL_ROW + 1, :] + total[:, 0:LANES]
    for k in range(1, count):
        flat[TAIL_ROW + k : TAIL_ROW + k + 1, :] = total[:, k * LANES : (k + 1) * LANES]


def split2(x):
    high = x.astype(BF16)
    return high, (x - high.astype(F32)).astype(BF16)


def split3(x):
    a = x.astype(BF16).astype(F32)
    b = (x - a).astype(BF16).astype(F32)
    return a, b, x - a - b


def kernel(
    cfg,
    params_hbm,
    table_hbm,
    coords_hbm,
    targets_hbm,
    seg_hbm,
    shape_code_hbm,
    loss_ref,
    grad_ref,
    grad_table_ref,
    params_ref,
    table_ref,
    coords_ref,
    targets_ref,
    seg_ref,
    shape_code_ref,
    fetched,
    buf,
    landing,
    flat,
    wide,
    v1,
    v2,
    g1,
    g2,
    w2t,
    w2b,
    w0,
    bias,
    head,
    points,
    hc,
    h1,
    slope1,
    h2,
    act,
    second,
    preds,
    d2b,
    df,
    d1b,
    dw2,
    dw1,
    dhead,
    sums,
    codes_buf,
    codes_landing,
    grads_buf,
    psend,
    precv,
    csend,
    crecv,
    dsend,
    drecv,
    rsend,
    rrecv,
):
    dims, per_device, tile = cfg["dims"], cfg["per_device"], cfg["tile"]
    used, kept = piece_rows(per_device, 2 * cfg["rows"])
    rows = cfg["rows"]
    shapes = cfg["shapes"]
    place = Place(dims)
    device = place.row * 2 + place.core
    tiles = seg_ref.shape[0] * LANES // tile
    per_tile = tile // LANES
    head_len = seg_ref.shape[0] * LANES // 16

    barrier = pltpu.get_barrier_semaphore()
    greeted = {place_steps for table in cfg["tables"] for _, _, order in table for axes in order for place_steps in steps_of(dims, axes)}
    pl.semaphore_signal(barrier, inc=1, device_id=place.sibling(), device_id_type=MESH)
    for o in sorted(greeted):
        pl.semaphore_signal(barrier, inc=1, device_id=place.peer(o)[1], device_id_type=MESH)

    inputs = dict(
        params=(params_hbm, params_ref),
        seg=(seg_hbm, seg_ref),
        codes=(shape_code_hbm, shape_code_ref),
        table=(table_hbm, table_ref),
        targets=(targets_hbm, targets_ref),
        coords=(coords_hbm, coords_ref),
    )
    copies = {}
    for i, (name, (src, dst)) in enumerate(inputs.items()):
        copies[name] = pltpu.make_async_copy(src, dst, fetched.at[i])
        copies[name].start()

    copies["params"].wait()
    copies["seg"].wait()
    seg_heads = seg_ref[0 : head_len // LANES, :].astype(F32)
    shared = jnp.max(jnp.max(seg_heads, axis=1, keepdims=True), axis=0, keepdims=True)

    def count(where):
        return jnp.sum(jnp.sum(where.astype(F32), axis=1, keepdims=True), axis=0, keepdims=True)

    mine = (device * 2).astype(F32)
    seg_all = seg_ref[...].astype(F32)
    counts = [count(seg_all == shared), count(seg_all == mine), count(seg_all == mine + 1.0)]

    phase = (device * per_device) % LANES
    own = buf.at[place.core, place.at[0], place.at[1], place.at[2]]
    raw = rows_of(params_ref, per_device)
    while raw.shape[0] < kept - 1:
        raw = jnp.concatenate([raw, jnp.zeros((1, LANES), F32)], axis=0)
    raw = jnp.concatenate([raw, jnp.broadcast_to(counts[0], (1, LANES))], axis=0)
    if any(p for _, _, p, _ in bounds(2 * rows, per_device)):
        moved = pltpu.roll(raw, phase, 1)
        before = jnp.concatenate([jnp.zeros((1, LANES), F32), moved[: kept - 1]], axis=0)
        raw = jnp.where((iota((kept, LANES), 1) < phase) & (iota((kept, LANES), 0) < kept - 1), before, moved)
    own[...] = raw

    pl.semaphore_wait(barrier, len(greeted) + 1)
    gather_table, reduce_table, codes_table, spread_table = cfg["tables"]
    gather = Gather(place, buf, gather_table, psend, precv)
    for k in range(len(gather_table)):
        gather.start(k, 0)

    for name in ("codes", "table", "targets", "coords"):
        copies[name].wait()

    base = (place.row * table_ref.shape[0]).astype(F32)
    codes_of = jnp.broadcast_to(shape_code_ref[...].astype(F32) + 1.0, (8, shapes))
    slots = rows * 8
    kind = iota((slots, shapes), 0) & 7
    owner = (iota((slots, shapes), 0) >> 3) * 2 + place.core
    shape_id = iota((slots, shapes), 1)
    asked = jnp.where(
        kind == 3,
        (shape_id.astype(F32) == shared).astype(F32),
        jnp.where((kind == 4) | (kind == 5), (shape_id == owner * 2 + kind - 4).astype(F32), 0.0),
    )
    wanted = dot_nt(asked, codes_of, EXACT)[:, 0:1] - 1.0 - base
    pick = (wanted == iota((slots, table_ref.shape[0]), 1).astype(F32)).astype(F32)
    answer = dot(pick, table_ref[...], EXACT)
    codes_buf[place.core] = answer.reshape(dims + (8, CODE))

    codes = Reduce(place, codes_buf, codes_landing, codes_table, csend, crecv, False)
    codes.begin()
    for q in range(per_tile):
        lanes = slice(q * LANES, (q + 1) * LANES)
        points[0, :, lanes] = seg_ref[pl.ds(q, tiles, stride=per_tile), :].astype(F32)
        points[1, :, lanes] = jnp.tanh(targets_ref[pl.ds(q, tiles, stride=per_tile), :] * (1.0 / CLAMP_DELTA))
    seg = points[0]

    for _ in itertools.zip_longest(gather.run(), codes.run()):
        pass
    z8 = codes_buf[place.core, place.at[0], place.at[1], place.at[2]]

    assemble(dims, per_device, buf, flat)
    unpack_first(flat, wide, v1)
    unpack_second(flat, v2)
    gain1, gain2, bias1, bias2, head_bias = unpack_tail(flat)
    norm1 = jnp.sum(v1[...] * v1[...], axis=0, keepdims=True) + NORM_EPS
    norm2 = jnp.sum(v2[0:H2, :] * v2[0:H2, :], axis=0, keepdims=True) + NORM_EPS
    inv1, inv2 = lax.rsqrt(norm1), lax.rsqrt(norm2)
    scale1, scale2 = gain1 * inv1, gain2 * inv2
    head_row = v2[H2 : H2 + 1, :]
    hbias = head_bias[:, 0:1]

    total = jnp.sum(buf[:, :, :, :, kept - 1 : kept, :], axis=(0, 1, 2, 3))[:, 0:1]
    counts_all = [total]
    for k in (1, 2):
        counts_all.append(jnp.where(shared == mine + (k - 1.0), total, jnp.maximum(counts[k], 1.0)))
    inv_counts = [1.0 / (n * float(shapes)) for n in counts_all]
    position = iota((tiles, tile), 0) * tile + iota((tiles, tile), 1)
    is_two = (seg == mine + 1.0) & (position >= head_len)
    per_point = jnp.where(
        position < head_len, inv_counts[0], jnp.where(is_two, inv_counts[2], inv_counts[1])
    )
    points[2] = jnp.where(seg >= 0.0, per_point, 0.0)
    points[3] = jnp.where(is_two, 1.0, 0.0)

    lane1 = iota((8, 256), 1)
    sub1 = iota((8, 256), 0)
    code1 = dot(z8, v1[0:CODE, :], THREE) * scale1 + bias1
    xyz1 = v1[CODE : CODE + 8, :] * scale1
    rows1 = 0.5 * jnp.where(sub1 < 3, xyz1, jnp.where(sub1 < 6, code1, 0.0))
    rows1 = jnp.where(lane1 < INNER, rows1, (lane1 == INNER + sub1).astype(F32))
    rows1 = jnp.where(sub1 < 6, rows1, 0.0)
    wa, wb, wc = split3(rows1)
    stack = jnp.concatenate([wa, wa, wb, wb, wa, wc] + [jnp.zeros((8, 256), F32)] * 10, axis=0)
    w0[...] = stack.T.astype(BF16)

    z_wide = turn(widen(z8, H2), INNER)
    code2 = 0.5 * (dot(z_wide, v2[0:H2, :], THREE) * scale2 + bias2)
    sub2 = iota((8, H2), 0)
    columns = jnp.where(sub2 == 6, jnp.broadcast_to(0.5 * head_row, (8, H2)), code2)
    columns = jnp.concatenate([columns, jnp.zeros((LANES - 8, H2), F32)], axis=0).T
    for k in range(3):
        bias[k] = jnp.broadcast_to(columns[:, 3 + k : 4 + k], (H2, LANES))
    head[...] = jnp.broadcast_to(columns[:, 6:7], (H2, LANES))
    last = jnp.where(sub2 < 5, v2[248:256, :], v2[H2 - 8 : H2, :])
    normal = jnp.concatenate([v2[0:248, :], last], axis=0) * scale2
    w2b[...] = (normal * (0.25 * head_row)).astype(BF16)
    high, low = split2(0.5 * normal.T)
    w2t[:, 0:256] = high
    w2t[:, 256:512] = high
    w2t[:, 512:768] = low

    dw2[...] = jnp.zeros(dw2.shape, F32)
    dw1[...] = jnp.zeros(dw1.shape, F32)
    dhead[...] = jnp.zeros(dhead.shape, F32)
    sums[...] = jnp.zeros(sums.shape, F32)
    block = 32

    def lanes_of(q):
        return slice(q * LANES, (q + 1) * LANES)

    def first_product(t):
        at = slice(t * tile, (t + 1) * tile)
        two = points[3, t : t + 1, :]
        is_head = (t * tile + iota((1, tile), 1) < head_len).astype(F32)
        x8 = jnp.concatenate(
            [coords_ref[:, at], is_head, 1.0 - two - is_head, two, jnp.zeros((2, tile), F32)], axis=0
        )
        xa, xb, xc = split3(x8)
        x48 = jnp.concatenate([xa, xb, xa, xb, xc, xa], axis=0).astype(BF16)
        hc[t % DEEP, 768:784, :] = jnp.concatenate([xa, xb], axis=0).astype(BF16)
        h1[t % 2] = dot(w0[:, 0:48], x48)
        yield

    def first_layer(t):
        for q in range(per_tile):
            lanes = lanes_of(q)
            for u in range(0, 256, block):
                us = slice(u, u + block)
                h = h1[t % 2, us, lanes]
                th = jnp.tanh(h)
                m = h * th
                f = h + m
                slope1[t % DEEP, us, lanes] = (1.0 + th) * (1.0 + (h - m))
                if u + block > INNER:
                    f = jnp.where(iota((block, LANES), 0) + u >= INNER, h, f)
                fh, fl = split2(f)
                hc[t % DEEP, us, lanes] = fh
                hc[t % DEEP, 256 + u : 256 + u + block, lanes] = fl
                hc[t % DEEP, 512 + u : 512 + u + block, lanes] = fh
                yield

    def second_product(t):
        for m in range(0, H2, 256):
            h2[t % 2, m : m + 256, :] = dot(w2t[m : m + 256, :], hc[t % DEEP, 0:768, :])
            yield

    def second_layer(t):
        parts = []
        for q in range(per_tile):
            lanes = lanes_of(q)
            in_head = t * per_tile + q < head_len // LANES
            is_second = jnp.broadcast_to(points[3, t : t + 1, lanes], (block, LANES)) > 0.5
            part = jnp.zeros((8, LANES), F32)
            for u in range(0, H2, block):
                us = slice(u, u + block)
                b = bias[0, us, :] if in_head else jnp.where(is_second, bias[2, us, :], bias[1, us, :])
                h = h2[t % 2, us, lanes] + b
                th = jnp.tanh(h)
                m = h * th
                s = h + m
                hw = head[us, :]
                second[t % 2, us, lanes] = s
                act[t % 2, us, lanes] = (1.0 + th) * (1.0 + (h - m))
                w = hw * s
                for v in range(0, block, 8):
                    part = part + w[v : v + 8]
                yield
            parts.append(jnp.sum(part, axis=0, keepdims=True))
        preds[t % 2, 0:1, :] = 2.0 * jnp.concatenate(parts, axis=1) + hbias

    def back_second(t):
        pred = jnp.tanh(preds[t % 2, 0:1, :])
        squash = jnp.tanh(pred * (1.0 / CLAMP_DELTA))
        resid = CLAMP_DELTA * squash - CLAMP_DELTA * points[1, t : t + 1, :]
        square = resid * resid + SMOOTH * SMOOTH
        inv_radius = lax.rsqrt(square)
        share = points[2, t : t + 1, :]
        dpred = share * (resid * inv_radius) * (1.0 - squash * squash) * (1.0 - pred * pred)
        sums[0:1, :] = sums[0:1, :] + share * (square * inv_radius - SMOOTH)
        sums[1:2, :] = sums[1:2, :] + dpred
        for u in range(0, H2, block):
            us = slice(u, u + block)
            total_u = dhead[us, :]
            for q in range(per_tile):
                lanes = lanes_of(q)
                dp = jnp.broadcast_to(dpred[:, lanes], (block, LANES))
                d2b[t % 2, us, lanes] = (act[t % 2, us, lanes] * dp).astype(BF16)
                total_u = total_u + second[t % 2, us, lanes] * dp
            dhead[us, :] = total_u
            yield

    def back_products(t):
        df[t % 2] = dot(w2b[...], d2b[t % 2])
        yield
        for n in range(0, H2, 256):
            dw2[:, n : n + 256] = dw2[:, n : n + 256] + dot_nt(hc[t % DEEP, 512:784, :], d2b[t % 2, n : n + 256, :])
            yield

    def back_first(t):
        for u in range(0, 256, block):
            us = slice(u, u + block)
            d1b[t % 2, us, :] = (df[t % 2, us, :] * slope1[t % DEEP, us, :]).astype(BF16)
            yield

    def back_first_product(t):
        dw1[...] = dw1[...] + dot_nt(hc[t % DEEP, 768:784, :], d1b[t % 2])
        yield

    products = ((second_product, 0), (back_products, -3), (first_product, 2), (back_first_product, -5))
    elementwise = ((back_second, -2), (second_layer, -1), (first_layer, 1), (back_first, -4))
    for i in range(-2, tiles + 5):

        def pieces(stages):
            return itertools.chain(*(stage(i + lag) for stage, lag in stages if 0 <= i + lag < tiles))

        rest = pieces(elementwise)
        for _ in pieces(products):
            for _ in itertools.islice(rest, 8):
                pass
        for _ in rest:
            pass

    outer1 = jnp.where(lane1 < INNER, dw1[0:8, :] + dw1[8:16, :], 0.0)
    dw2[...] = dw2[...] * (0.5 * head_row)
    outer2 = dw2[256:264, :] + dw2[264:272, :]
    slot_rows = (sub1 >= 3) & (sub1 < 6)
    d1 = jnp.where(slot_rows, outer1, 0.0)
    d2 = jnp.where((sub2 >= 3) & (sub2 < 6), outer2, 0.0)
    dz = dot_nt(d1 * scale1, v1[0:CODE, :], THREE)
    dz = dz + turn(dot_nt(d2 * scale2, v2[0:H2, :], THREE), -INNER)[:, 0:CODE]
    own_rows = (sub1 == 4) | (sub1 == 5)
    dz = dz + jnp.where(own_rows, (2.0 * PRIOR_WEIGHT / shapes) * z8, 0.0)
    prior = jnp.where(own_rows, z8 * z8, 0.0)
    prior = (PRIOR_WEIGHT / shapes) * jnp.sum(jnp.sum(prior, axis=1, keepdims=True), axis=0, keepdims=True)
    loss_here = jnp.sum(sums[0:1, :], axis=1, keepdims=True) + prior
    message = jnp.where(slot_rows, dz, 0.0)
    message = jnp.where(sub1 == 0, jnp.broadcast_to(loss_here, (8, CODE)), message)
    grads_buf[place.core, place.at[0], place.at[1], place.at[2]] = message
    spread = Gather(place, grads_buf, spread_table, dsend, drecv)
    spread.start(0, 0)

    g1[0:CODE, :] = dot_tn(z8, d1, THREE)
    g1[CODE : CODE + 8, :] = jnp.where(sub1 < 3, outer1, 0.0)
    along1 = jnp.sum(v1[...] * g1[...], axis=0, keepdims=True)
    g1[...] = g1[...] * scale1 - v1[...] * (scale1 * inv1 * inv1 * along1)
    g2[0:H2, :] = dot_tn(z_wide, d2, THREE)
    g2[0:256, :] = g2[0:256, :] + jnp.where(iota((256, H2), 0) < INNER, dw2[0:256, :], 0.0)
    g2[H2 - 8 : H2, :] = g2[H2 - 8 : H2, :] + jnp.where(sub2 >= 5, dw2[248:256, :], 0.0)
    along2 = jnp.sum(v2[0:H2, :] * g2[0:H2, :], axis=0, keepdims=True)
    g2[0:H2, :] = g2[0:H2, :] * scale2 - v2[0:H2, :] * (scale2 * inv2 * inv2 * along2)
    high, low = split2(dhead[...])
    ones = jnp.ones((16, LANES), BF16)
    g2[H2 : H2 + 8, :] = (dot_nt(ones, high) + dot_nt(ones, low))[0:8, :]
    dbias = jnp.broadcast_to(jnp.sum(sums[1:2, :], axis=1, keepdims=True), (1, LANES))
    pack_first(g1, wide, flat)
    pack_second(g2, flat)
    pack_tail(
        [
            along1 * inv1,
            along2 * inv2,
            jnp.sum(d1, axis=0, keepdims=True),
            jnp.sum(d2, axis=0, keepdims=True),
            dbias,
        ],
        flat,
    )
    gather.finish()
    codes.finish()
    scatter(dims, per_device, kept, flat, buf)
    reduce = Reduce(place, buf, landing, reduce_table, rsend, rrecv, True)
    reduce.begin()
    arriving, summing = spread.run(), reduce.run()
    for _ in range(2):
        next(summing)
        next(arriving)
    next(arriving)

    everyone = grads_buf[...].reshape(2 * slots, CODE)
    kind = iota((shapes, 2 * slots), 1) & 7
    owner = ((iota((shapes, 2 * slots), 1) >> 3) & (rows - 1)) * 2 + (iota((shapes, 2 * slots), 1) >> int(math.log2(slots)))
    shape_id = iota((shapes, 2 * slots), 0)
    asked = jnp.where(
        kind == 3,
        (shape_id.astype(F32) == shared).astype(F32),
        jnp.where((kind == 4) | (kind == 5), (shape_id == owner * 2 + kind - 4).astype(F32), 0.0),
    )
    code_rows = table_ref.shape[0]
    target_row = dot(codes_of, asked, EXACT)[0:1, :] - 1.0 - base
    pick = (target_row == iota((code_rows, 2 * slots), 0).astype(F32)).astype(F32)
    grad_table = dot(pick, everyone, THREE)
    grad_table_ref[...] = grad_table
    loss_ref[...] = jnp.sum(grads_buf[:, :, :, :, 0:8, 0:LANES], axis=(0, 1, 2, 3))[0:1, 0:1]
    next(summing)
    piece = own[...]
    if any(p for _, _, p, _ in bounds(2 * rows, per_device)):
        moved = pltpu.roll(piece, (LANES - phase) % LANES, 1)
        after = jnp.concatenate([moved[1:], moved[:1]], axis=0)
        piece = jnp.where(iota((kept, LANES), 1) < LANES - phase, moved, after)
    grad_ref[...] = piece

    spread.finish()
    reduce.finish()


def chunked(rows, parts):
    blocks = -(-rows // 8)
    whole = sum(share for share, _ in parts)
    out, at, upto = [], 0, 0
    for share, order in parts:
        upto += share
        end = min((blocks * upto + whole // 2) // whole * 8, rows)
        if end > at:
            out.append((at, end - at, order))
        at = end
    return out


def shards(rows, params, momentum, average, table, code_first, code_second, coords, targets, segment_ids, shape_code):
    per_device = params.shape[0]
    devices = 2 * rows
    used, kept = piece_rows(per_device, devices)
    dims = chip_dims(rows)
    points_here = segment_ids.shape[0]
    tile = 256
    tiles = points_here // tile
    shapes = shape_code.shape[0]
    code_rows = table.shape[0]
    out_first, out_last = ((0,), (1, 2)), ((1, 2), (0,))
    tables = [
        chunked(kept, [(4, out_first), (4, out_first), (3, out_last)]),
        chunked(kept, [(4, out_last), (4, out_last), (3, out_first)]),
        [(0, 8, out_last)],
        [(0, 8, out_first)],
    ]
    cfg = dict(
        dims=dims,
        rows=rows,
        per_device=per_device,
        tile=tile,
        shapes=shapes,
        tables=tables,
    )
    flat_rows = per_device * devices // LANES + kept + 8
    vm = pltpu.VMEM
    scratch = [
        vm((per_device,), F32),
        vm((code_rows, CODE), F32),
        vm((3, points_here), F32),
        vm((points_here // LANES, LANES), F32),
        vm((points_here // LANES, LANES), jnp.int32),
        vm((1, shapes), jnp.int32),
        pltpu.SemaphoreType.DMA((6,)),
        vm((2,) + dims + (kept, LANES), F32),
        landings(dims, tables[1], LANES, True),
        vm((flat_rows, LANES), F32),
        vm((272, 256), F32),
        vm((264, 256), F32),
        vm((520, H2), F32),
        vm((264, 256), F32),
        vm((520, H2), F32),
        vm((H2, 768), BF16),
        vm((256, H2), BF16),
        vm((256, LANES), BF16),
        vm((3, H2, LANES), F32),
        vm((H2, LANES), F32),
        vm((4, tiles, tile), F32),
        vm((DEEP, 784, tile), BF16),
        vm((2, 256, tile), F32),
        vm((DEEP, 256, tile), F32),
        vm((2, H2, tile), F32),
        vm((2, H2, tile), F32),
        vm((2, H2, tile), F32),
        vm((2, 8, tile), F32),
        vm((2, H2, tile), BF16),
        vm((2, 256, tile), F32),
        vm((2, 256, tile), BF16),
        vm((272, H2), F32),
        vm((16, 256), F32),
        vm((H2, LANES), F32),
        vm((8, tile), F32),
        vm((2,) + dims + (8, CODE), F32),
        landings(dims, tables[2], CODE, False),
        vm((2,) + dims + (8, CODE), F32),
        *semaphores(dims, tables[0]),
        *semaphores(dims, tables[2]),
        *semaphores(dims, tables[3]),
        *semaphores(dims, tables[1]),
    ]
    spec = pl.BlockSpec(memory_space=pltpu.VMEM)
    loss, grad, grad_table = pl.pallas_call(
        functools.partial(kernel, cfg),
        out_shape=(
            jax.ShapeDtypeStruct((1, 1), F32),
            jax.ShapeDtypeStruct((kept, LANES), F32),
            jax.ShapeDtypeStruct((code_rows, CODE), F32),
        ),
        in_specs=[pl.BlockSpec(memory_space=pl.ANY)] * 6,
        out_specs=(spec,) * 3,
        scratch_shapes=scratch,
        compiler_params=pltpu.CompilerParams(
            collective_id=0, has_side_effects=True, vmem_limit_bytes=56 << 20
        ),
    )(
        params,
        table,
        coords,
        targets.reshape(-1, LANES),
        segment_ids.reshape(-1, LANES),
        shape_code.reshape(1, shapes),
    )
    flat_out = jax.ShapeDtypeStruct((per_device,), F32)
    table_out = jax.ShapeDtypeStruct((code_rows, CODE), F32)
    outs = pl.pallas_call(
        functools.partial(update, per_device),
        out_shape=(jax.ShapeDtypeStruct((1, 1), F32),) + (flat_out,) * 3 + (table_out,) * 3,
        in_specs=[spec] * 10,
        out_specs=(spec,) * 7,
    )(grad, grad_table, shape_code.reshape(1, shapes), loss, params, momentum, average, table, code_first, code_second)
    return (outs[0].reshape(()),) + tuple(outs[1:])


def solution(mesh):
    flat = P(("rows", "mp"))
    placed = (flat, flat, flat, P("rows", None), P("rows", None), P("rows", None), P(None, ("rows", "mp")), flat, flat, P())
    return jax.shard_map(
        functools.partial(shards, mesh.shape["rows"]),
        mesh=mesh,
        in_specs=placed,
        out_specs=(P(), flat, flat, flat, P("rows", None), P("rows", None), P("rows", None)),
        check_vma=False,
    )
```

```python
import functools
import itertools
import math

import jax
import jax.numpy as jnp
from jax import lax
from jax.experimental import pallas as pl
from jax.experimental.pallas import tpu as pltpu
from jax.sharding import PartitionSpec as P

MESH = pl.DeviceIdType.MESH
F32, BF16 = jnp.float32, jnp.bfloat16
EXACT = lax.Precision.HIGHEST
THREE = lax.Precision.HIGH
DEEP = 8
CODE = 256
H2 = 512
INNER = H2 - CODE - 3
STEP = 10
CLAMP_DELTA = 0.1
SMOOTH = 0.01
PRIOR_WEIGHT = 0.001
LEARN_RATE = 200.0
MOMENTUM_DECAY = 0.9
AVERAGE_DECAY = 0.9
CODE_RATE = 0.5
BETA_FIRST = 0.9
BETA_SECOND = 0.999
ADAM_EPS = 1e-08
NORM_EPS = 1e-12
LANES = 128

SECOND_AT = (CODE + 3) * INNER
SECOND_ROW, SHIFT = divmod(SECOND_AT, LANES)
TAIL_AT = SECOND_AT + H2 * H2 + H2
TAIL_ROW = TAIL_AT // LANES
TAIL_PIECES = (INNER, H2, INNER, H2, 1)


def chip_dims(rows):
    return {16: (4, 2, 2), 128: (4, 4, 8)}.get(rows, (rows, 1, 1))


def piece_rows(per_device, devices):
    most = max((per_device * d) % LANES for d in range(devices))
    rows = -(-(most + per_device) // LANES)
    return rows, rows + 1


class Place:
    def __init__(self, dims):
        self.dims = dims
        self.row = lax.axis_index("rows")
        self.core = lax.axis_index("mp")
        d0, d1, d2 = dims
        self.at = [self.row // (d1 * d2), (self.row // d2) % d1, self.row % d2]

    def peer(self, steps):
        d0, d1, d2 = self.dims
        at = [(a + o) % d if o else a for a, o, d in zip(self.at, steps, self.dims)]
        return at, ((at[0] * d1 + at[1]) * d2 + at[2], self.core)

    def sibling(self):
        return (self.row, 1 - self.core)


def steps_of(dims, stage):
    ranges = [range(dims[d]) if d in stage else range(1) for d in range(3)]
    return [o for o in itertools.product(*ranges) if any(o)]


def rest_of(dims, order, stage):
    gone = [d for axes in order[: stage + 1] for d in axes]
    return tuple(dims[d] for d in range(3) if d not in gone)


def remote(src, dst, send, recv, device):
    return pltpu.make_async_remote_copy(
        src, dst, send, recv, device_id=device, device_id_type=MESH
    )


class Gather:
    def __init__(self, place, buf, chunks, send, recv):
        self.p, self.buf, self.chunks = place, buf, chunks
        self.send, self.recv, self.live = send, recv, {}

    def start(self, k, stage):
        begin, size, order = self.chunks[k]
        done = [d for axes in order[:stage] for d in axes]
        idx = tuple(slice(None) if d in done else self.p.at[d] for d in range(3))
        v = self.buf.at[(self.p.core,) + idx + (pl.ds(begin, size),)]
        if stage == len(order):
            devices = [self.p.sibling()]
        else:
            devices = [self.p.peer(o)[1] for o in steps_of(self.p.dims, order[stage])]
        self.live[k, stage] = [
            remote(v, v, self.send.at[k, stage, i], self.recv.at[k, stage, i], device)
            for i, device in enumerate(devices)
        ]
        for c in self.live[k, stage]:
            c.start()

    def arrive(self, k, stage):
        for c in self.live[k, stage]:
            c.wait_recv()

    def run(self):
        for stage in range(max(len(order) for _, _, order in self.chunks) + 1):
            for k, (_, _, order) in enumerate(self.chunks):
                if stage <= len(order):
                    self.arrive(k, stage)
                    if stage < len(order):
                        self.start(k, stage + 1)
            yield

    def finish(self):
        for copies in self.live.values():
            for c in copies:
                c.wait_send()


class Reduce:
    def __init__(self, place, buf, landing, chunks, send, recv, cores):
        self.p, self.buf, self.landing, self.chunks = place, buf, landing, chunks
        self.send, self.recv, self.first, self.live = send, recv, -1 if cores else 0, {}

    def index(self, k, stage, at):
        begin, size, order = self.chunks[k]
        gone = [d for axes in order[: stage + 1] for d in axes]
        return tuple(at[d] if d in gone else slice(None) for d in range(3)) + (pl.ds(begin, size),)

    def landed(self, k, stage, i):
        begin, size, order = self.chunks[k]
        rest = len(rest_of(self.p.dims, order, stage))
        return self.landing[k][stage + 1].at[(i,) + (slice(None),) * (rest + 2)]

    def start(self, k, stage):
        order = self.chunks[k][2]
        copies = []
        if stage < 0:
            src = self.buf.at[(1 - self.p.core,) + self.index(k, -1, None)]
            copies.append((src, self.p.sibling()))
        else:
            for o in steps_of(self.p.dims, order[stage]):
                at, device = self.p.peer(o)
                copies.append((self.buf.at[(self.p.core,) + self.index(k, stage, at)], device))
        self.live[k, stage] = [
            remote(
                src,
                self.landed(k, stage, i),
                self.send.at[k, stage + 1, i],
                self.recv.at[k, stage + 1, i],
                device,
            )
            for i, (src, device) in enumerate(copies)
        ]
        for c in self.live[k, stage]:
            c.start()

    def arrive(self, k, stage):
        mine = (self.p.core,) + self.index(k, stage, self.p.at)
        for c in self.live[k, stage]:
            c.wait_recv()
        total = self.buf[mine]
        for i in range(len(self.live[k, stage])):
            total = total + self.landed(k, stage, i)[...]
        self.buf[mine] = total

    def begin(self):
        for k in range(len(self.chunks)):
            self.start(k, self.first)

    def run(self):
        for stage in range(self.first, max(len(order) for _, _, order in self.chunks)):
            for k, (_, _, order) in enumerate(self.chunks):
                if stage < len(order):
                    self.arrive(k, stage)
                    if stage + 1 < len(order):
                        self.start(k, stage + 1)
            yield

    def finish(self):
        for copies in self.live.values():
            for c in copies:
                c.wait_send()


def landings(dims, chunks, width, cores):
    out = []
    for _, size, order in chunks:
        shapes = [(1,) + tuple(dims) + (size, width) if cores else (1, 8, 128)]
        for stage, axes in enumerate(order):
            shapes.append((len(steps_of(dims, axes)),) + rest_of(dims, order, stage) + (size, width))
        out.append([pltpu.VMEM(tuple(max(n, 1) for n in shape), F32) for shape in shapes])
    return out


def semaphores(dims, chunks):
    stages = max(len(order) for _, _, order in chunks) + 1
    most = max(len(steps_of(dims, axes)) for _, _, order in chunks for axes in order)
    return [pltpu.SemaphoreType.DMA((len(chunks), stages, max(most, 1)))] * 2


def iota(shape, dim):
    return lax.broadcasted_iota(jnp.int32, shape, dim)


def dot(a, b, precision=None):
    return jnp.dot(a, b, precision=precision, preferred_element_type=F32)


def dot_nt(a, b, precision=None):
    return lax.dot_general(
        a, b, (((1,), (1,)), ((), ())), precision=precision, preferred_element_type=F32
    )


def dot_tn(a, b, precision=None):
    return lax.dot_general(
        a, b, (((0,), (0,)), ((), ())), precision=precision, preferred_element_type=F32
    )


def turn(x, by):
    by = by % x.shape[1]
    return pltpu.roll(x, by, 1) if by else x


def widen(x, width):
    return jnp.concatenate([x, jnp.zeros((x.shape[0], width - x.shape[1]), F32)], axis=1)


def one_row(x, count):
    return jnp.concatenate([x[k : k + 1] for k in range(count)], axis=1)


def rows_of(ref, count):
    whole = count // LANES
    rows = ref[pl.ds(0, whole * LANES)].reshape(whole, LANES)
    if count % LANES:
        rest = ref[pl.ds(whole * LANES, count % LANES)].reshape(1, count % LANES)
        rows = jnp.concatenate([rows, widen(rest, LANES)], axis=0)
    return rows


def store_rows(ref, rows, count):
    whole = count // LANES
    ref[pl.ds(0, whole * LANES)] = rows[:whole].reshape(whole * LANES)
    if count % LANES:
        ref[pl.ds(whole * LANES, count % LANES)] = rows[whole : whole + 1, : count % LANES].reshape(count % LANES)


def update(
    per_device,
    grad_ref,
    grad_table_ref,
    shape_code_ref,
    loss_in_ref,
    params_ref,
    momentum_ref,
    average_ref,
    table_ref,
    code_first_ref,
    code_second_ref,
    loss_ref,
    new_momentum_ref,
    new_params_ref,
    new_average_ref,
    new_table_ref,
    new_first_ref,
    new_second_ref,
):
    count = -(-per_device // LANES)
    grad = grad_ref[0:count, :]
    params = rows_of(params_ref, per_device)
    new_momentum = MOMENTUM_DECAY * rows_of(momentum_ref, per_device) + grad
    new_params = params - LEARN_RATE * (grad + MOMENTUM_DECAY * new_momentum)
    new_average = AVERAGE_DECAY * rows_of(average_ref, per_device) + (1.0 - AVERAGE_DECAY) * new_params
    store_rows(new_momentum_ref, new_momentum, per_device)
    store_rows(new_params_ref, new_params, per_device)
    store_rows(new_average_ref, new_average, per_device)
    grad_table = grad_table_ref[...]
    code_rows = table_ref.shape[0]
    here = shape_code_ref[...] - lax.axis_index("rows") * code_rows == iota((code_rows, shape_code_ref.shape[1]), 0)
    is_used = jnp.sum(here.astype(F32), axis=1, keepdims=True) > 0.5
    table, code_first, code_second = table_ref[...], code_first_ref[...], code_second_ref[...]
    first_new = BETA_FIRST * code_first + (1.0 - BETA_FIRST) * grad_table
    second_new = BETA_SECOND * code_second + (1.0 - BETA_SECOND) * grad_table * grad_table
    step_vals = (
        CODE_RATE
        * (first_new / (1.0 - BETA_FIRST**STEP))
        / (jnp.sqrt(second_new / (1.0 - BETA_SECOND**STEP)) + ADAM_EPS)
    )
    new_table_ref[...] = jnp.where(is_used, table - step_vals, table)
    new_first_ref[...] = jnp.where(is_used, first_new, code_first)
    new_second_ref[...] = jnp.where(is_used, second_new, code_second)
    loss_ref[...] = loss_in_ref[...]


def bounds(devices, per_device):
    for d in range(devices):
        row, phase = divmod(per_device * d, LANES)
        yield d, row, phase, -(-(phase + per_device) // LANES)


def assemble(dims, per_device, buf, flat):
    rows = dims[0] * dims[1] * dims[2]
    for d, row, phase, count in bounds(2 * rows, per_device):
        chip = d // 2
        src = buf.at[d % 2, chip // (dims[1] * dims[2]), (chip // dims[2]) % dims[1], chip % dims[2]]
        if phase:
            flat[row : row + 1, :] = flat[row : row + 1, :] + src[0:1, :]
            flat[row + 1 : row + count, :] = src[1:count, :]
        else:
            flat[row : row + count, :] = src[0:count, :]


def scatter(dims, per_device, chunk, flat, buf):
    rows = dims[0] * dims[1] * dims[2]
    for d, row, phase, count in bounds(2 * rows, per_device):
        chip = d // 2
        dst = buf.at[d % 2, chip // (dims[1] * dims[2]), (chip // dims[2]) % dims[1], chip % dims[2]]
        begin, size, _ = chunk
        dst[begin : begin + size, :] = flat[row + begin : row + begin + size, :]


def first_blocks():
    for back in range(4):
        begin = -(-256 * back // 3)
        end = min(-(-256 * (back + 1) // 3), CODE + 3)
        for at in range(begin, end, 8):
            yield back, at, min(8, end - at)


def unpack_first(flat, wide, v1):
    wide[0:8, :] = jnp.zeros((8, 256), F32)
    for half in range(2):
        lanes = slice(half * LANES, (half + 1) * LANES)
        wide[8:272, lanes] = flat[pl.ds(half, 264, stride=2), :]
    v1[256:264, :] = jnp.zeros((8, 256), F32)
    for back, at, n in first_blocks():
        base = 3 * at - 256 * back
        lane = iota((n, 256), 1)
        move = base + 3 * iota((n, 256), 0)
        here = wide[8 + at - back : 8 + at - back + n, :]
        before = wide[7 + at - back : 7 + at - back + n, :]
        mixed = jnp.where(lane < 256 - move, here, before)
        mixed = turn(mixed, base)
        if n > 1:
            mixed = pltpu.roll(mixed, 0, 1, stride=3, stride_axis=0)
        v1[at : at + n, :] = jnp.where(lane < INNER, mixed, 0.0)


def pack_first(v1, wide, flat):
    wide[...] = jnp.zeros(wide.shape, F32)
    for back, at, n in first_blocks():
        base = 3 * at - 256 * back
        lane = iota((n, 256), 1)
        sub = iota((n, 256), 0)
        moved = turn(v1[at : at + n, :], -base)
        for bit in range(3):
            moved = jnp.where((sub >> bit) & 1 == 1, turn(moved, -3 * (1 << bit)), moved)
        here = lane < 256 - (base + 3 * sub)
        a = slice(8 + at - back, 8 + at - back + n)
        b = slice(7 + at - back, 7 + at - back + n)
        wide[a, :] = wide[a, :] + jnp.where(here, moved, 0.0)
        wide[b, :] = wide[b, :] + jnp.where(here, 0.0, moved)
    for half in range(2):
        lanes = slice(half * LANES, (half + 1) * LANES)
        flat[pl.ds(half, 256, stride=2), :] = wide[8:264, lanes]


def unpack_second(flat, v2):
    for q in range(H2 // LANES):
        lanes = slice(q * LANES, (q + 1) * LANES)
        for at in range(0, H2 + 8, 104):
            rows = flat[pl.ds(SECOND_ROW + q + 4 * at, 104, stride=4), :]
            if q == 0:
                after = flat[pl.ds(SECOND_ROW + 4 + 4 * at, 104, stride=4), :]
                rows = jnp.where(iota((104, LANES), 1) < SHIFT, after, rows)
            v2[at : at + 104, lanes] = rows


def pack_second(v2, flat):
    low = iota((1, LANES), 1) < SHIFT
    for q in range(1, H2 // LANES):
        lanes = slice(q * LANES, (q + 1) * LANES)
        flat[pl.ds(SECOND_ROW + q, H2, stride=4), :] = v2[0:H2, lanes]
        flat[SECOND_ROW + q + 4 * H2 : SECOND_ROW + q + 4 * H2 + 1, :] = v2[H2 : H2 + 1, lanes]
    flat[pl.ds(SECOND_ROW + 4, H2, stride=4), :] = jnp.where(low, v2[0:H2, 0:LANES], v2[1 : H2 + 1, 0:LANES])
    flat[SECOND_ROW : SECOND_ROW + 1, :] = jnp.where(
        low, flat[SECOND_ROW : SECOND_ROW + 1, :], v2[0:1, 0:LANES]
    )
    flat[TAIL_ROW : TAIL_ROW + 1, :] = jnp.where(low, v2[H2 : H2 + 1, 0:LANES], 0.0)


def unpack_tail(flat):
    count = 13
    tail = one_row(flat[TAIL_ROW : TAIL_ROW + count, :], count)
    at = SHIFT
    parts = []
    for width in TAIL_PIECES:
        lanes = {INNER: 256, H2: H2, 1: LANES}[width]
        piece = turn(tail, -at)[:, 0:lanes]
        if width == H2:
            piece = turn(piece, SHIFT)
        else:
            piece = jnp.where(iota((1, lanes), 1) < width, piece, 0.0)
        parts.append(piece)
        at += width
    return parts


def pack_tail(parts, flat):
    count = 13
    at = SHIFT
    total = jnp.zeros((1, count * LANES), F32)
    for width, piece in zip(TAIL_PIECES, parts):
        if width == H2:
            piece = turn(piece, -SHIFT)
        else:
            piece = jnp.where(iota(piece.shape, 1) < width, piece, 0.0)
        total = total + turn(widen(piece, count * LANES), at)
        at += width
    flat[TAIL_ROW : TAIL_ROW + 1, :] = flat[TAIL_ROW : TAIL_ROW + 1, :] + total[:, 0:LANES]
    for k in range(1, count):
        flat[TAIL_ROW + k : TAIL_ROW + k + 1, :] = total[:, k * LANES : (k + 1) * LANES]


def split2(x):
    high = x.astype(BF16)
    return high, (x - high.astype(F32)).astype(BF16)


def split3(x):
    a = x.astype(BF16).astype(F32)
    b = (x - a).astype(BF16).astype(F32)
    return a, b, x - a - b


def kernel(
    cfg,
    params_hbm,
    table_hbm,
    coords_hbm,
    targets_hbm,
    seg_hbm,
    shape_code_hbm,
    loss_ref,
    grad_ref,
    grad_table_ref,
    params_ref,
    table_ref,
    coords_ref,
    targets_ref,
    seg_ref,
    shape_code_ref,
    fetched,
    buf,
    landing,
    flat,
    wide,
    v1,
    v2,
    g1,
    g2,
    w2t,
    w2b,
    w0,
    bias,
    head,
    points,
    hc,
    h1,
    slope1,
    h2,
    act,
    second,
    preds,
    d2b,
    df,
    d1b,
    dw2,
    dw1,
    dhead,
    sums,
    codes_buf,
    codes_landing,
    grads_buf,
    psend,
    precv,
    csend,
    crecv,
    dsend,
    drecv,
    rsend,
    rrecv,
):
    dims, per_device, tile = cfg["dims"], cfg["per_device"], cfg["tile"]
    used, kept = piece_rows(per_device, 2 * cfg["rows"])
    rows = cfg["rows"]
    shapes = cfg["shapes"]
    place = Place(dims)
    device = place.row * 2 + place.core
    tiles = seg_ref.shape[0] * LANES // tile
    per_tile = tile // LANES
    head_len = seg_ref.shape[0] * LANES // 16

    barrier = pltpu.get_barrier_semaphore()
    greeted = {place_steps for table in cfg["tables"] for _, _, order in table for axes in order for place_steps in steps_of(dims, axes)}
    pl.semaphore_signal(barrier, inc=1, device_id=place.sibling(), device_id_type=MESH)
    for o in sorted(greeted):
        pl.semaphore_signal(barrier, inc=1, device_id=place.peer(o)[1], device_id_type=MESH)

    inputs = dict(
        params=(params_hbm, params_ref),
        seg=(seg_hbm, seg_ref),
        codes=(shape_code_hbm, shape_code_ref),
        table=(table_hbm, table_ref),
        targets=(targets_hbm, targets_ref),
        coords=(coords_hbm, coords_ref),
    )
    copies = {}
    for i, (name, (src, dst)) in enumerate(inputs.items()):
        copies[name] = pltpu.make_async_copy(src, dst, fetched.at[i])
        copies[name].start()

    copies["params"].wait()
    phase = (device * per_device) % LANES
    own = buf.at[place.core, place.at[0], place.at[1], place.at[2]]
    raw = rows_of(params_ref, per_device)
    while raw.shape[0] < kept - 1:
        raw = jnp.concatenate([raw, jnp.zeros((1, LANES), F32)], axis=0)
    if any(p for _, _, p, _ in bounds(2 * rows, per_device)):
        moved = pltpu.roll(raw, phase, 1)
        before = jnp.concatenate([jnp.zeros((1, LANES), F32), moved[: kept - 2]], axis=0)
        raw = jnp.where(iota((kept - 1, LANES), 1) < phase, before, moved)
    own[0 : kept - 1, :] = raw

    pl.semaphore_wait(barrier, len(greeted) + 1)
    gather_table, reduce_table, codes_table, spread_table = cfg["tables"]
    gather = Gather(place, buf, gather_table, psend, precv)
    for k in range(len(gather_table) - 1):
        gather.start(k, 0)

    copies["seg"].wait()
    seg_heads = seg_ref[0 : head_len // LANES, :].astype(F32)
    shared = jnp.max(jnp.max(seg_heads, axis=1, keepdims=True), axis=0, keepdims=True)

    def count(where):
        return jnp.sum(jnp.sum(where.astype(F32), axis=1, keepdims=True), axis=0, keepdims=True)

    mine = (device * 2).astype(F32)
    seg_all = seg_ref[...].astype(F32)
    counts = [count(seg_all == shared), count(seg_all == mine), count(seg_all == mine + 1.0)]
    own[kept - 1 : kept, :] = jnp.broadcast_to(counts[0], (1, LANES))
    gather.start(len(gather_table) - 1, 0)

    for name in ("codes", "table", "targets", "coords"):
        copies[name].wait()

    base = (place.row * table_ref.shape[0]).astype(F32)
    codes_of = jnp.broadcast_to(shape_code_ref[...].astype(F32) + 1.0, (8, shapes))
    slots = rows * 8
    kind = iota((slots, shapes), 0) & 7
    owner = (iota((slots, shapes), 0) >> 3) * 2 + place.core
    shape_id = iota((slots, shapes), 1)
    asked = jnp.where(
        kind == 3,
        (shape_id.astype(F32) == shared).astype(F32),
        jnp.where((kind == 4) | (kind == 5), (shape_id == owner * 2 + kind - 4).astype(F32), 0.0),
    )
    wanted = dot_nt(asked, codes_of, EXACT)[:, 0:1] - 1.0 - base
    pick = (wanted == iota((slots, table_ref.shape[0]), 1).astype(F32)).astype(F32)
    answer = dot(pick, table_ref[...], EXACT)
    codes_buf[place.core] = answer.reshape(dims + (8, CODE))

    codes = Reduce(place, codes_buf, codes_landing, codes_table, csend, crecv, False)
    codes.begin()
    for q in range(per_tile):
        lanes = slice(q * LANES, (q + 1) * LANES)
        points[0, :, lanes] = seg_ref[pl.ds(q, tiles, stride=per_tile), :].astype(F32)
        points[1, :, lanes] = jnp.tanh(targets_ref[pl.ds(q, tiles, stride=per_tile), :] * (1.0 / CLAMP_DELTA))
    seg = points[0]

    for _ in itertools.zip_longest(gather.run(), codes.run()):
        pass
    z8 = codes_buf[place.core, place.at[0], place.at[1], place.at[2]]

    assemble(dims, per_device, buf, flat)
    unpack_first(flat, wide, v1)
    unpack_second(flat, v2)
    gain1, gain2, bias1, bias2, head_bias = unpack_tail(flat)
    norm1 = jnp.sum(v1[...] * v1[...], axis=0, keepdims=True) + NORM_EPS
    norm2 = jnp.sum(v2[0:H2, :] * v2[0:H2, :], axis=0, keepdims=True) + NORM_EPS
    inv1, inv2 = lax.rsqrt(norm1), lax.rsqrt(norm2)
    scale1, scale2 = gain1 * inv1, gain2 * inv2
    head_row = v2[H2 : H2 + 1, :]
    hbias = head_bias[:, 0:1]

    total = jnp.sum(buf[:, :, :, :, kept - 1 : kept, :], axis=(0, 1, 2, 3))[:, 0:1]
    counts_all = [total]
    for k in (1, 2):
        counts_all.append(jnp.where(shared == mine + (k - 1.0), total, jnp.maximum(counts[k], 1.0)))
    inv_counts = [1.0 / (n * float(shapes)) for n in counts_all]
    position = iota((tiles, tile), 0) * tile + iota((tiles, tile), 1)
    is_two = (seg == mine + 1.0) & (position >= head_len)
    per_point = jnp.where(
        position < head_len, inv_counts[0], jnp.where(is_two, inv_counts[2], inv_counts[1])
    )
    points[2] = jnp.where(seg >= 0.0, per_point, 0.0)
    points[3] = jnp.where(is_two, 1.0, 0.0)

    lane1 = iota((8, 256), 1)
    sub1 = iota((8, 256), 0)
    code1 = dot(z8, v1[0:CODE, :], THREE) * scale1 + bias1
    xyz1 = v1[CODE : CODE + 8, :] * scale1
    rows1 = 0.5 * jnp.where(sub1 < 3, xyz1, jnp.where(sub1 < 6, code1, 0.0))
    rows1 = jnp.where(lane1 < INNER, rows1, (lane1 == INNER + sub1).astype(F32))
    rows1 = jnp.where(sub1 < 6, rows1, 0.0)
    wa, wb, wc = split3(rows1)
    stack = jnp.concatenate([wa, wa, wb, wb, wa, wc] + [jnp.zeros((8, 256), F32)] * 10, axis=0)
    w0[...] = stack.T.astype(BF16)

    z_wide = turn(widen(z8, H2), INNER)
    code2 = 0.5 * (dot(z_wide, v2[0:H2, :], THREE) * scale2 + bias2)
    sub2 = iota((8, H2), 0)
    columns = jnp.where(sub2 == 6, jnp.broadcast_to(0.5 * head_row, (8, H2)), code2)
    columns = jnp.concatenate([columns, jnp.zeros((LANES - 8, H2), F32)], axis=0).T
    for k in range(3):
        bias[k] = jnp.broadcast_to(columns[:, 3 + k : 4 + k], (H2, LANES))
    head[...] = jnp.broadcast_to(columns[:, 6:7], (H2, LANES))
    last = jnp.where(sub2 < 5, v2[248:256, :], v2[H2 - 8 : H2, :])
    normal = jnp.concatenate([v2[0:248, :], last], axis=0) * scale2
    w2b[...] = (normal * (0.25 * head_row)).astype(BF16)
    high, low = split2(0.5 * normal.T)
    w2t[:, 0:256] = high
    w2t[:, 256:512] = high
    w2t[:, 512:768] = low

    dw2[...] = jnp.zeros(dw2.shape, F32)
    dw1[...] = jnp.zeros(dw1.shape, F32)
    dhead[...] = jnp.zeros(dhead.shape, F32)
    sums[...] = jnp.zeros(sums.shape, F32)
    block = 32

    def lanes_of(q):
        return slice(q * LANES, (q + 1) * LANES)

    def first_product(t):
        at = slice(t * tile, (t + 1) * tile)
        two = points[3, t : t + 1, :]
        is_head = (t * tile + iota((1, tile), 1) < head_len).astype(F32)
        x8 = jnp.concatenate(
            [coords_ref[:, at], is_head, 1.0 - two - is_head, two, jnp.zeros((2, tile), F32)], axis=0
        )
        xa, xb, xc = split3(x8)
        x48 = jnp.concatenate([xa, xb, xa, xb, xc, xa], axis=0).astype(BF16)
        hc[t % DEEP, 768:784, :] = jnp.concatenate([xa, xb], axis=0).astype(BF16)
        h1[t % 2] = dot(w0[:, 0:48], x48)
        yield

    def first_layer(t):
        for q in range(per_tile):
            lanes = lanes_of(q)
            for u in range(0, 256, block):
                us = slice(u, u + block)
                h = h1[t % 2, us, lanes]
                th = jnp.tanh(h)
                m = h * th
                f = h + m
                slope1[t % DEEP, us, lanes] = (1.0 + th) * (1.0 + (h - m))
                if u + block > INNER:
                    f = jnp.where(iota((block, LANES), 0) + u >= INNER, h, f)
                fh, fl = split2(f)
                hc[t % DEEP, us, lanes] = fh
                hc[t % DEEP, 256 + u : 256 + u + block, lanes] = fl
                hc[t % DEEP, 512 + u : 512 + u + block, lanes] = fh
                yield

    def second_product(t):
        for m in range(0, H2, 256):
            h2[t % 2, m : m + 256, :] = dot(w2t[m : m + 256, :], hc[t % DEEP, 0:768, :])
            yield

    def second_layer(t):
        parts = []
        for q in range(per_tile):
            lanes = lanes_of(q)
            in_head = t * per_tile + q < head_len // LANES
            is_second = jnp.broadcast_to(points[3, t : t + 1, lanes], (block, LANES)) > 0.5
            part = jnp.zeros((8, LANES), F32)
            for u in range(0, H2, block):
                us = slice(u, u + block)
                b = bias[0, us, :] if in_head else jnp.where(is_second, bias[2, us, :], bias[1, us, :])
                h = h2[t % 2, us, lanes] + b
                th = jnp.tanh(h)
                m = h * th
                s = h + m
                hw = head[us, :]
                second[t % 2, us, lanes] = s
                act[t % 2, us, lanes] = (1.0 + th) * (1.0 + (h - m))
                w = hw * s
                for v in range(0, block, 8):
                    part = part + w[v : v + 8]
                yield
            parts.append(jnp.sum(part, axis=0, keepdims=True))
        preds[t % 2, 0:1, :] = 2.0 * jnp.concatenate(parts, axis=1) + hbias

    def back_second(t):
        pred = jnp.tanh(preds[t % 2, 0:1, :])
        squash = jnp.tanh(pred * (1.0 / CLAMP_DELTA))
        resid = CLAMP_DELTA * squash - CLAMP_DELTA * points[1, t : t + 1, :]
        square = resid * resid + SMOOTH * SMOOTH
        inv_radius = lax.rsqrt(square)
        share = points[2, t : t + 1, :]
        dpred = share * (resid * inv_radius) * (1.0 - squash * squash) * (1.0 - pred * pred)
        sums[0:1, :] = sums[0:1, :] + share * (square * inv_radius - SMOOTH)
        sums[1:2, :] = sums[1:2, :] + dpred
        for u in range(0, H2, block):
            us = slice(u, u + block)
            total_u = dhead[us, :]
            for q in range(per_tile):
                lanes = lanes_of(q)
                dp = jnp.broadcast_to(dpred[:, lanes], (block, LANES))
                d2b[t % 2, us, lanes] = (act[t % 2, us, lanes] * dp).astype(BF16)
                total_u = total_u + second[t % 2, us, lanes] * dp
            dhead[us, :] = total_u
            yield

    def back_products(t):
        df[t % 2] = dot(w2b[...], d2b[t % 2])
        yield
        for n in range(0, H2, 256):
            dw2[:, n : n + 256] = dw2[:, n : n + 256] + dot_nt(hc[t % DEEP, 512:784, :], d2b[t % 2, n : n + 256, :])
            yield

    def back_first(t):
        for u in range(0, 256, block):
            us = slice(u, u + block)
            d1b[t % 2, us, :] = (df[t % 2, us, :] * slope1[t % DEEP, us, :]).astype(BF16)
            yield

    def back_first_product(t):
        dw1[...] = dw1[...] + dot_nt(hc[t % DEEP, 768:784, :], d1b[t % 2])
        yield

    products = ((second_product, 0), (back_products, -3), (first_product, 2), (back_first_product, -5))
    elementwise = ((back_second, -2), (second_layer, -1), (first_layer, 1), (back_first, -4))
    for i in range(-2, tiles + 5):

        def pieces(stages):
            return itertools.chain(*(stage(i + lag) for stage, lag in stages if 0 <= i + lag < tiles))

        rest = pieces(elementwise)
        for _ in pieces(products):
            for _ in itertools.islice(rest, 8):
                pass
        for _ in rest:
            pass

    outer1 = jnp.where(lane1 < INNER, dw1[0:8, :] + dw1[8:16, :], 0.0)
    dw2[...] = dw2[...] * (0.5 * head_row)
    outer2 = dw2[256:264, :] + dw2[264:272, :]
    slot_rows = (sub1 >= 3) & (sub1 < 6)
    d1 = jnp.where(slot_rows, outer1, 0.0)
    d2 = jnp.where((sub2 >= 3) & (sub2 < 6), outer2, 0.0)
    dz = dot_nt(d1 * scale1, v1[0:CODE, :], THREE)
    dz = dz + turn(dot_nt(d2 * scale2, v2[0:H2, :], THREE), -INNER)[:, 0:CODE]
    own_rows = (sub1 == 4) | (sub1 == 5)
    dz = dz + jnp.where(own_rows, (2.0 * PRIOR_WEIGHT / shapes) * z8, 0.0)
    prior = jnp.where(own_rows, z8 * z8, 0.0)
    prior = (PRIOR_WEIGHT / shapes) * jnp.sum(jnp.sum(prior, axis=1, keepdims=True), axis=0, keepdims=True)
    loss_here = jnp.sum(sums[0:1, :], axis=1, keepdims=True) + prior
    message = jnp.where(slot_rows, dz, 0.0)
    message = jnp.where(sub1 == 0, jnp.broadcast_to(loss_here, (8, CODE)), message)
    grads_buf[place.core, place.at[0], place.at[1], place.at[2]] = message
    spread = Gather(place, grads_buf, spread_table, dsend, drecv)
    spread.start(0, 0)

    g1[0:CODE, :] = dot_tn(z8, d1, THREE)
    g1[CODE : CODE + 8, :] = jnp.where(sub1 < 3, outer1, 0.0)
    along1 = jnp.sum(v1[...] * g1[...], axis=0, keepdims=True)
    g1[...] = g1[...] * scale1 - v1[...] * (scale1 * inv1 * inv1 * along1)
    g2[0:H2, :] = dot_tn(z_wide, d2, THREE)
    g2[0:256, :] = g2[0:256, :] + jnp.where(iota((256, H2), 0) < INNER, dw2[0:256, :], 0.0)
    g2[H2 - 8 : H2, :] = g2[H2 - 8 : H2, :] + jnp.where(sub2 >= 5, dw2[248:256, :], 0.0)
    along2 = jnp.sum(v2[0:H2, :] * g2[0:H2, :], axis=0, keepdims=True)
    g2[0:H2, :] = g2[0:H2, :] * scale2 - v2[0:H2, :] * (scale2 * inv2 * inv2 * along2)
    high, low = split2(dhead[...])
    ones = jnp.ones((16, LANES), BF16)
    g2[H2 : H2 + 8, :] = (dot_nt(ones, high) + dot_nt(ones, low))[0:8, :]
    dbias = jnp.broadcast_to(jnp.sum(sums[1:2, :], axis=1, keepdims=True), (1, LANES))
    pack_first(g1, wide, flat)
    pack_second(g2, flat)
    pack_tail(
        [
            along1 * inv1,
            along2 * inv2,
            jnp.sum(d1, axis=0, keepdims=True),
            jnp.sum(d2, axis=0, keepdims=True),
            dbias,
        ],
        flat,
    )
    gather.finish()
    codes.finish()
    reduce = Reduce(place, buf, landing, reduce_table, rsend, rrecv, True)
    for k, chunk in enumerate(reduce_table):
        scatter(dims, per_device, chunk, flat, buf)
        reduce.start(k, -1)
    arriving, summing = spread.run(), reduce.run()
    for _ in range(2):
        next(summing)
        next(arriving)
    next(arriving)

    everyone = grads_buf[...].reshape(2 * slots, CODE)
    kind = iota((shapes, 2 * slots), 1) & 7
    owner = ((iota((shapes, 2 * slots), 1) >> 3) & (rows - 1)) * 2 + (iota((shapes, 2 * slots), 1) >> int(math.log2(slots)))
    shape_id = iota((shapes, 2 * slots), 0)
    asked = jnp.where(
        kind == 3,
        (shape_id.astype(F32) == shared).astype(F32),
        jnp.where((kind == 4) | (kind == 5), (shape_id == owner * 2 + kind - 4).astype(F32), 0.0),
    )
    code_rows = table_ref.shape[0]
    target_row = dot(codes_of, asked, EXACT)[0:1, :] - 1.0 - base
    pick = (target_row == iota((code_rows, 2 * slots), 0).astype(F32)).astype(F32)
    grad_table = dot(pick, everyone, THREE)
    grad_table_ref[...] = grad_table
    loss_ref[...] = jnp.sum(grads_buf[:, :, :, :, 0:8, 0:LANES], axis=(0, 1, 2, 3))[0:1, 0:1]
    next(summing)
    piece = own[...]
    if any(p for _, _, p, _ in bounds(2 * rows, per_device)):
        moved = pltpu.roll(piece, (LANES - phase) % LANES, 1)
        after = jnp.concatenate([moved[1:], moved[:1]], axis=0)
        piece = jnp.where(iota((kept, LANES), 1) < LANES - phase, moved, after)
    grad_ref[...] = piece

    spread.finish()
    reduce.finish()


def chunked(rows, parts):
    blocks = -(-rows // 8)
    whole = sum(share for share, _ in parts)
    out, at, upto = [], 0, 0
    for share, order in parts:
        upto += share
        end = min((blocks * upto + whole // 2) // whole * 8, rows)
        if end > at:
            out.append((at, end - at, order))
        at = end
    return out


def shards(rows, params, momentum, average, table, code_first, code_second, coords, targets, segment_ids, shape_code):
    per_device = params.shape[0]
    devices = 2 * rows
    used, kept = piece_rows(per_device, devices)
    dims = chip_dims(rows)
    points_here = segment_ids.shape[0]
    tile = 256
    tiles = points_here // tile
    shapes = shape_code.shape[0]
    code_rows = table.shape[0]
    out_first, out_last = ((0,), (1, 2)), ((1, 2), (0,))
    tables = [
        chunked(kept, [(4, out_first), (3, out_first), (4, out_last)]),
        chunked(kept, [(3, out_first), (4, out_last), (4, out_last)]),
        [(0, 8, out_last)],
        [(0, 8, out_first)],
    ]
    cfg = dict(
        dims=dims,
        rows=rows,
        per_device=per_device,
        tile=tile,
        shapes=shapes,
        tables=tables,
    )
    flat_rows = per_device * devices // LANES + kept + 8
    vm = pltpu.VMEM
    scratch = [
        vm((per_device,), F32),
        vm((code_rows, CODE), F32),
        vm((3, points_here), F32),
        vm((points_here // LANES, LANES), F32),
        vm((points_here // LANES, LANES), jnp.int32),
        vm((1, shapes), jnp.int32),
        pltpu.SemaphoreType.DMA((6,)),
        vm((2,) + dims + (kept, LANES), F32),
        landings(dims, tables[1], LANES, True),
        vm((flat_rows, LANES), F32),
        vm((272, 256), F32),
        vm((264, 256), F32),
        vm((520, H2), F32),
        vm((264, 256), F32),
        vm((520, H2), F32),
        vm((H2, 768), BF16),
        vm((256, H2), BF16),
        vm((256, LANES), BF16),
        vm((3, H2, LANES), F32),
        vm((H2, LANES), F32),
        vm((4, tiles, tile), F32),
        vm((DEEP, 784, tile), BF16),
        vm((2, 256, tile), F32),
        vm((DEEP, 256, tile), F32),
        vm((2, H2, tile), F32),
        vm((2, H2, tile), F32),
        vm((2, H2, tile), F32),
        vm((2, 8, tile), F32),
        vm((2, H2, tile), BF16),
        vm((2, 256, tile), F32),
        vm((2, 256, tile), BF16),
        vm((272, H2), F32),
        vm((16, 256), F32),
        vm((H2, LANES), F32),
        vm((8, tile), F32),
        vm((2,) + dims + (8, CODE), F32),
        landings(dims, tables[2], CODE, False),
        vm((2,) + dims + (8, CODE), F32),
        *semaphores(dims, tables[0]),
        *semaphores(dims, tables[2]),
        *semaphores(dims, tables[3]),
        *semaphores(dims, tables[1]),
    ]
    spec = pl.BlockSpec(memory_space=pltpu.VMEM)
    loss, grad, grad_table = pl.pallas_call(
        functools.partial(kernel, cfg),
        out_shape=(
            jax.ShapeDtypeStruct((1, 1), F32),
            jax.ShapeDtypeStruct((kept, LANES), F32),
            jax.ShapeDtypeStruct((code_rows, CODE), F32),
        ),
        in_specs=[pl.BlockSpec(memory_space=pl.ANY)] * 6,
        out_specs=(spec,) * 3,
        scratch_shapes=scratch,
        compiler_params=pltpu.CompilerParams(
            collective_id=0, has_side_effects=True, vmem_limit_bytes=56 << 20
        ),
    )(
        params,
        table,
        coords,
        targets.reshape(-1, LANES),
        segment_ids.reshape(-1, LANES),
        shape_code.reshape(1, shapes),
    )
    flat_out = jax.ShapeDtypeStruct((per_device,), F32)
    table_out = jax.ShapeDtypeStruct((code_rows, CODE), F32)
    outs = pl.pallas_call(
        functools.partial(update, per_device),
        out_shape=(jax.ShapeDtypeStruct((1, 1), F32),) + (flat_out,) * 3 + (table_out,) * 3,
        in_specs=[spec] * 10,
        out_specs=(spec,) * 7,
    )(grad, grad_table, shape_code.reshape(1, shapes), loss, params, momentum, average, table, code_first, code_second)
    return (outs[0].reshape(()),) + tuple(outs[1:])


def solution(mesh):
    flat = P(("rows", "mp"))
    placed = (flat, flat, flat, P("rows", None), P("rows", None), P("rows", None), P(None, ("rows", "mp")), flat, flat, P())
    return jax.shard_map(
        functools.partial(shards, mesh.shape["rows"]),
        mesh=mesh,
        in_specs=placed,
        out_specs=(P(), flat, flat, flat, P("rows", None), P("rows", None), P("rows", None)),
        check_vma=False,
    )
```
